32 devices in a mesh: tm: 8 (over z, y), dom: 4 (over x, core).
Axes of the slice: x: 2, y: 2, z: 4, core: 2. Of those that a mesh axis runs over, the one named last changes fastest.
Arguments:
- starting_voltage_guess: float32 [128, 4, 128], P('tm', 'dom'), may hold values from -3 to 3
- injected_amperes: float32 [128, 4, 128], P('tm', 'dom'), may hold values from -6 to 6
- capacitance: float32 [4, 128], P('dom'), may hold values from 0.5 to 2
- conductance: float32 [4, 128, 128], P('dom'), may hold values from -0.5 to 0.5
- block_pattern: int32 [4, 1, 1], P('dom'), may hold values 0 or 1
- device_gain: float32 [4, 128], P('dom'), may hold values from 0.2 to 2
- link_weight: float32 [4, 128, 128], P('dom'), may hold values from -0.5 to 0.5
- boundary_vertex_list: int32 [4, 128], P('dom'), may hold values from 0 to 127, as said below
- diagonal_reciprocals: float32 [128, 4, 1, 128, 128], P('tm', 'dom')
- boundary_jacobian: float32 [4, 128, 128], P('dom'), may hold values from -6 to 6
- transfer: float32 [128, 4, 1, 128, 128], P('tm', 'dom')
Outputs:
- periodic_state: float32 [128, 4, 128], P('tm', 'dom')
The draws below stay inside these ranges and needn't reach their ends.
Inputs may be any that keep to these rules, and one draw needn't show every extreme that they name: `boundary_vertex_list`: the 128 interface nodes of one partition are distinct.
All inputs are finite; a program needn't handle non-finite values. No bound on the sum of `block_pattern` on one device may be relied on, other than what follows from the above.
Results may differ from the reference program's by a relative error of at most 0.0003.
Values sent between devices are 32-bit elements; how exact they have to be, the bound alone decides.
No kernel may reach another device: no remote copies, remote signals or barrier semaphores. Data moves between devices by JAX's collectives and lax.ppermute only.
A program may use at most 64 MiB of HBM per device.

```python
import math
import jax
import jax.numpy as jnp
from jax import lax

BLOCK_WIDTH_NODE = 128
LINKED_NODES = 128
JACOBIAN_TILES = 1
TPD = 16
ITERS = 2
PART_VERTICES = 128
GRID_MOMENTS = 128
SUBCIRCUITS = 4
N_TM = 8


def identity_operator():
    row_index = lax.broadcasted_iota(jnp.int32, (BLOCK_WIDTH_NODE, BLOCK_WIDTH_NODE), 0)
    col_index = lax.broadcasted_iota(jnp.int32, (BLOCK_WIDTH_NODE, BLOCK_WIDTH_NODE), 1)
    return (row_index == col_index).astype(jnp.float32)


def draw_boundary_vertex_list(key, part):
    keys = jax.random.split(key, SUBCIRCUITS)
    chosen = jax.vmap(lambda single_entry: jax.random.permutation(single_entry, PART_VERTICES)[:LINKED_NODES])(keys)
    return chosen.astype(jnp.int32)


def draw_diagonal_reciprocals(key, part):
    leading_operand = jax.random.fold_in(key, 0)
    perturbation = jax.random.normal(leading_operand, (GRID_MOMENTS, SUBCIRCUITS, JACOBIAN_TILES, BLOCK_WIDTH_NODE, BLOCK_WIDTH_NODE), jnp.float32)
    linear_operator = (identity_operator() + 0.5 * perturbation / math.sqrt(BLOCK_WIDTH_NODE)) * (0.5 / math.sqrt(GRID_MOMENTS))
    return linear_operator


def draw_transfer(key, part):
    leading_operand, trailing_operand, third, power_four_contribution = jax.random.split(key, 4)
    perturbation = jax.random.normal(leading_operand, (GRID_MOMENTS, SUBCIRCUITS, JACOBIAN_TILES, BLOCK_WIDTH_NODE, BLOCK_WIDTH_NODE), jnp.float32)
    mixing = (identity_operator() + 0.1 * perturbation / math.sqrt(BLOCK_WIDTH_NODE)) / math.sqrt(1.01)
    quick_portion = 0.5
    selected = jax.random.uniform(trailing_operand, (SUBCIRCUITS, JACOBIAN_TILES, BLOCK_WIDTH_NODE), jnp.float32)
    gradual_aggregate = jnp.exp(jax.random.uniform(third, (SUBCIRCUITS, JACOBIAN_TILES, BLOCK_WIDTH_NODE), jnp.float32, math.log(0.1), math.log(1.5)))
    slope_readings = jnp.where(selected < quick_portion, 1.0 / 40.0, gradual_aggregate / GRID_MOMENTS)
    orbit_bundles = jax.random.uniform(power_four_contribution, (GRID_MOMENTS,), jnp.float32) < 4.0 / GRID_MOMENTS
    multiplier_pieces = jnp.exp(-slope_readings)[None] * jnp.where(orbit_bundles, 0.65, 1.0)[:, None, None, None]
    return multiplier_pieces[..., None] * mixing


def with_ends(entries, own_key, least, largest):
    longest = entries.shape.index(max(entries.shape))
    spots = []
    for shift in (0, 1):
        where = [jax.random.randint(jax.random.fold_in(own_key, axis), (), 0, length) for axis, length in enumerate(entries.shape)]
        where[longest] = (where[longest] + shift) % entries.shape[longest]
        spots.append(tuple(where))
    return entries.at[spots[0]].set(least).at[spots[1]].set(largest)


def block_scale(own_key, dims, pieces, low, top_value):
    gain = 1.0
    for dim, shards_of in pieces:
        heights = jax.random.uniform(jax.random.fold_in(jax.random.fold_in(own_key, 6), dim), (shards_of,), jnp.float32, low / len(pieces), top_value / len(pieces))
        gain = gain * jnp.repeat(jnp.exp(heights), dims[dim] // shards_of).reshape((-1,) + (1,) * (len(dims) - 1 - dim))
    return gain


def normal_values(own_key, extent, width, bound, cuts=(), held_as=jnp.bfloat16):
    array = jax.random.normal(own_key, extent, jnp.float32) * width
    if len(cuts) > 0:
        array = block_scale(own_key, extent, cuts, -0.22, 0.18) * array
    return jnp.clip(array, min=-bound, max=bound).astype(held_as)


def setup_inputs(seed: int = 0) -> dict:
    splits = jax.random.split(jax.random.key(seed), 12)
    starting_voltage_guess = normal_values(splits[0], (GRID_MOMENTS, SUBCIRCUITS, PART_VERTICES), 0.5, 3.0, ((0, 8), (1, 4)), jnp.float32)
    injected_amperes = normal_values(splits[1], (GRID_MOMENTS, SUBCIRCUITS, PART_VERTICES), 1.0, 6.0, ((0, 8), (1, 4)), jnp.float32)
    capacitance = jnp.clip(jnp.exp(math.log(2.0) - 1.3862944 * jax.random.uniform(splits[2], (SUBCIRCUITS, PART_VERTICES), jnp.float32) ** block_scale(splits[2], (SUBCIRCUITS, PART_VERTICES), ((0, 4),), -0.2, 0.2)), 0.5, 2.0)
    conductance = normal_values(splits[3], (SUBCIRCUITS, PART_VERTICES, PART_VERTICES), PART_VERTICES ** -0.5, 0.5, ((0, 4),), jnp.float32)
    block_pattern = with_ends((jax.random.randint(splits[4], (SUBCIRCUITS, JACOBIAN_TILES, JACOBIAN_TILES), 0, 4) < 3).astype(jnp.int32), jax.random.fold_in(splits[4], 1), 0, 1)
    device_gain = jnp.clip(jnp.exp(math.log(2.0) - 2.3025851 * jax.random.uniform(splits[5], (SUBCIRCUITS, PART_VERTICES), jnp.float32) ** block_scale(splits[5], (SUBCIRCUITS, PART_VERTICES), ((0, 4),), -0.2, 0.2)), 0.2, 2.0)
    link_weight = normal_values(splits[6], (SUBCIRCUITS, PART_VERTICES, LINKED_NODES), LINKED_NODES ** -0.5, 0.5, ((0, 4),), jnp.float32)
    boundary_vertex_list = draw_boundary_vertex_list(jax.random.fold_in(splits[11], 71), 0)
    diagonal_reciprocals = draw_diagonal_reciprocals(jax.random.fold_in(splits[11], 71), 0)
    boundary_jacobian = normal_values(splits[9], (SUBCIRCUITS, PART_VERTICES, LINKED_NODES), (0.8 * GRID_MOMENTS ** 0.5 / LINKED_NODES ** 0.5), 6.0, ((0, 4),), jnp.float32)
    transfer = draw_transfer(jax.random.fold_in(splits[11], 71), 0)
    return dict(starting_voltage_guess=starting_voltage_guess, injected_amperes=injected_amperes, capacitance=capacitance, conductance=conductance, block_pattern=block_pattern, device_gain=device_gain, link_weight=link_weight, boundary_vertex_list=boundary_vertex_list, diagonal_reciprocals=diagonal_reciprocals, boundary_jacobian=boundary_jacobian, transfer=transfer)


EXACT_MODE = lax.Precision.HIGHEST


def linear_map_action(linear_operator, column_array):
    return jnp.einsum('...ij,...j->...i', linear_operator, column_array, precision=EXACT_MODE)


def compose(later_map, earlier_map):
    return jnp.einsum('...ij,...jk->...ik', later_map, earlier_map, precision=EXACT_MODE)


def block_prefix(matrices):
    identity = jnp.broadcast_to(jnp.eye(BLOCK_WIDTH_NODE, dtype=jnp.float32), matrices.shape[1:])

    def forward_step(running, linear_operator):
        running = compose(linear_operator, running)
        return running, running

    def backward_step(running, linear_operator):
        return compose(running, linear_operator), running

    _, prefix = lax.scan(forward_step, identity, matrices)
    _, suffix = lax.scan(backward_step, identity, matrices, reverse=True)
    return prefix, suffix


def periodic_sum(prefix, suffix, matrices, stored_coulombs):
    zero_vector = jnp.zeros(stored_coulombs.shape[1:], jnp.float32)

    def accumulate(running, element):
        linear_operator, column_array = element
        running = linear_map_action(linear_operator, running) + column_array
        return running, running

    _, local_sum = lax.scan(accumulate, zero_vector, (matrices, stored_coulombs))

    def gather_tail(running, element):
        linear_operator, column_array = element
        return running + linear_map_action(linear_operator, column_array), running

    _, tail_sum = lax.scan(gather_tail, zero_vector, (suffix, stored_coulombs), reverse=True)
    whole_map = prefix[-1]
    full_period_sum = local_sum[-1]
    identity = jnp.broadcast_to(jnp.eye(BLOCK_WIDTH_NODE, dtype=jnp.float32), whole_map.shape[1:])
    zero_block = jnp.zeros(full_period_sum.shape[1:], jnp.float32)

    def front_step(running, element):
        map_sofar, sum_sofar = running
        block_map, block_sum = element
        return (compose(block_map, map_sofar), block_sum + linear_map_action(block_map, sum_sofar)), running

    def back_step(running, element):
        map_sofar, sum_sofar = running
        block_map, block_sum = element
        return (compose(map_sofar, block_map), sum_sofar + linear_map_action(map_sofar, block_sum)), running

    _, (front_map, front_sum) = lax.scan(front_step, (identity, zero_block), (whole_map, full_period_sum))
    _, (back_map, back_sum) = lax.scan(back_step, (identity, zero_block), (whole_map, full_period_sum), reverse=True)
    around_map = compose(front_map, back_map)
    around_sum = front_sum + linear_map_action(front_map, back_sum)
    incoming = around_sum[None] + linear_map_action(around_map[None], tail_sum)
    return local_sum + linear_map_action(prefix, incoming)


def carve_submatrix(values):
    reshaped_blocks = values.reshape((N_TM, TPD) + values.shape[1:])
    return jnp.swapaxes(reshaped_blocks, 0, 1)


def reference(starting_voltage_guess, injected_amperes, capacitance, conductance, block_pattern, device_gain, link_weight, boundary_vertex_list, diagonal_reciprocals, boundary_jacobian, transfer):
    expand = jnp.repeat(jnp.repeat(block_pattern, BLOCK_WIDTH_NODE, axis=1), BLOCK_WIDTH_NODE, axis=2).astype(jnp.float32)
    effective = conductance * expand
    matrices = carve_submatrix(transfer)
    prefix, suffix = block_prefix(matrices)
    voltage_profile = starting_voltage_guess
    lookup_position = jnp.broadcast_to(boundary_vertex_list[None], (GRID_MOMENTS, SUBCIRCUITS, LINKED_NODES)).astype(jnp.int32)
    for newton_step in range(ITERS):
        before = jnp.roll(voltage_profile, 1, axis=0)
        outlets = jnp.take_along_axis(voltage_profile, lookup_position, axis=2)
        upstream = jnp.concatenate([jnp.zeros_like(outlets[:, :1]), outlets[:, :-1]], axis=1)
        flows = jnp.einsum('pij,tpj->tpi', effective, voltage_profile, precision=EXACT_MODE)
        linked = jnp.einsum('pik,tpk->tpi', link_weight, upstream, precision=EXACT_MODE)
        residual = capacitance[None] * (voltage_profile - before) + flows + device_gain[None] * jnp.tanh(voltage_profile) - linked - injected_amperes
        entering_current = jnp.zeros((GRID_MOMENTS, LINKED_NODES), jnp.float32)
        solved_parts = []
        for subcircuit in range(SUBCIRCUITS):
            excitation = -residual[:, subcircuit] + jnp.dot(entering_current, boundary_jacobian[subcircuit].T, precision=EXACT_MODE)
            resolved_unknowns = linear_map_action(diagonal_reciprocals[:, subcircuit], excitation.reshape(GRID_MOMENTS, JACOBIAN_TILES, BLOCK_WIDTH_NODE)).reshape(GRID_MOMENTS, PART_VERTICES)
            solved_parts.append(resolved_unknowns)
            entering_current = resolved_unknowns[:, boundary_vertex_list[subcircuit]]
        chord_correction_vector = jnp.stack(solved_parts, axis=1)
        stored_coulombs = carve_submatrix(chord_correction_vector.reshape(GRID_MOMENTS, SUBCIRCUITS, JACOBIAN_TILES, BLOCK_WIDTH_NODE))
        refinement = periodic_sum(prefix, suffix, matrices, stored_coulombs)
        voltage_profile = voltage_profile + jnp.swapaxes(refinement, 0, 1).reshape(GRID_MOMENTS, SUBCIRCUITS, PART_VERTICES)
    return voltage_profile
```

```python
import functools

import jax
import jax.numpy as jnp
from jax import lax
from jax.experimental import pallas as pl
from jax.experimental.pallas import tpu as pltpu
from jax.sharding import PartitionSpec as P

ITERS = 2
F32 = jnp.float32
BF16 = jnp.bfloat16


def halves(x):
    hi = x.astype(BF16)
    return hi, (x - hi.astype(F32)).astype(BF16)


def split_cols(matrix):
    return jnp.concatenate(halves(matrix), axis=1)


def split_rows(vectors):
    hi, lo = halves(vectors)
    hi, lo = hi.astype(F32), lo.astype(F32)
    top = jnp.concatenate([hi, hi], axis=1)
    low = jnp.concatenate([lo, jnp.zeros_like(lo)], axis=1)
    return jnp.concatenate([top, low], axis=0).astype(BF16)


def dot_nt(a, b):
    return lax.dot_general(a, b, (((1,), (1,)), ((), ())), preferred_element_type=F32)


def times(a, b):
    ah, al = halves(a)
    bh, bl = halves(b)
    left = jnp.concatenate([ah, al, ah], axis=1)
    right = jnp.concatenate([bh, bh, bl], axis=0)
    return jnp.dot(left, right, preferred_element_type=F32)


def mapped(matrix_split, vectors):
    count = vectors.shape[0]
    both = dot_nt(split_rows(vectors), matrix_split)
    return both[:count] + both[count:]


def mapped_each(matrices_split, vectors):
    count, width = vectors.shape
    both = dot_nt(matrices_split, split_rows(vectors)).reshape(count, width, 2 * count)
    lane = lax.broadcasted_iota(jnp.int32, (width, 2 * count), 1) % count
    picked = jnp.zeros((width, 2 * count), F32)
    for r in range(count):
        picked = jnp.where(lane == r, both[r], picked)
    rows = picked.T
    return rows[:count] + rows[count:]


def call(kernel, outs, *args):
    vmem = pl.BlockSpec(memory_space=pltpu.VMEM)
    return pl.pallas_call(
        kernel,
        out_shape=[jax.ShapeDtypeStruct(s, d) for s, d in outs],
        in_specs=[vmem] * len(args),
        out_specs=[vmem] * len(outs),
        compiler_params=pltpu.CompilerParams(vmem_limit_bytes=24 * 2**20),
    )(*args)


def suffix_kernel(r_ref, s_ref, w_ref):
    points, width = r_ref.shape[0], r_ref.shape[1]
    u = [r_ref[i] for i in range(points)]
    span = 1
    while span < points:
        for base in range(0, points, 2 * span):
            mid = u[base + span]
            prod = times(mid, jnp.concatenate(u[base : base + span], axis=1))
            for i in range(span):
                u[base + i] = prod[:, i * width : (i + 1) * width]
        span *= 2
    w_ref[...] = u[0]
    for i in range(points - 1):
        s_ref[i * width : (i + 1) * width, :] = split_cols(u[i + 1])
    eye = (
        lax.broadcasted_iota(jnp.int32, (width, width), 0)
        == lax.broadcasted_iota(jnp.int32, (width, width), 1)
    ).astype(F32)
    s_ref[(points - 1) * width :, :] = split_cols(eye)


def prefix_kernel(r_ref, p_ref, l_ref):
    points, width = r_ref.shape[0], r_ref.shape[1]
    q = [r_ref[i] for i in range(points)]
    span, level, half = 1, 0, points // 2
    while span < points:
        slot = 0
        for base in range(0, points, 2 * span):
            upper = q[base + span : base + 2 * span]
            for matrix in upper:
                row = (level * half + slot) * width
                l_ref[row : row + width, :] = split_cols(matrix)
                slot += 1
            prod = times(jnp.concatenate(upper, axis=0), q[base + span - 1])
            for i in range(span):
                q[base + span + i] = prod[i * width : (i + 1) * width]
        span *= 2
        level += 1
    for i in range(points):
        p_ref[i * width : (i + 1) * width, :] = split_cols(q[i])


def scan_kernel(c_ref, l_ref, x_ref):
    points, width = c_ref.shape
    half = points // 2
    x = [c_ref[i : i + 1, :] for i in range(points)]
    span, level = 1, 0
    while span < points:
        heads = []
        for base in range(0, points, 2 * span):
            heads.extend([x[base + span - 1]] * span)
        moved = mapped_each(
            l_ref[level * half * width : (level + 1) * half * width, :],
            jnp.concatenate(heads, axis=0),
        )
        slot = 0
        for base in range(0, points, 2 * span):
            for i in range(base + span, base + 2 * span):
                x[i] = x[i] + moved[slot : slot + 1, :]
                slot += 1
        span *= 2
        level += 1
    x_ref[...] = jnp.concatenate(x, axis=0)


def prepare_kernel(d_ref, j_ref, k_ref, g_ref, mask_ref, ds_ref, js_ref, ks_ref, gs_ref):
    points, width = d_ref.shape[0], d_ref.shape[1]
    for i in range(points):
        ds_ref[i * width : (i + 1) * width, :] = split_cols(d_ref[i])
    js_ref[...] = split_cols(j_ref[...])
    ks_ref[...] = split_cols(k_ref[...])
    gs_ref[...] = split_cols(g_ref[...] * mask_ref[...].astype(F32))


def taken(rows, lanes):
    return jnp.take_along_axis(rows, jnp.broadcast_to(lanes, rows.shape), axis=1)


def first_half_of_step(s, halo, inj, cap, gain, gs_ref, ds_ref, bnd_ref, nr_ref, c_ref, msg_ref):
    points = s.shape[0]
    before = jnp.concatenate([halo, s[: points - 1]], axis=0)
    nr = inj - cap * (s - before) - mapped(gs_ref[...], s) - gain * jnp.tanh(s)
    c = mapped_each(ds_ref[...], nr)
    nr_ref[...] = nr
    c_ref[...] = c
    msg_ref[:points] = taken(c, bnd_ref[...])
    msg_ref[points:] = taken(s, bnd_ref[...])


def start_kernel(
    halo_ref, s_ref, inj_ref, cap_ref, gain_ref, gs_ref, ds_ref, bnd_ref, nr_ref, c_ref, msg_ref
):
    first_half_of_step(
        s_ref[...], halo_ref[...], inj_ref[...], cap_ref[...], gain_ref[...],
        gs_ref, ds_ref, bnd_ref, nr_ref, c_ref, msg_ref,
    )


def inflow_applied(got_ref, nr_ref, ds_ref, js_ref, ks_ref):
    points = nr_ref.shape[0]
    got = got_ref[...]
    nr = nr_ref[...] + mapped(js_ref[...], got[:points]) + mapped(ks_ref[...], got[points:])
    return mapped_each(ds_ref[...], nr)


def hop_kernel(
    place, got_ref, c_ref, msg_ref, nr_ref, ds_ref, js_ref, ks_ref, bnd_ref, new_c_ref, new_msg_ref
):
    points = c_ref.shape[0]
    here = lax.axis_index("dom") == place
    new_msg_ref[points:] = msg_ref[points:]

    @pl.when(here)
    def _():
        c = inflow_applied(got_ref, nr_ref, ds_ref, js_ref, ks_ref)
        new_c_ref[...] = c
        new_msg_ref[:points] = taken(c, bnd_ref[...])

    @pl.when(jnp.logical_not(here))
    def _():
        new_c_ref[...] = c_ref[...]
        new_msg_ref[:points] = msg_ref[:points]


def last_hop_kernel(
    place, got_ref, c_ref, nr_ref, ds_ref, js_ref, ks_ref, ss_ref, new_c_ref, tail_ref, f_ref
):
    points, width = c_ref.shape
    here = lax.axis_index("dom") == place

    @pl.when(here)
    def _():
        new_c_ref[...] = inflow_applied(got_ref, nr_ref, ds_ref, js_ref, ks_ref)

    @pl.when(jnp.logical_not(here))
    def _():
        new_c_ref[...] = c_ref[...]

    total = mapped_each(ss_ref[...], new_c_ref[...])
    shift = 1
    while shift < points:
        total = total + jnp.concatenate([total[shift:], jnp.zeros((shift, width), F32)], axis=0)
        shift *= 2
    tail_ref[:points] = jnp.concatenate([total[1:], jnp.zeros((1, width), F32)], axis=0)
    tail_ref[points:] = jnp.broadcast_to(total[:1], (8, width))
    f_ref[...] = jnp.broadcast_to(total[:1], (8, width))


def is_later(distance):
    return (lax.axis_index("tm") // distance) % 2 == 1


def first_level_kernel(
    distance, mw_ref, mf_ref, gw_ref, gf_ref,
    tw_ref, tf_ref, a_ref, bw_ref, bf_ref, aw_ref, af_ref,
):
    width = mw_ref.shape[0]
    later = is_later(distance)
    mw, mf, gw, gf = mw_ref[...], mf_ref[...], gw_ref[...], gf_ref[...]
    a = jnp.where(later, mw, gw)
    tw_ref[...] = times(a, jnp.where(later, gw, mw))
    a_split = split_cols(a)
    a_ref[...] = a_split
    tf_ref[...] = mapped(a_split, jnp.where(later, gf, mf)) + jnp.where(later, mf, gf)
    eye = (
        lax.broadcasted_iota(jnp.int32, (width, width), 0)
        == lax.broadcasted_iota(jnp.int32, (width, width), 1)
    ).astype(F32)
    bw_ref[...] = jnp.where(later, gw, eye)
    bf_ref[...] = jnp.where(later, gf, 0.0)
    aw_ref[...] = jnp.where(later, eye, gw)
    af_ref[...] = jnp.where(later, 0.0, gf)


def next_level_kernel(
    distance, mw_ref, mf_ref, gw_ref, gf_ref, bw_ref, bf_ref, aw_ref, af_ref,
    tw_ref, tf_ref, a_ref, x_ref, nbw_ref, nbf_ref, naw_ref, naf_ref,
):
    later = is_later(distance)
    mw, mf, gw, gf = mw_ref[...], mf_ref[...], gw_ref[...], gf_ref[...]
    bw, bf, aw, af = bw_ref[...], bf_ref[...], aw_ref[...], af_ref[...]
    a = jnp.where(later, mw, gw)
    tw_ref[...] = times(a, jnp.where(later, gw, mw))
    a_split = split_cols(a)
    a_ref[...] = a_split
    tf_ref[...] = mapped(a_split, jnp.where(later, gf, mf)) + jnp.where(later, mf, gf)
    x = jnp.where(later, bw, gw)
    joined = times(x, jnp.where(later, gw, aw))
    x_split = split_cols(x)
    x_ref[...] = x_split
    sums = mapped(x_split, jnp.where(later, gf, af)) + jnp.where(later, bf, gf)
    nbw_ref[...] = jnp.where(later, joined, bw)
    nbf_ref[...] = jnp.where(later, sums, bf)
    naw_ref[...] = jnp.where(later, aw, joined)
    naf_ref[...] = jnp.where(later, af, sums)


def again_first_kernel(distance, mf_ref, gf_ref, a_ref, tf_ref, bf_ref, af_ref):
    later = is_later(distance)
    mf, gf = mf_ref[...], gf_ref[...]
    tf_ref[...] = mapped(a_ref[...], jnp.where(later, gf, mf)) + jnp.where(later, mf, gf)
    bf_ref[...] = jnp.where(later, gf, 0.0)
    af_ref[...] = jnp.where(later, 0.0, gf)


def again_next_kernel(
    distance, mf_ref, gf_ref, bf_ref, af_ref, a_ref, x_ref, tf_ref, nbf_ref, naf_ref
):
    later = is_later(distance)
    mf, gf, bf, af = mf_ref[...], gf_ref[...], bf_ref[...], af_ref[...]
    tf_ref[...] = mapped(a_ref[...], jnp.where(later, gf, mf)) + jnp.where(later, mf, gf)
    sums = mapped(x_ref[...], jnp.where(later, gf, af)) + jnp.where(later, bf, gf)
    nbf_ref[...] = jnp.where(later, sums, bf)
    naf_ref[...] = jnp.where(later, af, sums)


def incoming(tail, maps, sums):
    for matrix, vector in zip(maps, sums):
        tail = mapped(matrix, tail) + vector[:1]
    return tail


def turn_kernel(
    tail_ref, aws_ref, af_ref, gws_ref, gf_ref, bws_ref, bf_ref, ps_ref, x_ref, s_ref,
    halo_ref, inj_ref, cap_ref, gain_ref, gs_ref, ds_ref, bnd_ref,
    new_s_ref, new_halo_ref, nr_ref, c_ref, msg_ref,
):
    points = s_ref.shape[0]
    came = incoming(
        tail_ref[...],
        (aws_ref[...], gws_ref[...], bws_ref[...]),
        (af_ref[...], gf_ref[...], bf_ref[...]),
    )
    s = s_ref[...] + x_ref[...] + mapped_each(ps_ref[...], came[:points])
    halo = halo_ref[...] + came[points : points + 1]
    new_s_ref[...] = s
    new_halo_ref[...] = halo
    first_half_of_step(
        s, halo, inj_ref[...], cap_ref[...], gain_ref[...],
        gs_ref, ds_ref, bnd_ref, nr_ref, c_ref, msg_ref,
    )


def end_kernel(
    tail_ref, aws_ref, af_ref, gws_ref, gf_ref, bws_ref, bf_ref, ps_ref, x_ref, s_ref, new_s_ref
):
    points = s_ref.shape[0]
    came = incoming(
        tail_ref[...],
        (aws_ref[...], gws_ref[...], bws_ref[...]),
        (af_ref[...], gf_ref[...], bf_ref[...]),
    )
    new_s_ref[...] = s_ref[...] + x_ref[...] + mapped_each(ps_ref[...], came[:points])


def splits_kernel(a_ref, b_ref, c_ref, as_ref, bs_ref, cs_ref):
    as_ref[...] = split_cols(a_ref[...])
    bs_ref[...] = split_cols(b_ref[...])
    cs_ref[...] = split_cols(c_ref[...])


def exchanged(value, distance):
    devices = range(lax.axis_size("tm"))
    return jax.tree.map(lambda v: lax.ppermute(v, "tm", [(i, i ^ distance) for i in devices]), value)


def handed_on(message, place):
    count = lax.axis_size("dom")
    pairs = []
    for i in range(0, count, 2):
        a, b = (i + place - 1) % count, (i + place) % count
        pairs += [(a, b), (b, a)]
    return lax.ppermute(message, "dom", pairs)


def per_device(
    starting_voltage_guess,
    injected_amperes,
    capacitance,
    conductance,
    block_pattern,
    device_gain,
    link_weight,
    boundary_vertex_list,
    diagonal_reciprocals,
    boundary_jacobian,
    transfer,
):
    points, _, width = starting_voltage_guess.shape
    segments, parts = lax.axis_size("tm"), lax.axis_size("dom")
    s = starting_voltage_guess[:, 0]
    inj = injected_amperes[:, 0]
    r = transfer[:, 0, 0]
    d = diagonal_reciprocals[:, 0, 0]
    cap, gain, bnd = capacitance, device_gain, boundary_vertex_list
    vec, eight, square = ((points, width), F32), ((8, width), F32), ((width, width), F32)
    square_split = ((width, 2 * width), BF16)
    many_split = ((points * width, 2 * width), BF16)
    one = ((1, width), F32)
    msg_shape = ((2 * points, width), F32)

    halo = lax.ppermute(
        s[points - 1 :], "tm", [(i, (i + 1) % segments) for i in range(segments)]
    )
    ds, js, ks, gs = call(
        prepare_kernel, [many_split] + [square_split] * 3,
        d, boundary_jacobian[0], link_weight[0], conductance[0], block_pattern[0],
    )
    ss, w = call(suffix_kernel, [many_split, square], r)
    levels = points.bit_length() - 1
    ps, ls = call(
        prefix_kernel, [many_split, ((levels * points // 2 * width, 2 * width), BF16)], r
    )
    nr, c, msg = call(start_kernel, [vec, vec, msg_shape], halo, s, inj, cap, gain, gs, ds, bnd)
    distances = [2**k for k in range(segments.bit_length() - 1)]
    kept = {}
    for step in range(ITERS):
        for place in range(1, parts):
            got = handed_on(msg, place)
            if place < parts - 1:
                c, msg = call(
                    functools.partial(hop_kernel, place), [vec, msg_shape],
                    got, c, msg, nr, ds, js, ks, bnd,
                )
        c, tail, f = call(
            functools.partial(last_hop_kernel, parts - 1),
            [vec, ((points + 8, width), F32), eight],
            got, c, nr, ds, js, ks, ss,
        )
        (x,) = call(scan_kernel, [vec], c, ls)
        for level, distance in enumerate(distances):
            last = level == len(distances) - 1
            if step == 0:
                both = exchanged(jnp.concatenate([w, f], axis=0), distance)
                gw, gf = both[:width], both[width:]
                if last:
                    kept["maps"] = call(splits_kernel, [square_split] * 3, aw, gw, bw)
                elif level == 0:
                    w, f, kept["a", 0], bw, bf, aw, af = call(
                        functools.partial(first_level_kernel, distance),
                        [square, eight, square_split, square, eight, square, eight],
                        w, f, gw, gf,
                    )
                else:
                    w, f, kept["a", level], kept["x", level], bw, bf, aw, af = call(
                        functools.partial(next_level_kernel, distance),
                        [square, eight, square_split, square_split, square, eight, square, eight],
                        w, f, gw, gf, bw, bf, aw, af,
                    )
            else:
                gf = exchanged(f, distance)
                if last:
                    pass
                elif level == 0:
                    f, bf, af = call(
                        functools.partial(again_first_kernel, distance), [eight] * 3,
                        f, gf, kept["a", 0],
                    )
                else:
                    f, bf, af = call(
                        functools.partial(again_next_kernel, distance), [eight] * 3,
                        f, gf, bf, af, kept["a", level], kept["x", level],
                    )
        aws, gws, bws = kept["maps"]
        ring = (tail, aws, af, gws, gf, bws, bf, ps, x, s)
        if step < ITERS - 1:
            s, halo, nr, c, msg = call(
                turn_kernel, [vec, one, vec, vec, msg_shape],
                *ring, halo, inj, cap, gain, gs, ds, bnd,
            )
        else:
            (s,) = call(end_kernel, [vec], *ring)
    return s[:, None]


def solution(mesh):
    in_specs = (
        P("tm", "dom", None),
        P("tm", "dom", None),
        P("dom", None),
        P("dom", None, None),
        P("dom", None, None),
        P("dom", None),
        P("dom", None, None),
        P("dom", None),
        P("tm", "dom", None, None, None),
        P("dom", None, None),
        P("tm", "dom", None, None, None),
    )
    out_specs = P("tm", "dom", None)
    return jax.shard_map(
        per_device, mesh=mesh, in_specs=in_specs, out_specs=out_specs, check_vma=False
    )
```

```python
import functools

import jax
import jax.numpy as jnp
from jax import lax
from jax.experimental import pallas as pl
from jax.experimental.pallas import tpu as pltpu
from jax.sharding import PartitionSpec as P

ITERS = 2
F32 = jnp.float32
BF16 = jnp.bfloat16


def halves(x):
    hi = x.astype(BF16)
    return hi, (x - hi.astype(F32)).astype(BF16)


def split_cols(matrix):
    return jnp.concatenate(halves(matrix), axis=1)


def split_rows(vectors):
    hi, lo = halves(vectors)
    hi, lo = hi.astype(F32), lo.astype(F32)
    top = jnp.concatenate([hi, hi], axis=1)
    low = jnp.concatenate([lo, jnp.zeros_like(lo)], axis=1)
    return jnp.concatenate([top, low], axis=0).astype(BF16)


def dot_nt(a, b):
    return lax.dot_general(a, b, (((1,), (1,)), ((), ())), preferred_element_type=F32)


def times(a, b):
    ah, al = halves(a)
    bh, bl = halves(b)
    left = jnp.concatenate([ah, al, ah], axis=1)
    right = jnp.concatenate([bh, bh, bl], axis=0)
    return jnp.dot(left, right, preferred_element_type=F32)


def mapped(matrix_split, vectors):
    count = vectors.shape[0]
    both = dot_nt(split_rows(vectors), matrix_split)
    return both[:count] + both[count:]


def mapped_each(matrices, vectors):
    rows = []
    for r in range(vectors.shape[0]):
        products = matrices[r] * vectors[r : r + 1, :]
        rows.append(jnp.sum(products.T, axis=0, keepdims=True))
    return jnp.concatenate(rows, axis=0)


def call(kernel, outs, *args, source=pltpu.VMEM, scratch=(), cost=None):
    return pl.pallas_call(
        kernel,
        out_shape=[jax.ShapeDtypeStruct(s, d) for s, d in outs],
        in_specs=[pl.BlockSpec(memory_space=source)] * len(args),
        out_specs=[pl.BlockSpec(memory_space=pltpu.VMEM)] * len(outs),
        scratch_shapes=list(scratch),
        cost_estimate=cost,
        compiler_params=pltpu.CompilerParams(vmem_limit_bytes=24 * 2**20),
    )(*args)


def identity(width):
    return (
        lax.broadcasted_iota(jnp.int32, (width, width), 0)
        == lax.broadcasted_iota(jnp.int32, (width, width), 1)
    ).astype(F32)


def identity_kernel(eye_ref):
    eye_ref[...] = identity(eye_ref.shape[0])


def suffix_products(r_ref, eye, s_ref, w_ref):
    points, width = r_ref.shape[0], r_ref.shape[1]
    u = [r_ref[i] for i in range(points)]
    span = 1
    while span < points:
        for base in range(0, points, 2 * span):
            mid = u[base + span]
            prod = times(mid, jnp.concatenate(u[base : base + span], axis=1))
            for i in range(span):
                u[base + i] = prod[:, i * width : (i + 1) * width]
        span *= 2
    w_ref[...] = u[0]
    for i in range(points - 1):
        s_ref[i] = u[i + 1]
    s_ref[points - 1] = eye


def prefix_products(r_ref, p_ref, l_ref):
    points, width = r_ref.shape[0], r_ref.shape[1]
    q = [r_ref[i] for i in range(points)]
    span, slot = 1, 0
    while span < points:
        for base in range(0, points, 2 * span):
            upper = q[base + span : base + 2 * span]
            for matrix in upper:
                l_ref[slot] = matrix
                slot += 1
            prod = times(jnp.concatenate(upper, axis=0), q[base + span - 1])
            for i in range(span):
                q[base + span + i] = prod[i * width : (i + 1) * width]
        span *= 2
    for i in range(points):
        p_ref[i] = q[i]


def scanned(c, l_ref):
    points = c.shape[0]
    half = points // 2
    x = [c[i : i + 1, :] for i in range(points)]
    span, level = 1, 0
    while span < points:
        slot = level * half
        for base in range(0, points, 2 * span):
            head = x[base + span - 1]
            for i in range(base + span, base + 2 * span):
                x[i] = x[i] + mapped_each(l_ref[slot : slot + 1], head)
                slot += 1
        span *= 2
        level += 1
    return jnp.concatenate(x, axis=0)


def taken(rows, lanes):
    return jnp.take_along_axis(rows, jnp.broadcast_to(lanes, rows.shape), axis=1)


def negative_residual(s, before, inj, cap, gain, gs):
    return inj - cap * (s - before) - mapped(gs, s) - gain * jnp.tanh(s)


def load_kernel(
    eye, s, inj, cap, g, mask, gain, k, d, j, r,
    js, ks, gs, nr, c, ss, w, ps, ls,
):
    points, width = s.shape
    js[...] = split_cols(j[...])
    ks[...] = split_cols(k[...])
    gs[...] = split_cols(g[...] * mask[...].astype(F32))
    volts = s[...]
    before = jnp.concatenate([jnp.zeros((1, width), F32), volts[: points - 1]], axis=0)
    nr[...] = negative_residual(volts, before, inj[...], cap[...], gain[...], gs[...])
    suffix_products(r, eye[...], ss, w)
    prefix_products(r, ps, ls)
    c[...] = mapped_each(d, nr[...])


def start_kernel(
    halo_ref, s_ref, cap_ref, bnd_ref, d_ref, nr_ref, c_ref,
    halo_out_ref, new_nr_ref, new_c_ref, msg_ref,
):
    points = s_ref.shape[0]
    halo = halo_ref[points - 1 :]
    halo_out_ref[...] = halo
    extra = cap_ref[...] * halo
    new_nr_ref[...] = nr_ref[...]
    new_nr_ref[:1] = nr_ref[:1] + extra
    new_c_ref[...] = c_ref[...]
    new_c_ref[:1] = c_ref[:1] + mapped_each(d_ref[:1], extra)
    msg_ref[:points] = taken(new_c_ref[...], bnd_ref[...])
    msg_ref[points:] = taken(s_ref[...], bnd_ref[...])


def inflow_applied(got_ref, nr_ref, d_ref, js_ref, ks_ref):
    points = nr_ref.shape[0]
    got = got_ref[...]
    nr = nr_ref[...] + mapped(js_ref[...], got[:points]) + mapped(ks_ref[...], got[points:])
    return mapped_each(d_ref, nr)


def hop_kernel(
    place, got_ref, c_ref, msg_ref, nr_ref, d_ref, js_ref, ks_ref, bnd_ref, new_c_ref, new_msg_ref
):
    points = c_ref.shape[0]
    here = lax.axis_index("dom") == place
    new_msg_ref[points:] = msg_ref[points:]

    @pl.when(here)
    def _():
        c = inflow_applied(got_ref, nr_ref, d_ref, js_ref, ks_ref)
        new_c_ref[...] = c
        new_msg_ref[:points] = taken(c, bnd_ref[...])

    @pl.when(jnp.logical_not(here))
    def _():
        new_c_ref[...] = c_ref[...]
        new_msg_ref[:points] = msg_ref[:points]


def last_hop_kernel(
    place, got_ref, c_ref, nr_ref, d_ref, js_ref, ks_ref, ss_ref, new_c_ref, tail_ref, f_ref
):
    points, width = c_ref.shape
    here = lax.axis_index("dom") == place

    @pl.when(here)
    def _():
        new_c_ref[...] = inflow_applied(got_ref, nr_ref, d_ref, js_ref, ks_ref)

    @pl.when(jnp.logical_not(here))
    def _():
        new_c_ref[...] = c_ref[...]

    total = mapped_each(ss_ref, new_c_ref[...])
    shift = 1
    while shift < points:
        total = total + jnp.concatenate([total[shift:], jnp.zeros((shift, width), F32)], axis=0)
        shift *= 2
    tail_ref[:points] = jnp.concatenate([total[1:], jnp.zeros((1, width), F32)], axis=0)
    tail_ref[points:] = jnp.broadcast_to(total[:1], (8, width))
    f_ref[...] = jnp.broadcast_to(total[:1], (8, width))


def is_later(distance):
    return (lax.axis_index("tm") // distance) % 2 == 1


def first_level_kernel(
    distance, mw_ref, mf_ref, gw_ref, gf_ref,
    tw_ref, tf_ref, a_ref, bw_ref, bf_ref, aw_ref, af_ref,
):
    width = mw_ref.shape[0]
    later = is_later(distance)
    mw, mf, gw, gf = mw_ref[...], mf_ref[...], gw_ref[...], gf_ref[...]
    a = jnp.where(later, mw, gw)
    tw_ref[...] = times(a, jnp.where(later, gw, mw))
    a_split = split_cols(a)
    a_ref[...] = a_split
    tf_ref[...] = mapped(a_split, jnp.where(later, gf, mf)) + jnp.where(later, mf, gf)
    eye = identity(width)
    bw_ref[...] = jnp.where(later, gw, eye)
    bf_ref[...] = jnp.where(later, gf, 0.0)
    aw_ref[...] = jnp.where(later, eye, gw)
    af_ref[...] = jnp.where(later, 0.0, gf)


def next_level_kernel(
    distance, mw_ref, mf_ref, gw_ref, gf_ref, bw_ref, bf_ref, aw_ref, af_ref,
    tw_ref, tf_ref, a_ref, x_ref, nbw_ref, nbf_ref, naw_ref, naf_ref,
):
    later = is_later(distance)
    mw, mf, gw, gf = mw_ref[...], mf_ref[...], gw_ref[...], gf_ref[...]
    bw, bf, aw, af = bw_ref[...], bf_ref[...], aw_ref[...], af_ref[...]
    a = jnp.where(later, mw, gw)
    tw_ref[...] = times(a, jnp.where(later, gw, mw))
    a_split = split_cols(a)
    a_ref[...] = a_split
    tf_ref[...] = mapped(a_split, jnp.where(later, gf, mf)) + jnp.where(later, mf, gf)
    x = jnp.where(later, bw, gw)
    joined = times(x, jnp.where(later, gw, aw))
    x_split = split_cols(x)
    x_ref[...] = x_split
    sums = mapped(x_split, jnp.where(later, gf, af)) + jnp.where(later, bf, gf)
    nbw_ref[...] = jnp.where(later, joined, bw)
    nbf_ref[...] = jnp.where(later, sums, bf)
    naw_ref[...] = jnp.where(later, aw, joined)
    naf_ref[...] = jnp.where(later, af, sums)


def again_first_kernel(distance, mf_ref, gf_ref, a_ref, tf_ref, bf_ref, af_ref):
    later = is_later(distance)
    mf, gf = mf_ref[...], gf_ref[...]
    tf_ref[...] = mapped(a_ref[...], jnp.where(later, gf, mf)) + jnp.where(later, mf, gf)
    bf_ref[...] = jnp.where(later, gf, 0.0)
    af_ref[...] = jnp.where(later, 0.0, gf)


def again_next_kernel(
    distance, mf_ref, gf_ref, bf_ref, af_ref, a_ref, x_ref, tf_ref, nbf_ref, naf_ref
):
    later = is_later(distance)
    mf, gf, bf, af = mf_ref[...], gf_ref[...], bf_ref[...], af_ref[...]
    tf_ref[...] = mapped(a_ref[...], jnp.where(later, gf, mf)) + jnp.where(later, mf, gf)
    sums = mapped(x_ref[...], jnp.where(later, gf, af)) + jnp.where(later, bf, gf)
    nbf_ref[...] = jnp.where(later, sums, bf)
    naf_ref[...] = jnp.where(later, af, sums)


def local_kernel(c_ref, ls_ref, tail_ref, aw_ref, af_ref, s_ref, base_ref, v_ref):
    base_ref[...] = s_ref[...] + scanned(c_ref[...], ls_ref)
    v_ref[...] = mapped(split_cols(aw_ref[...]), tail_ref[...]) + af_ref[:1]


def turn_kernel(
    v_ref, got_ref, bw_ref, bf_ref, ps_ref, base_ref,
    halo_ref, inj_ref, cap_ref, gain_ref, gs_ref, d_ref, bnd_ref,
    new_s_ref, nr_ref, c_ref, msg_ref,
):
    points, width = base_ref.shape
    v = mapped(split_cols(got_ref[:width]), v_ref[...]) + got_ref[width : width + 1]
    v = mapped(split_cols(bw_ref[...]), v) + bf_ref[:1]
    s = base_ref[...] + mapped_each(ps_ref, v[:points])
    new_s_ref[...] = s
    before = jnp.concatenate([halo_ref[...] + v[points : points + 1], s[: points - 1]], axis=0)
    nr = negative_residual(s, before, inj_ref[...], cap_ref[...], gain_ref[...], gs_ref[...])
    c = mapped_each(d_ref, nr)
    nr_ref[...] = nr
    c_ref[...] = c
    msg_ref[:points] = taken(c, bnd_ref[...])
    msg_ref[points:] = taken(s, bnd_ref[...])


def last_local_kernel(
    c_ref, ls_ref, tail_ref, aw_ref, af_ref, gw_ref, bw_ref, bf_ref, ps_ref, s_ref, base_ref
):
    points, width = s_ref.shape
    v = mapped(split_cols(aw_ref[...]), tail_ref[:points]) + af_ref[:1]
    v = mapped(split_cols(gw_ref[:width]), v)
    v = mapped(split_cols(bw_ref[...]), v) + bf_ref[:1]
    base_ref[...] = s_ref[...] + scanned(c_ref[...], ls_ref) + mapped_each(ps_ref, v)


def end_kernel(gf_ref, bw_ref, ps_ref, base_ref, s_ref):
    points, width = base_ref.shape
    v = mapped(split_cols(bw_ref[...]), gf_ref[...])[:1]
    s_ref[...] = base_ref[...] + mapped_each(ps_ref, jnp.broadcast_to(v, (points, width)))


def exchanged(value, distance):
    devices = range(lax.axis_size("tm"))
    return jax.tree.map(lambda v: lax.ppermute(v, "tm", [(i, i ^ distance) for i in devices]), value)


def handed_on(message, place):
    count = lax.axis_size("dom")
    pairs = []
    for i in range(0, count, 2):
        a, b = (i + place - 1) % count, (i + place) % count
        pairs += [(a, b), (b, a)]
    return lax.ppermute(message, "dom", pairs)


def per_device(
    starting_voltage_guess,
    injected_amperes,
    capacitance,
    conductance,
    block_pattern,
    device_gain,
    link_weight,
    boundary_vertex_list,
    diagonal_reciprocals,
    boundary_jacobian,
    transfer,
):
    points, _, width = starting_voltage_guess.shape
    segments, parts = lax.axis_size("tm"), lax.axis_size("dom")
    vec, eight, square = ((points, width), F32), ((8, width), F32), ((width, width), F32)
    square_split = ((width, 2 * width), BF16)
    many = ((points, width, width), F32)
    one = ((1, width), F32)
    longer = ((points + 8, width), F32)
    msg_shape = ((2 * points, width), F32)
    levels = points.bit_length() - 1

    halo = lax.ppermute(
        starting_voltage_guess, "tm", [(i, (i + 1) % segments) for i in range(segments)]
    )
    s, inj = starting_voltage_guess[:, 0], injected_amperes[:, 0]
    cap, gain, bnd = capacitance, device_gain, boundary_vertex_list
    d = diagonal_reciprocals[:, 0, 0]
    (eye,) = call(
        identity_kernel, [square],
        cost=pl.CostEstimate(flops=2**33, bytes_accessed=2**25, transcendentals=0),
    )
    js, ks, gs, nr, c, ss, w, ps, ls = call(
        load_kernel,
        [square_split] * 3
        + [vec, vec, many, square, many, ((levels * points // 2, width, width), F32)],
        eye, s, inj, cap, conductance[0], block_pattern[0], gain, link_weight[0], d,
        boundary_jacobian[0], transfer[:, 0, 0],
    )
    halo, nr, c, msg = call(
        start_kernel, [one, vec, vec, msg_shape], halo[:, 0], s, cap, bnd, d, nr, c
    )
    distances = [2**k for k in range(segments.bit_length() - 1)]
    kept = {}
    for step in range(ITERS):
        for place in range(1, parts):
            got = handed_on(msg, place)
            if place < parts - 1:
                c, msg = call(
                    functools.partial(hop_kernel, place), [vec, msg_shape],
                    got, c, msg, nr, d, js, ks, bnd,
                )
        c, tail, f = call(
            functools.partial(last_hop_kernel, parts - 1), [vec, longer, eight],
            got, c, nr, d, js, ks, ss,
        )
        for level, distance in enumerate(distances[:-1]):
            if step == 0:
                both = exchanged(jnp.concatenate([w, f], axis=0), distance)
                got = both[:width], both[width:]
                if level == 0:
                    w, f, kept["a", 0], bw, bf, aw, af = call(
                        functools.partial(first_level_kernel, distance),
                        [square, eight, square_split, square, eight, square, eight],
                        w, f, *got,
                    )
                else:
                    w, f, kept["a", level], kept["x", level], bw, bf, aw, af = call(
                        functools.partial(next_level_kernel, distance),
                        [square, eight, square_split, square_split, square, eight, square, eight],
                        w, f, *got, bw, bf, aw, af,
                    )
            else:
                got = exchanged(f, distance)
                if level == 0:
                    f, bf, af = call(
                        functools.partial(again_first_kernel, distance), [eight] * 3,
                        f, got, kept["a", 0],
                    )
                else:
                    f, bf, af = call(
                        functools.partial(again_next_kernel, distance), [eight] * 3,
                        f, got, bf, af, kept["a", level], kept["x", level],
                    )
        if step == 0:
            last = exchanged(jnp.concatenate([w, f], axis=0), distances[-1])
        else:
            last_f = exchanged(f, distances[-1])
        if step < ITERS - 1:
            base, v = call(local_kernel, [vec, longer], c, ls, tail, aw, af, s)
            s, nr, c, msg = call(
                turn_kernel, [vec, vec, vec, msg_shape],
                v, last, bw, bf, ps, base, halo, inj, cap, gain, gs, d, bnd,
            )
        else:
            (base,) = call(last_local_kernel, [vec], c, ls, tail, aw, af, last, bw, bf, ps, s)
            (s,) = call(end_kernel, [vec], last_f, bw, ps, base)
    return s[:, None]


def solution(mesh):
    in_specs = (
        P("tm", "dom", None),
        P("tm", "dom", None),
        P("dom", None),
        P("dom", None, None),
        P("dom", None, None),
        P("dom", None),
        P("dom", None, None),
        P("dom", None),
        P("tm", "dom", None, None, None),
        P("dom", None, None),
        P("tm", "dom", None, None, None),
    )
    out_specs = P("tm", "dom", None)
    return jax.shard_map(
        per_device, mesh=mesh, in_specs=in_specs, out_specs=out_specs, check_vma=False
    )
```

```python
import functools

import jax
import jax.numpy as jnp
from jax import lax
from jax.experimental import pallas as pl
from jax.experimental.pallas import tpu as pltpu
from jax.sharding import PartitionSpec as P

F32 = jnp.float32
BF16 = jnp.bfloat16
PAIR = 2


def halves(x):
    hi = x.astype(BF16)
    return hi, (x - hi.astype(F32)).astype(BF16)


def split_cols(matrix):
    return jnp.concatenate(halves(matrix), axis=1)


def split_rows(vectors):
    hi, lo = halves(vectors)
    hi, lo = hi.astype(F32), lo.astype(F32)
    top = jnp.concatenate([hi, hi], axis=1)
    low = jnp.concatenate([lo, jnp.zeros_like(lo)], axis=1)
    return jnp.concatenate([top, low], axis=0).astype(BF16)


def dot_nt(a, b):
    return lax.dot_general(a, b, (((1,), (1,)), ((), ())), preferred_element_type=F32)


def times(a, b):
    ah, al = halves(a)
    bh, bl = halves(b)
    left = jnp.concatenate([ah, al, ah], axis=1)
    right = jnp.concatenate([bh, bh, bl], axis=0)
    return jnp.dot(left, right, preferred_element_type=F32)


def mapped(matrix_split, vectors):
    count = vectors.shape[0]
    both = dot_nt(split_rows(vectors), matrix_split)
    return both[:count] + both[count:]


def mapped_each(matrices, vectors):
    rows = []
    for r in range(vectors.shape[0]):
        products = matrices[r] * vectors[r : r + 1, :]
        rows.append(jnp.sum(products.T, axis=0, keepdims=True))
    return jnp.concatenate(rows, axis=0)


def call(kernel, outs, *args, cost=None):
    vmem = pl.BlockSpec(memory_space=pltpu.VMEM)
    return pl.pallas_call(
        kernel,
        out_shape=[jax.ShapeDtypeStruct(s, d) for s, d in outs],
        in_specs=[vmem] * len(args),
        out_specs=[vmem] * len(outs),
        cost_estimate=cost,
        compiler_params=pltpu.CompilerParams(vmem_limit_bytes=24 * 2**20),
    )(*args)


def identity(width):
    return (
        lax.broadcasted_iota(jnp.int32, (width, width), 0)
        == lax.broadcasted_iota(jnp.int32, (width, width), 1)
    ).astype(F32)


def halo_kernel(s_ref, near_ref, msg_ref):
    points, width = s_ref.shape
    msg_ref[:4] = jnp.broadcast_to(near_ref[points - 1 :], (4, width))
    msg_ref[4:] = jnp.broadcast_to(s_ref[points - 1 :], (4, width))


def ones_kernel(one_ref):
    one_ref[...] = jnp.ones(one_ref.shape, F32)


def pack_kernel(one_ref, g_ref, mask_ref, k_ref, j_ref, inj_ref, cap_ref, gain_ref, bnd_ref, pack_ref):
    points, width = inj_ref.shape
    pack_ref[:width] = g_ref[...] * (mask_ref[...] * one_ref[...])
    pack_ref[width : 2 * width] = k_ref[...]
    pack_ref[2 * width : 3 * width] = j_ref[...]
    at = 3 * width
    pack_ref[at : at + points] = inj_ref[...]
    at += points
    for one in (cap_ref[...], gain_ref[...], bnd_ref[...].astype(F32)):
        pack_ref[at : at + 8] = jnp.broadcast_to(one, (8, width))
        at += 8


def unpacked(pack_ref, points):
    width = pack_ref.shape[1]
    at = 3 * width
    inj = pack_ref[at : at + points]
    at += points
    cap, gain, bnd = (pack_ref[at + 8 * i : at + 8 * i + 1] for i in range(3))
    return inj, cap, gain, bnd.astype(jnp.int32)


def suffix_kernel(lo_ref, hi_ref, s_ref, w_ref):
    points, width = lo_ref.shape[0], lo_ref.shape[1]
    for g, r_ref in enumerate((lo_ref, hi_ref)):
        u = [r_ref[i] for i in range(points)]
        span = 1
        while span < points:
            for base in range(0, points, 2 * span):
                prod = times(u[base + span], jnp.concatenate(u[base : base + span], axis=1))
                for i in range(span):
                    u[base + i] = prod[:, i * width : (i + 1) * width]
            span *= 2
        w_ref[g * width : (g + 1) * width] = u[0]
        for i in range(points - 1):
            s_ref[g * points + i] = u[i + 1]
        s_ref[(g + 1) * points - 1] = identity(width)


def prefix_kernel(lo_ref, hi_ref, p_ref, l_ref):
    points, width = lo_ref.shape[0], lo_ref.shape[1]
    slot = 0
    for g, r_ref in enumerate((lo_ref, hi_ref)):
        q = [r_ref[i] for i in range(points)]
        span = 1
        while span < points:
            for base in range(0, points, 2 * span):
                upper = q[base + span : base + 2 * span]
                for matrix in upper:
                    l_ref[slot] = matrix
                    slot += 1
                prod = times(jnp.concatenate(upper, axis=0), q[base + span - 1])
                for i in range(span):
                    q[base + span + i] = prod[i * width : (i + 1) * width]
            span *= 2
        for i in range(points):
            p_ref[g * points + i] = q[i]


def scanned(c, l_ref, slot):
    points = c.shape[0]
    x = [c[i : i + 1, :] for i in range(points)]
    span = 1
    while span < points:
        for base in range(0, points, 2 * span):
            head = x[base + span - 1]
            for i in range(base + span, base + 2 * span):
                x[i] = x[i] + mapped_each(l_ref[slot : slot + 1], head)
                slot += 1
        span *= 2
    return jnp.concatenate(x, axis=0)


def taken(rows, lanes):
    return jnp.take_along_axis(rows, jnp.broadcast_to(lanes, rows.shape), axis=1)


def negative_residual(s, halo, inj, cap, gain, gs):
    before = jnp.concatenate([halo, s[: s.shape[0] - 1]], axis=0)
    return inj - cap * (s - before) - mapped(gs, s) - gain * jnp.tanh(s)


def corrected(nr, c_before, s_before, d_ref, js, ks):
    return mapped_each(d_ref, nr + mapped(js, c_before) + mapped(ks, s_before))


def pair_corrected(nr, s_lo, c_lo, bnd_lo, d_hi_ref, js, ks):
    return corrected(nr, taken(c_lo, bnd_lo), taken(s_lo, bnd_lo), d_hi_ref, js, ks)


def correct_both(
    s_lo, s_hi, halo_lo, halo_hi, pack_lo, pack_hi, lo_maps, hi_maps, d_lo, d_hi, nr_ref, c_ref, msg_ref
):
    points = s_lo.shape[0]
    inj_lo, cap_lo, gain_lo, bnd_lo = unpacked(pack_lo, points)
    inj_hi, cap_hi, gain_hi, bnd_hi = unpacked(pack_hi, points)
    nr_lo = negative_residual(s_lo, halo_lo, inj_lo, cap_lo, gain_lo, lo_maps[0])
    nr_hi = negative_residual(s_hi, halo_hi, inj_hi, cap_hi, gain_hi, hi_maps[0])
    c_lo = mapped_each(d_lo, nr_lo)
    c_hi = pair_corrected(nr_hi, s_lo, c_lo, bnd_lo, d_hi, hi_maps[2], hi_maps[1])
    nr_ref[:points], nr_ref[points:] = nr_lo, nr_hi
    c_ref[:points], c_ref[points:] = c_lo, c_hi
    msg_ref[:points] = taken(c_hi, bnd_hi)
    msg_ref[points:] = taken(s_hi, bnd_hi)


def early_kernel(s_lo, s_hi, pack_lo, pack_hi, d_lo, d_hi, maps_ref, nr_ref, c_ref, msg_ref):
    points, width = s_lo.shape
    for i in range(3):
        rows = slice(i * width, (i + 1) * width)
        maps_ref[i] = split_cols(pack_lo[rows])
        maps_ref[3 + i] = split_cols(pack_hi[rows])
    none = jnp.zeros((1, width), F32)
    correct_both(
        s_lo[...], s_hi[...], none, none, pack_lo, pack_hi,
        [maps_ref[i] for i in range(3)], [maps_ref[i] for i in range(3, 6)],
        d_lo, d_hi, nr_ref, c_ref, msg_ref,
    )


def first_kernel(
    halo_ref, s_lo, s_hi, pack_lo, pack_hi, maps_ref, d_lo, d_hi, old_nr, old_c, old_msg,
    s_ref, nr_ref, c_ref, msg_ref,
):
    points = s_lo.shape[0]
    _, cap_lo, _, bnd_lo = unpacked(pack_lo, points)
    _, cap_hi, _, bnd_hi = unpacked(pack_hi, points)
    s_ref[:points], s_ref[points:] = s_lo[...], s_hi[...]
    nr_ref[...], c_ref[...], msg_ref[...] = old_nr[...], old_c[...], old_msg[...]
    nr_lo = old_nr[:1] + cap_lo * halo_ref[:1]
    nr_hi = old_nr[points : points + 1] + cap_hi * halo_ref[4:5]
    c_lo = mapped_each(d_lo, nr_lo)
    came = mapped(maps_ref[5], taken(jnp.broadcast_to(c_lo, (8, c_lo.shape[1])), bnd_lo))
    came = came + mapped(maps_ref[4], taken(s_lo[:8], bnd_lo))
    c_hi = mapped_each(d_hi, nr_hi + came[:1])
    nr_ref[:1], nr_ref[points : points + 1] = nr_lo, nr_hi
    c_ref[:1], c_ref[points : points + 1] = c_lo, c_hi
    msg_ref[:1] = taken(jnp.broadcast_to(c_hi, (8, c_hi.shape[1])), bnd_hi)[:1]


def second_kernel(
    got_ref, s_ref, nr_ref, c_ref, pack_lo, maps_ref, d_lo, d_hi, ss_ref, new_c_ref, tail_ref, f_ref
):
    points, width = got_ref.shape[0] // 2, got_ref.shape[1]
    second_pair = lax.axis_index("dom") >= PAIR

    @pl.when(second_pair)
    def _():
        bnd_lo = unpacked(pack_lo, points)[3]
        c_lo = corrected(
            nr_ref[:points], got_ref[:points], got_ref[points:], d_lo, maps_ref[2], maps_ref[1]
        )
        new_c_ref[:points] = c_lo
        new_c_ref[points:] = pair_corrected(
            nr_ref[points:], s_ref[:points], c_lo, bnd_lo, d_hi, maps_ref[5], maps_ref[4]
        )

    @pl.when(jnp.logical_not(second_pair))
    def _():
        new_c_ref[...] = c_ref[...]

    each = mapped_each(ss_ref, new_c_ref[...])
    for g in range(PAIR):
        total = each[g * points : (g + 1) * points]
        shift = 1
        while shift < points:
            total = total + jnp.concatenate(
                [total[shift:], jnp.zeros((shift, width), F32)], axis=0
            )
            shift *= 2
        at = g * (points + 8)
        tail_ref[at : at + points] = jnp.concatenate(
            [total[1:], jnp.zeros((1, width), F32)], axis=0
        )
        whole = jnp.broadcast_to(total[:1], (8, width))
        tail_ref[at + points : at + points + 8] = whole
        f_ref[8 * g : 8 * g + 8] = whole


def is_later(distance):
    return (lax.axis_index("tm") // distance) % 2 == 1


def sections(width):
    return [
        (slice(g * width, (g + 1) * width), slice(8 * g, 8 * g + 8)) for g in range(PAIR)
    ]


def first_level_kernel(
    distance, mw_ref, mf_ref, got_ref, tw_ref, tf_ref, a_ref, bw_ref, bf_ref, aw_ref, af_ref
):
    width = mw_ref.shape[1]
    later = is_later(distance)
    eye = identity(width)
    for wide, short in sections(width):
        mw, mf, gw = mw_ref[wide], mf_ref[short], got_ref[wide]
        gf = got_ref[PAIR * width + short.start : PAIR * width + short.stop]
        a = jnp.where(later, mw, gw)
        tw_ref[wide] = times(a, jnp.where(later, gw, mw))
        a_split = split_cols(a)
        a_ref[wide] = a_split
        tf_ref[short] = mapped(a_split, jnp.where(later, gf, mf)) + jnp.where(later, mf, gf)
        bw_ref[wide] = jnp.where(later, gw, eye)
        bf_ref[short] = jnp.where(later, gf, 0.0)
        aw_ref[wide] = jnp.where(later, eye, gw)
        af_ref[short] = jnp.where(later, 0.0, gf)


def next_level_kernel(
    distance, mw_ref, mf_ref, got_ref, bw_ref, bf_ref, aw_ref, af_ref,
    tw_ref, tf_ref, a_ref, x_ref, nbw_ref, nbf_ref, naw_ref, naf_ref,
):
    width = mw_ref.shape[1]
    later = is_later(distance)
    for wide, short in sections(width):
        mw, mf, gw = mw_ref[wide], mf_ref[short], got_ref[wide]
        gf = got_ref[PAIR * width + short.start : PAIR * width + short.stop]
        bw, bf, aw, af = bw_ref[wide], bf_ref[short], aw_ref[wide], af_ref[short]
        a = jnp.where(later, mw, gw)
        tw_ref[wide] = times(a, jnp.where(later, gw, mw))
        a_split = split_cols(a)
        a_ref[wide] = a_split
        tf_ref[short] = mapped(a_split, jnp.where(later, gf, mf)) + jnp.where(later, mf, gf)
        x = jnp.where(later, bw, gw)
        joined = times(x, jnp.where(later, gw, aw))
        x_split = split_cols(x)
        x_ref[wide] = x_split
        sums = mapped(x_split, jnp.where(later, gf, af)) + jnp.where(later, bf, gf)
        nbw_ref[wide] = jnp.where(later, joined, bw)
        nbf_ref[short] = jnp.where(later, sums, bf)
        naw_ref[wide] = jnp.where(later, aw, joined)
        naf_ref[short] = jnp.where(later, af, sums)


def again_first_kernel(distance, mf_ref, gf_ref, a_ref, tf_ref, bf_ref, af_ref):
    later = is_later(distance)
    for wide, short in sections(a_ref.shape[0] // PAIR):
        mf, gf = mf_ref[short], gf_ref[short]
        tf_ref[short] = mapped(a_ref[wide], jnp.where(later, gf, mf)) + jnp.where(later, mf, gf)
        bf_ref[short] = jnp.where(later, gf, 0.0)
        af_ref[short] = jnp.where(later, 0.0, gf)


def again_next_kernel(
    distance, mf_ref, gf_ref, bf_ref, af_ref, a_ref, x_ref, tf_ref, nbf_ref, naf_ref
):
    later = is_later(distance)
    for wide, short in sections(a_ref.shape[0] // PAIR):
        mf, gf, bf, af = mf_ref[short], gf_ref[short], bf_ref[short], af_ref[short]
        tf_ref[short] = mapped(a_ref[wide], jnp.where(later, gf, mf)) + jnp.where(later, mf, gf)
        sums = mapped(x_ref[wide], jnp.where(later, gf, af)) + jnp.where(later, bf, gf)
        nbf_ref[short] = jnp.where(later, sums, bf)
        naf_ref[short] = jnp.where(later, af, sums)


def local_kernel(c_ref, ls_ref, tail_ref, aw_ref, af_ref, s_ref, base_ref, v_ref):
    points, width = s_ref.shape[0] // PAIR, s_ref.shape[1]
    for g, (wide, short) in enumerate(sections(width)):
        rows = slice(g * points, (g + 1) * points)
        long = slice(g * (points + 8), (g + 1) * (points + 8))
        slot = g * (ls_ref.shape[0] // PAIR)
        base_ref[rows] = s_ref[rows] + scanned(c_ref[rows], ls_ref, slot)
        v_ref[long] = mapped(split_cols(aw_ref[wide]), tail_ref[long]) + af_ref[short][:1]


def turn_kernel(
    v_ref, got_ref, bw_ref, bf_ref, ps_ref, base_ref, halo_ref, pack_lo, pack_hi, maps_ref,
    d_lo, d_hi, s_ref, nr_ref, c_ref, msg_ref,
):
    points, width = s_ref.shape[0] // PAIR, s_ref.shape[1]
    came = []
    for g, (wide, short) in enumerate(sections(width)):
        long = slice(g * (points + 8), (g + 1) * (points + 8))
        gf = got_ref[PAIR * width + 8 * g : PAIR * width + 8 * g + 1]
        v = mapped(split_cols(got_ref[wide]), v_ref[long]) + gf
        came.append(mapped(split_cols(bw_ref[wide]), v) + bf_ref[short][:1])
    moved = mapped_each(ps_ref, jnp.concatenate([v[:points] for v in came], axis=0))
    s = base_ref[...] + moved
    s_ref[...] = s
    correct_both(
        s[:points], s[points:],
        halo_ref[:1] + came[0][points : points + 1],
        halo_ref[4:5] + came[1][points : points + 1],
        pack_lo, pack_hi, [maps_ref[i] for i in range(3)], [maps_ref[i] for i in range(3, 6)],
        d_lo, d_hi, nr_ref, c_ref, msg_ref,
    )


def last_local_kernel(
    c_ref, ls_ref, tail_ref, aw_ref, af_ref, gw_ref, bw_ref, bf_ref, ps_ref, s_ref, base_ref
):
    points, width = s_ref.shape[0] // PAIR, s_ref.shape[1]
    came = []
    for g, (wide, short) in enumerate(sections(width)):
        at = g * (points + 8)
        v = mapped(split_cols(aw_ref[wide]), tail_ref[at : at + points]) + af_ref[short][:1]
        v = mapped(split_cols(gw_ref[wide]), v)
        came.append(mapped(split_cols(bw_ref[wide]), v) + bf_ref[short][:1])
    moved = mapped_each(ps_ref, jnp.concatenate(came, axis=0))
    for g in range(PAIR):
        rows = slice(g * points, (g + 1) * points)
        slot = g * (ls_ref.shape[0] // PAIR)
        base_ref[rows] = s_ref[rows] + moved[rows] + scanned(c_ref[rows], ls_ref, slot)


def end_kernel(gf_ref, bw_ref, ps_ref, base_ref, s_ref):
    points, width = s_ref.shape[0] // PAIR, s_ref.shape[1]
    came = []
    for wide, short in sections(width):
        v = mapped(split_cols(bw_ref[wide]), gf_ref[short])[:1]
        came.append(jnp.broadcast_to(v, (points, width)))
    s_ref[...] = base_ref[...] + mapped_each(ps_ref, jnp.concatenate(came, axis=0))


def choose_kernel(both_ref, got_ref, s_ref):
    points = s_ref.shape[0]
    odd = lax.axis_index("dom") % 2 == 1
    s_ref[...] = jnp.where(odd, both_ref[points:], got_ref[:points])


def exchanged(value, distance):
    return lax.ppermute(
        value, "tm", [(i, i ^ distance) for i in range(lax.axis_size("tm"))]
    )


def swapped(value, distance):
    return lax.ppermute(value, "dom", [(i, i ^ distance) for i in range(lax.axis_size("dom"))])


def both_partitions(s, nr, c, msg, halo, maps, pack_lo, pack_hi, d_lo, d_hi, r_lo, r_hi):
    points, width = s.shape[0] // PAIR, s.shape[1]
    vec, square = ((PAIR * points, width), F32), ((PAIR * width, width), F32)
    square_split = ((PAIR * width, 2 * width), BF16)
    eight = ((PAIR * 8, width), F32)
    longer = ((PAIR * (points + 8), width), F32)
    many = ((PAIR * points, width, width), F32)
    steps = (points.bit_length() - 1) * points // 2
    distances = [2**k for k in range(lax.axis_size("tm").bit_length() - 1)]

    got = swapped(msg, 2)
    ss, w = call(suffix_kernel, [many, square], r_lo, r_hi)
    ps, ls = call(prefix_kernel, [many, ((PAIR * steps, width, width), F32)], r_lo, r_hi)
    c, tail, f = call(
        second_kernel, [vec, longer, eight], got, s, nr, c, pack_lo, maps, d_lo, d_hi, ss
    )
    kept = []
    for level, distance in enumerate(distances[:-1]):
        got = exchanged(jnp.concatenate([w, f], axis=0), distance)
        if level == 0:
            w, f, a, bw, bf, aw, af = call(
                functools.partial(first_level_kernel, distance),
                [square, eight, square_split, square, eight, square, eight], w, f, got,
            )
            kept.append((a,))
        else:
            w, f, a, x, bw, bf, aw, af = call(
                functools.partial(next_level_kernel, distance),
                [square, eight, square_split, square_split, square, eight, square, eight],
                w, f, got, bw, bf, aw, af,
            )
            kept.append((a, x))
    last = exchanged(jnp.concatenate([w, f], axis=0), distances[-1])
    base, v = call(local_kernel, [vec, longer], c, ls, tail, aw, af, s)
    s, nr, c, msg = call(
        turn_kernel, [vec] * 4,
        v, last, bw, bf, ps, base, halo, pack_lo, pack_hi, maps, d_lo, d_hi,
    )
    got = swapped(msg, 2)
    c, tail, f = call(
        second_kernel, [vec, longer, eight], got, s, nr, c, pack_lo, maps, d_lo, d_hi, ss
    )
    for level, distance in enumerate(distances[:-1]):
        got = exchanged(f, distance)
        if level == 0:
            f, bf, af = call(
                functools.partial(again_first_kernel, distance), [eight] * 3, f, got, *kept[0]
            )
        else:
            f, bf, af = call(
                functools.partial(again_next_kernel, distance), [eight] * 3,
                f, got, bf, af, *kept[level],
            )
    got = exchanged(f, distances[-1])
    (base,) = call(last_local_kernel, [vec], c, ls, tail, aw, af, last, bw, bf, ps, s)
    return call(end_kernel, [vec], got, bw, ps, base)[0]


def per_device(
    starting_voltage_guess,
    injected_amperes,
    capacitance,
    conductance,
    block_pattern,
    device_gain,
    link_weight,
    boundary_vertex_list,
    diagonal_reciprocals,
    boundary_jacobian,
    transfer,
):
    points, _, width = starting_voltage_guess.shape
    segments = lax.axis_size("tm")
    (one,) = call(
        ones_kernel, [((1, width), F32)],
        cost=pl.CostEstimate(flops=2**33, bytes_accessed=2**25, transcendentals=0),
    )
    mask = jnp.broadcast_to(block_pattern[0].astype(F32), (1, width))
    s = starting_voltage_guess[:, 0]
    near_s = swapped(starting_voltage_guess, 1)[:, 0]
    d, r, near_s, mask, one = lax.optimization_barrier(
        (diagonal_reciprocals, transfer, near_s, mask, one)
    )
    d, near_d = d[:, 0, 0], swapped(d, 1)[:, 0, 0]
    r, near_r = r[:, 0, 0], swapped(r, 1)[:, 0, 0]
    (rows,) = call(halo_kernel, [((8, width), F32)], s, near_s)
    halo = lax.ppermute(rows, "tm", [(i, (i + 1) % segments) for i in range(segments)])
    (pack,) = call(
        pack_kernel, [((3 * width + points + 24, width), F32)],
        one, conductance[0], mask, link_weight[0], boundary_jacobian[0],
        injected_amperes[:, 0], capacitance, device_gain, boundary_vertex_list,
    )
    near_pack = swapped(pack, 1)
    vec = ((PAIR * points, width), F32)
    maps, nr, c, msg = call(
        early_kernel, [((6, width, 2 * width), BF16), vec, vec, vec],
        near_s, s, near_pack, pack, near_d, d,
    )
    s, nr, c, msg = call(
        first_kernel, [vec] * 4,
        halo, near_s, s, near_pack, pack, maps, near_d, d, nr, c, msg,
    )
    odd = lax.axis_index("dom") % 2 == 1
    both = lax.cond(
        odd,
        both_partitions,
        lambda s, *rest: s,
        s, nr, c, msg, halo, maps, near_pack, pack, near_d, d, near_r, r,
    )
    (s,) = call(choose_kernel, [((points, width), F32)], both, swapped(both, 1))
    return s[:, None]


def solution(mesh):
    in_specs = (
        P("tm", "dom", None),
        P("tm", "dom", None),
        P("dom", None),
        P("dom", None, None),
        P("dom", None, None),
        P("dom", None),
        P("dom", None, None),
        P("dom", None),
        P("tm", "dom", None, None, None),
        P("dom", None, None),
        P("tm", "dom", None, None, None),
    )
    out_specs = P("tm", "dom", None)
    return jax.shard_map(
        per_device, mesh=mesh, in_specs=in_specs, out_specs=out_specs, check_vma=False
    )
```

```python
import functools

import jax
import jax.numpy as jnp
from jax import lax
from jax.experimental import pallas as pl
from jax.experimental.pallas import tpu as pltpu
from jax.sharding import PartitionSpec as P

F32 = jnp.float32
BF16 = jnp.bfloat16
PAIR = 2


def halves(x):
    hi = x.astype(BF16)
    return hi, (x - hi.astype(F32)).astype(BF16)


def split_cols(matrix):
    return jnp.concatenate(halves(matrix), axis=1)


def split_rows(vectors):
    hi, lo = halves(vectors)
    hi, lo = hi.astype(F32), lo.astype(F32)
    top = jnp.concatenate([hi, hi], axis=1)
    low = jnp.concatenate([lo, jnp.zeros_like(lo)], axis=1)
    return jnp.concatenate([top, low], axis=0).astype(BF16)


def dot_nt(a, b):
    return lax.dot_general(a, b, (((1,), (1,)), ((), ())), preferred_element_type=F32)


def times(a, b):
    ah, al = halves(a)
    bh, bl = halves(b)
    left = jnp.concatenate([ah, al, ah], axis=1)
    right = jnp.concatenate([bh, bh, bl], axis=0)
    return jnp.dot(left, right, preferred_element_type=F32)


def mapped(matrix_split, vectors):
    count = vectors.shape[0]
    both = dot_nt(split_rows(vectors), matrix_split)
    return both[:count] + both[count:]


def mapped_each(matrices, vectors):
    rows = []
    for r in range(vectors.shape[0]):
        products = matrices[r] * vectors[r : r + 1, :]
        rows.append(jnp.sum(products.T, axis=0, keepdims=True))
    return jnp.concatenate(rows, axis=0)


def call(kernel, outs, *args, cost=None, source=pltpu.VMEM, scratch=()):
    vmem = pl.BlockSpec(memory_space=pltpu.VMEM)
    return pl.pallas_call(
        kernel,
        out_shape=[jax.ShapeDtypeStruct(s, d) for s, d in outs],
        in_specs=[pl.BlockSpec(memory_space=source)] * len(args),
        out_specs=[vmem] * len(outs),
        scratch_shapes=list(scratch),
        cost_estimate=cost,
        compiler_params=pltpu.CompilerParams(vmem_limit_bytes=24 * 2**20),
    )(*args)


def identity(width):
    return (
        lax.broadcasted_iota(jnp.int32, (width, width), 0)
        == lax.broadcasted_iota(jnp.int32, (width, width), 1)
    ).astype(F32)


def halo_kernel(s_ref, near_ref, msg_ref):
    points, width = s_ref.shape
    msg_ref[:4] = jnp.broadcast_to(near_ref[points - 1 :], (4, width))
    msg_ref[4:] = jnp.broadcast_to(s_ref[points - 1 :], (4, width))


def ones_kernel(one_ref):
    one_ref[...] = jnp.ones(one_ref.shape, F32)


def pack_kernel(one_ref, g_ref, mask_ref, k_ref, j_ref, inj_ref, cap_ref, gain_ref, bnd_ref, pack_ref):
    points, width = inj_ref.shape
    pack_ref[:width] = g_ref[...] * (mask_ref[...] * one_ref[...])
    pack_ref[width : 2 * width] = k_ref[...]
    pack_ref[2 * width : 3 * width] = j_ref[...]
    at = 3 * width
    pack_ref[at : at + points] = inj_ref[...]
    at += points
    for one in (cap_ref[...], gain_ref[...], bnd_ref[...].astype(F32)):
        pack_ref[at : at + 8] = jnp.broadcast_to(one, (8, width))
        at += 8


def vectors(small_ref, g, points):
    at = g * (points + 24)
    inj = small_ref[at : at + points]
    at += points
    cap, gain, bnd = (small_ref[at + 8 * i : at + 8 * i + 1] for i in range(3))
    return inj, cap, gain, bnd.astype(jnp.int32)


def whole_kernel(lo_ref, hi_ref, w_ref, r_lo, r_hi, sems):
    points, width = lo_ref.shape[0], lo_ref.shape[1]
    moves = [
        pltpu.make_async_copy(source, target, sems.at[g])
        for g, (source, target) in enumerate(((lo_ref, r_lo), (hi_ref, r_hi)))
    ]
    for move in moves:
        move.start()
    u = []
    for g, r_ref in enumerate((r_lo, r_hi)):
        moves[g].wait()
        u += [times(r_ref[i + 1], r_ref[i]) for i in range(0, points, 2)]
    while len(u) > PAIR:
        u = [times(u[i + 1], u[i]) for i in range(0, len(u), 2)]
    for g in range(PAIR):
        w_ref[g * width : (g + 1) * width] = u[g]


def suffix_kernel(r_lo, r_hi, _, s_ref):
    points, width = r_lo.shape[0], r_lo.shape[1]
    for g, r_ref in enumerate((r_lo, r_hi)):
        u = [r_ref[i] for i in range(points)]
        span = 1
        while span < points:
            for base in range(0, points, 2 * span):
                prod = times(u[base + span], jnp.concatenate(u[base : base + span], axis=1))
                for i in range(span):
                    u[base + i] = prod[:, i * width : (i + 1) * width]
            span *= 2
        for i in range(points - 1):
            s_ref[g * points + i] = u[i + 1]
        s_ref[(g + 1) * points - 1] = identity(width)


def prefix_kernel(r_ref, p_ref, l_ref):
    points, width = r_ref.shape[0], r_ref.shape[1]
    q = [r_ref[i] for i in range(points)]
    span, slot = 1, 0
    while span < points:
        for base in range(0, points, 2 * span):
            upper = q[base + span : base + 2 * span]
            for matrix in upper:
                l_ref[slot] = matrix
                slot += 1
            prod = times(jnp.concatenate(upper, axis=0), q[base + span - 1])
            for i in range(span):
                q[base + span + i] = prod[i * width : (i + 1) * width]
        span *= 2
    for i in range(points):
        p_ref[i] = q[i]


def scanned(c, l_ref):
    points = c.shape[0]
    x = [c[i : i + 1, :] for i in range(points)]
    span, slot = 1, 0
    while span < points:
        for base in range(0, points, 2 * span):
            head = x[base + span - 1]
            for i in range(base + span, base + 2 * span):
                x[i] = x[i] + mapped_each(l_ref[slot : slot + 1], head)
                slot += 1
        span *= 2
    return jnp.concatenate(x, axis=0)


def taken(rows, lanes):
    return jnp.take_along_axis(rows, jnp.broadcast_to(lanes, rows.shape), axis=1)


def negative_residual(s, halo, inj, cap, gain, gs):
    before = jnp.concatenate([halo, s[: s.shape[0] - 1]], axis=0)
    return inj - cap * (s - before) - mapped(gs, s) - gain * jnp.tanh(s)


def corrected(nr, c_before, s_before, d_ref, js, ks):
    return mapped_each(d_ref, nr + mapped(js, c_before) + mapped(ks, s_before))


def pair_corrected(nr, s_lo, c_lo, bnd_lo, d_hi_ref, js, ks):
    return corrected(nr, taken(c_lo, bnd_lo), taken(s_lo, bnd_lo), d_hi_ref, js, ks)


def correct_both(
    s_lo, s_hi, halo_lo, halo_hi, small_ref, maps_ref, d_lo, d_hi, nr_ref, c_ref, msg_ref
):
    lo_maps, hi_maps = [maps_ref[i] for i in range(3)], [maps_ref[i] for i in range(3, 6)]
    points = s_lo.shape[0]
    inj_lo, cap_lo, gain_lo, bnd_lo = vectors(small_ref, 0, points)
    inj_hi, cap_hi, gain_hi, bnd_hi = vectors(small_ref, 1, points)
    nr_lo = negative_residual(s_lo, halo_lo, inj_lo, cap_lo, gain_lo, lo_maps[0])
    nr_hi = negative_residual(s_hi, halo_hi, inj_hi, cap_hi, gain_hi, hi_maps[0])
    c_lo = mapped_each(d_lo, nr_lo)
    c_hi = pair_corrected(nr_hi, s_lo, c_lo, bnd_lo, d_hi, hi_maps[2], hi_maps[1])
    nr_ref[:points], nr_ref[points:] = nr_lo, nr_hi
    c_ref[:points], c_ref[points:] = c_lo, c_hi
    msg_ref[:points] = taken(c_hi, bnd_hi)
    msg_ref[points:] = taken(s_hi, bnd_hi)


def early_kernel(
    s_lo, s_hi, pack_lo, pack_hi, d_lo, d_hi, maps_ref, small_ref, nr_ref, c_ref, msg_ref
):
    points, width = s_lo.shape
    for i in range(3):
        rows = slice(i * width, (i + 1) * width)
        maps_ref[i] = split_cols(pack_lo[rows])
        maps_ref[3 + i] = split_cols(pack_hi[rows])
    small_ref[: points + 24] = pack_lo[3 * width :]
    small_ref[points + 24 :] = pack_hi[3 * width :]
    none = jnp.zeros((1, width), F32)
    correct_both(
        s_lo[...], s_hi[...], none, none, small_ref, maps_ref, d_lo, d_hi, nr_ref, c_ref, msg_ref
    )


def first_kernel(
    halo_ref, s_lo, s_hi, small_ref, maps_ref, d_lo, d_hi, old_nr, old_c, old_msg,
    s_ref, nr_ref, c_ref, msg_ref,
):
    points = s_lo.shape[0]
    _, cap_lo, _, bnd_lo = vectors(small_ref, 0, points)
    _, cap_hi, _, bnd_hi = vectors(small_ref, 1, points)
    s_ref[:points], s_ref[points:] = s_lo[...], s_hi[...]
    nr_ref[...], c_ref[...], msg_ref[...] = old_nr[...], old_c[...], old_msg[...]
    nr_lo = old_nr[:1] + cap_lo * halo_ref[:1]
    nr_hi = old_nr[points : points + 1] + cap_hi * halo_ref[4:5]
    c_lo = mapped_each(d_lo, nr_lo)
    came = mapped(maps_ref[5], taken(jnp.broadcast_to(c_lo, (8, c_lo.shape[1])), bnd_lo))
    came = came + mapped(maps_ref[4], taken(s_lo[:8], bnd_lo))
    c_hi = mapped_each(d_hi, nr_hi + came[:1])
    nr_ref[:1], nr_ref[points : points + 1] = nr_lo, nr_hi
    c_ref[:1], c_ref[points : points + 1] = c_lo, c_hi
    msg_ref[:1] = taken(jnp.broadcast_to(c_hi, (8, c_hi.shape[1])), bnd_hi)[:1]


def second_kernel(
    got_ref, s_ref, nr_ref, c_ref, small_ref, maps_ref, d_lo, d_hi, ss_ref, new_c_ref, tail_ref, f_ref
):
    points, width = got_ref.shape[0] // 2, got_ref.shape[1]
    second_pair = lax.axis_index("dom") >= PAIR

    @pl.when(second_pair)
    def _():
        bnd_lo = vectors(small_ref, 0, points)[3]
        c_lo = corrected(
            nr_ref[:points], got_ref[:points], got_ref[points:], d_lo, maps_ref[2], maps_ref[1]
        )
        new_c_ref[:points] = c_lo
        new_c_ref[points:] = pair_corrected(
            nr_ref[points:], s_ref[:points], c_lo, bnd_lo, d_hi, maps_ref[5], maps_ref[4]
        )

    @pl.when(jnp.logical_not(second_pair))
    def _():
        new_c_ref[...] = c_ref[...]

    each = mapped_each(ss_ref, new_c_ref[...])
    for g in range(PAIR):
        total = each[g * points : (g + 1) * points]
        shift = 1
        while shift < points:
            total = total + jnp.concatenate(
                [total[shift:], jnp.zeros((shift, width), F32)], axis=0
            )
            shift *= 2
        at = g * (points + 8)
        tail_ref[at : at + points] = jnp.concatenate(
            [total[1:], jnp.zeros((1, width), F32)], axis=0
        )
        whole = jnp.broadcast_to(total[:1], (8, width))
        tail_ref[at + points : at + points + 8] = whole
        f_ref[8 * g : 8 * g + 8] = whole


def is_later(distance):
    return (lax.axis_index("tm") // distance) % 2 == 1


def sections(width):
    return [
        (slice(g * width, (g + 1) * width), slice(8 * g, 8 * g + 8)) for g in range(PAIR)
    ]


def first_maps_kernel(distance, mw_ref, gw_ref, _, tw_ref, a_ref, bw_ref, aw_ref):
    width = mw_ref.shape[1]
    later = is_later(distance)
    eye = identity(width)
    for wide, _ in sections(width):
        mw, gw = mw_ref[wide], gw_ref[wide]
        a = jnp.where(later, mw, gw)
        tw_ref[wide] = times(a, jnp.where(later, gw, mw))
        a_ref[wide] = split_cols(a)
        bw_ref[wide] = jnp.where(later, gw, eye)
        aw_ref[wide] = jnp.where(later, eye, gw)


def next_maps_kernel(
    distance, mw_ref, gw_ref, bw_ref, aw_ref, _, tw_ref, a_ref, x_ref, nbw_ref, naw_ref
):
    width = mw_ref.shape[1]
    later = is_later(distance)
    for wide, _ in sections(width):
        mw, gw, bw, aw = mw_ref[wide], gw_ref[wide], bw_ref[wide], aw_ref[wide]
        a = jnp.where(later, mw, gw)
        tw_ref[wide] = times(a, jnp.where(later, gw, mw))
        a_ref[wide] = split_cols(a)
        x = jnp.where(later, bw, gw)
        joined = times(x, jnp.where(later, gw, aw))
        x_ref[wide] = split_cols(x)
        nbw_ref[wide] = jnp.where(later, joined, bw)
        naw_ref[wide] = jnp.where(later, aw, joined)


def first_sums_kernel(distance, mf_ref, gf_ref, a_ref, _, tf_ref, bf_ref, af_ref):
    later = is_later(distance)
    for wide, short in sections(a_ref.shape[0] // PAIR):
        mf, gf = mf_ref[short], gf_ref[short]
        tf_ref[short] = mapped(a_ref[wide], jnp.where(later, gf, mf)) + jnp.where(later, mf, gf)
        bf_ref[short] = jnp.where(later, gf, 0.0)
        af_ref[short] = jnp.where(later, 0.0, gf)


def next_sums_kernel(
    distance, mf_ref, gf_ref, bf_ref, af_ref, a_ref, x_ref, _, tf_ref, nbf_ref, naf_ref
):
    later = is_later(distance)
    for wide, short in sections(a_ref.shape[0] // PAIR):
        mf, gf, bf, af = mf_ref[short], gf_ref[short], bf_ref[short], af_ref[short]
        tf_ref[short] = mapped(a_ref[wide], jnp.where(later, gf, mf)) + jnp.where(later, mf, gf)
        sums = mapped(x_ref[wide], jnp.where(later, gf, af)) + jnp.where(later, bf, gf)
        nbf_ref[short] = jnp.where(later, sums, bf)
        naf_ref[short] = jnp.where(later, af, sums)


def local_kernel(c_ref, l_lo, l_hi, tail_ref, aw_ref, af_ref, s_ref, base_ref, v_ref):
    points, width = s_ref.shape[0] // PAIR, s_ref.shape[1]
    for g, (wide, short) in enumerate(sections(width)):
        rows = slice(g * points, (g + 1) * points)
        long = slice(g * (points + 8), (g + 1) * (points + 8))
        base_ref[rows] = s_ref[rows] + scanned(c_ref[rows], (l_lo, l_hi)[g])
        v_ref[long] = mapped(split_cols(aw_ref[wide]), tail_ref[long]) + af_ref[short][:1]


def turn_kernel(
    v_ref, gw_ref, gf_ref, bw_ref, bf_ref, p_lo, p_hi, base_ref, halo_ref, small_ref, maps_ref,
    d_lo, d_hi, s_ref, nr_ref, c_ref, msg_ref,
):
    points, width = s_ref.shape[0] // PAIR, s_ref.shape[1]
    came = []
    for g, (wide, short) in enumerate(sections(width)):
        long = slice(g * (points + 8), (g + 1) * (points + 8))
        v = mapped(split_cols(gw_ref[wide]), v_ref[long]) + gf_ref[short][:1]
        came.append(mapped(split_cols(bw_ref[wide]), v) + bf_ref[short][:1])
    moved = [mapped_each(p, v[:points]) for p, v in zip((p_lo, p_hi), came)]
    s = base_ref[...] + jnp.concatenate(moved, axis=0)
    s_ref[...] = s
    correct_both(
        s[:points], s[points:],
        halo_ref[:1] + came[0][points : points + 1],
        halo_ref[4:5] + came[1][points : points + 1],
        small_ref, maps_ref, d_lo, d_hi, nr_ref, c_ref, msg_ref,
    )


def last_local_kernel(
    c_ref, l_lo, l_hi, tail_ref, aw_ref, af_ref, gw_ref, bw_ref, bf_ref, p_lo, p_hi, s_ref, base_ref
):
    points, width = s_ref.shape[0] // PAIR, s_ref.shape[1]
    came = []
    for g, (wide, short) in enumerate(sections(width)):
        at = g * (points + 8)
        v = mapped(split_cols(aw_ref[wide]), tail_ref[at : at + points]) + af_ref[short][:1]
        v = mapped(split_cols(gw_ref[wide]), v)
        came.append(mapped(split_cols(bw_ref[wide]), v) + bf_ref[short][:1])
    for g in range(PAIR):
        rows = slice(g * points, (g + 1) * points)
        moved = mapped_each((p_lo, p_hi)[g], came[g])
        base_ref[rows] = s_ref[rows] + moved + scanned(c_ref[rows], (l_lo, l_hi)[g])


def end_kernel(gf_ref, bw_ref, p_lo, p_hi, base_ref, s_ref):
    points, width = s_ref.shape[0] // PAIR, s_ref.shape[1]
    for g, (wide, short) in enumerate(sections(width)):
        rows = slice(g * points, (g + 1) * points)
        v = mapped(split_cols(bw_ref[wide]), gf_ref[short])[:1]
        moved = mapped_each((p_lo, p_hi)[g], jnp.broadcast_to(v, (points, width)))
        s_ref[rows] = base_ref[rows] + moved


def choose_kernel(both_ref, got_ref, s_ref):
    points = s_ref.shape[0]
    odd = lax.axis_index("dom") % 2 == 1
    s_ref[...] = jnp.where(odd, both_ref[points:], got_ref[:points])


def exchanged(value, distance):
    return lax.ppermute(
        value, "tm", [(i, i ^ distance) for i in range(lax.axis_size("tm"))]
    )


def swapped(value, distance):
    return lax.ppermute(value, "dom", [(i, i ^ distance) for i in range(lax.axis_size("dom"))])


def both_partitions(
    s, nr, c, msg, halo, small, maps, d_lo, d_hi, r_lo, r_hi
):
    points, width = s.shape[0] // PAIR, s.shape[1]
    vec, square = ((PAIR * points, width), F32), ((PAIR * width, width), F32)
    square_split = ((PAIR * width, 2 * width), BF16)
    eight = ((PAIR * 8, width), F32)
    longer = ((PAIR * (points + 8), width), F32)
    many = ((PAIR * points, width, width), F32)
    steps = (points.bit_length() - 1) * points // 2
    distances = [2**k for k in range(lax.axis_size("tm").bit_length() - 1)]

    def sums_level(level, f, bf, af, beside):
        got = exchanged(f, distances[level])
        if level == 0:
            return call(
                functools.partial(first_sums_kernel, distances[0]), [eight] * 3,
                f, got, *kept[0], beside,
            )
        return call(
            functools.partial(next_sums_kernel, distances[level]), [eight] * 3,
            f, got, bf, af, *kept[level], beside,
            cost=pl.CostEstimate(flops=2**33, bytes_accessed=2**25, transcendentals=0),
        )

    got = swapped(msg, 2)
    w, r_lo, r_hi = call(
        whole_kernel, [square] + [((points, width, width), F32)] * 2, r_lo, r_hi,
        source=pltpu.HBM, scratch=[pltpu.SemaphoreType.DMA((2,))],
    )
    got_w = exchanged(w, distances[0])
    (ss,) = call(
        suffix_kernel, [many], r_lo, r_hi, got,
        cost=pl.CostEstimate(flops=2**33, bytes_accessed=2**25, transcendentals=0),
    )
    p_shapes = [((points, width, width), F32), ((steps, width, width), F32)]
    p_lo, l_lo = call(prefix_kernel, p_shapes, r_lo)
    p_hi, l_hi = call(prefix_kernel, p_shapes, r_hi)
    beside = [p_lo] + [ss] * (len(distances) - 2)
    c, tail, f = call(
        second_kernel, [vec, longer, eight], got, s, nr, c, small, maps, d_lo, d_hi, ss
    )
    kept, bf, af = [], None, None
    for level, distance in enumerate(distances[:-1]):
        if level == 0:
            w, a, bw, aw = call(
                functools.partial(first_maps_kernel, distance),
                [square, square_split, square, square], w, got_w, f,
            )
            kept.append((a,))
        else:
            w, a, x, bw, aw = call(
                functools.partial(next_maps_kernel, distance),
                [square, square_split, square_split, square, square], w, got_w, bw, aw, f,
            )
            kept.append((a, x))
        got_w = exchanged(w, distances[level + 1])
        f, bf, af = sums_level(level, f, bf, af, beside[level])
    got, last = exchanged(f, distances[-1]), got_w
    base, v = call(local_kernel, [vec, longer], c, l_lo, l_hi, tail, aw, af, s)
    s, nr, c, msg = call(
        turn_kernel, [vec] * 4,
        v, last, got, bw, bf, p_lo, p_hi, base, halo, small, maps, d_lo, d_hi,
    )
    got = swapped(msg, 2)
    c, tail, f = call(
        second_kernel, [vec, longer, eight], got, s, nr, c, small, maps, d_lo, d_hi, ss
    )
    for level in range(len(distances) - 1):
        f, bf, af = sums_level(level, f, bf, af, beside[level])
    got = exchanged(f, distances[-1])
    (base,) = call(last_local_kernel, [vec], c, l_lo, l_hi, tail, aw, af, last, bw, bf, p_lo, p_hi, s)
    return call(end_kernel, [vec], got, bw, p_lo, p_hi, base)[0]


def per_device(
    starting_voltage_guess,
    injected_amperes,
    capacitance,
    conductance,
    block_pattern,
    device_gain,
    link_weight,
    boundary_vertex_list,
    diagonal_reciprocals,
    boundary_jacobian,
    transfer,
):
    points, _, width = starting_voltage_guess.shape
    segments = lax.axis_size("tm")
    (one,) = call(
        ones_kernel, [((1, width), F32)],
        cost=pl.CostEstimate(flops=2**33, bytes_accessed=2**25, transcendentals=0),
    )
    mask = jnp.broadcast_to(block_pattern[0].astype(F32), (1, width))
    s = starting_voltage_guess[:, 0]
    near_s = swapped(starting_voltage_guess, 1)[:, 0]
    d, r, near_s, mask, one = lax.optimization_barrier(
        (diagonal_reciprocals, transfer, near_s, mask, one)
    )
    d, near_d = d[:, 0, 0], swapped(d, 1)[:, 0, 0]
    r, near_r = r[:, 0, 0], swapped(r, 1)[:, 0, 0]
    (rows,) = call(halo_kernel, [((8, width), F32)], s, near_s)
    halo = lax.ppermute(rows, "tm", [(i, (i + 1) % segments) for i in range(segments)])
    (pack,) = call(
        pack_kernel, [((3 * width + points + 24, width), F32)],
        one, conductance[0], mask, link_weight[0], boundary_jacobian[0],
        injected_amperes[:, 0], capacitance, device_gain, boundary_vertex_list,
    )
    near_pack = swapped(pack, 1)
    vec = ((PAIR * points, width), F32)
    maps, small, nr, c, msg = call(
        early_kernel,
        [((6, width, 2 * width), BF16), ((PAIR * (points + 24), width), F32), vec, vec, vec],
        near_s, s, near_pack, pack, near_d, d,
    )
    s, nr, c, msg = call(
        first_kernel, [vec] * 4,
        halo, near_s, s, small, maps, near_d, d, nr, c, msg,
    )
    odd = lax.axis_index("dom") % 2 == 1
    both = lax.cond(
        odd,
        both_partitions,
        lambda s, *rest: s,
        s, nr, c, msg, halo, small, maps, near_d, d, near_r, r,
    )
    (s,) = call(choose_kernel, [((points, width), F32)], both, swapped(both, 1))
    return s[:, None]


def solution(mesh):
    in_specs = (
        P("tm", "dom", None),
        P("tm", "dom", None),
        P("dom", None),
        P("dom", None, None),
        P("dom", None, None),
        P("dom", None),
        P("dom", None, None),
        P("dom", None),
        P("tm", "dom", None, None, None),
        P("dom", None, None),
        P("tm", "dom", None, None, None),
    )
    out_specs = P("tm", "dom", None)
    return jax.shard_map(
        per_device, mesh=mesh, in_specs=in_specs, out_specs=out_specs, check_vma=False
    )
```

```python
import functools

import jax
import jax.numpy as jnp
from jax import lax
from jax.experimental import pallas as pl
from jax.experimental.pallas import tpu as pltpu
from jax.sharding import PartitionSpec as P

F32 = jnp.float32
BF16 = jnp.bfloat16
PAIR = 2


def halves(x):
    hi = x.astype(BF16)
    return hi, (x - hi.astype(F32)).astype(BF16)


def split_cols(matrix):
    return jnp.concatenate(halves(matrix), axis=1)


def split_rows(vectors):
    hi, lo = halves(vectors)
    hi, lo = hi.astype(F32), lo.astype(F32)
    top = jnp.concatenate([hi, hi], axis=1)
    low = jnp.concatenate([lo, jnp.zeros_like(lo)], axis=1)
    return jnp.concatenate([top, low], axis=0).astype(BF16)


def dot_nt(a, b):
    return lax.dot_general(a, b, (((1,), (1,)), ((), ())), preferred_element_type=F32)


def times(a, b):
    ah, al = halves(a)
    bh, bl = halves(b)
    left = jnp.concatenate([ah, al, ah], axis=1)
    right = jnp.concatenate([bh, bh, bl], axis=0)
    return jnp.dot(left, right, preferred_element_type=F32)


def mapped(matrix_split, vectors):
    count = vectors.shape[0]
    both = dot_nt(split_rows(vectors), matrix_split)
    return both[:count] + both[count:]


def mapped_each(matrices, vectors):
    rows = []
    for r in range(vectors.shape[0]):
        products = matrices[r] * vectors[r : r + 1, :]
        rows.append(jnp.sum(products.T, axis=0, keepdims=True))
    return jnp.concatenate(rows, axis=0)


def mapped_each_split(matrices_split, vectors):
    count, width = vectors.shape
    both = dot_nt(split_rows(vectors), matrices_split)
    row = lax.broadcasted_iota(jnp.int32, (2 * count, width), 0) % count
    picked = [
        jnp.where(row == r, both[:, r * width : (r + 1) * width], 0.0) for r in range(count)
    ]
    while len(picked) > 1:
        picked = [a + b for a, b in zip(picked[::2], picked[1::2])]
    return picked[0][:count] + picked[0][count:]


def mapped_sum(matrices, vectors):
    products = matrices[0] * vectors[:1, :]
    for r in range(1, vectors.shape[0]):
        products = products + matrices[r] * vectors[r : r + 1, :]
    return jnp.sum(products.T, axis=0, keepdims=True)


def call(kernel, outs, *args, cost=None, in_hbm=0, scratch=()):
    vmem = pl.BlockSpec(memory_space=pltpu.VMEM)
    return pl.pallas_call(
        kernel,
        out_shape=[jax.ShapeDtypeStruct(s, d) for s, d in outs],
        in_specs=[vmem] * (len(args) - in_hbm) + [pl.BlockSpec(memory_space=pltpu.HBM)] * in_hbm,
        out_specs=[vmem] * len(outs),
        scratch_shapes=list(scratch),
        cost_estimate=cost,
        compiler_params=pltpu.CompilerParams(vmem_limit_bytes=24 * 2**20),
    )(*args)


def identity(width):
    return (
        lax.broadcasted_iota(jnp.int32, (width, width), 0)
        == lax.broadcasted_iota(jnp.int32, (width, width), 1)
    ).astype(F32)


def halo_kernel(s_ref, near_ref, msg_ref):
    points, width = s_ref.shape
    msg_ref[:4] = jnp.broadcast_to(near_ref[points - 1 :], (4, width))
    msg_ref[4:] = jnp.broadcast_to(s_ref[points - 1 :], (4, width))


def ones_kernel(one_ref):
    one_ref[...] = jnp.ones(one_ref.shape, F32)


def pack_kernel(one_ref, g_ref, mask_ref, k_ref, j_ref, inj_ref, cap_ref, gain_ref, bnd_ref, pack_ref):
    points, width = inj_ref.shape
    pack_ref[:width] = g_ref[...] * (mask_ref[...] * one_ref[...])
    pack_ref[width : 2 * width] = k_ref[...]
    pack_ref[2 * width : 3 * width] = j_ref[...]
    at = 3 * width
    pack_ref[at : at + points] = inj_ref[...]
    at += points
    for one in (cap_ref[...], gain_ref[...], bnd_ref[...].astype(F32)):
        pack_ref[at : at + 8] = jnp.broadcast_to(one, (8, width))
        at += 8


def vectors(small_ref, g, points):
    at = g * (points + 24)
    inj = small_ref[at : at + points]
    at += points
    cap, gain, bnd = (small_ref[at + 8 * i : at + 8 * i + 1] for i in range(3))
    return inj, cap, gain, bnd.astype(jnp.int32)


def fetched(sources, targets, sems):
    moves = [
        pltpu.make_async_copy(source, target, sems.at[i])
        for i, (source, target) in enumerate(zip(sources, targets))
    ]
    for move in moves:
        move.start()
    return moves


def whole_kernel(lo_ref, hi_ref, w_ref, r_lo, r_hi, sems):
    points, width = lo_ref.shape[0], lo_ref.shape[1]
    moves = fetched((lo_ref, hi_ref), (r_lo, r_hi), sems)
    u = []
    for move, r_ref in zip(moves, (r_lo, r_hi)):
        move.wait()
        u += [times(r_ref[i + 1], r_ref[i]) for i in range(0, points, 2)]
    while len(u) > PAIR:
        u = [times(u[i + 1], u[i]) for i in range(0, len(u), 2)]
    for g in range(PAIR):
        w_ref[g * width : (g + 1) * width] = u[g]


def suffix_kernel(lo_ref, hi_ref, s_ref, r_lo, r_hi, sems):
    points, width = lo_ref.shape[0], lo_ref.shape[1]
    moves = fetched((lo_ref, hi_ref), (r_lo, r_hi), sems)
    for g, r_ref in enumerate((r_lo, r_hi)):
        moves[g].wait()
        u = [r_ref[i] for i in range(points)]
        span = 1
        while span < points:
            for base in range(0, points, 2 * span):
                prod = times(u[base + span], jnp.concatenate(u[base : base + span], axis=1))
                for i in range(span):
                    u[base + i] = prod[:, i * width : (i + 1) * width]
            span *= 2
        for i in range(points - 1):
            s_ref[g * points + i] = u[i + 1]
        s_ref[(g + 1) * points - 1] = identity(width)


def prefix_kernel(split, r_ref, p_ref, l_ref):
    points, width = r_ref.shape[0], r_ref.shape[1]
    q = [r_ref[i] for i in range(points)]
    span, slot = 1, 0
    while span < points:
        for base in range(0, points, 2 * span):
            upper = q[base + span : base + 2 * span]
            for matrix in upper:
                l_ref[slot] = matrix
                slot += 1
            prod = times(jnp.concatenate(upper, axis=0), q[base + span - 1])
            for i in range(span):
                q[base + span + i] = prod[i * width : (i + 1) * width]
        span *= 2
    for i in range(points):
        if split:
            p_ref[i * width : (i + 1) * width] = split_cols(q[i])
        else:
            p_ref[i] = q[i]


def scanned(c, l_ref):
    points = c.shape[0]
    x = [c[i : i + 1, :] for i in range(points)]
    span, slot = 1, 0
    while span < points:
        for base in range(0, points, 2 * span):
            head = x[base + span - 1]
            for i in range(base + span, base + 2 * span):
                x[i] = x[i] + mapped_each(l_ref[slot : slot + 1], head)
                slot += 1
        span *= 2
    return jnp.concatenate(x, axis=0)


def taken(rows, lanes):
    return jnp.take_along_axis(rows, jnp.broadcast_to(lanes, rows.shape), axis=1)


def negative_residual(s, halo, inj, cap, gain, gs):
    before = jnp.concatenate([halo, s[: s.shape[0] - 1]], axis=0)
    return inj - cap * (s - before) - mapped(gs, s) - gain * jnp.tanh(s)


def corrected(nr, c_before, s_before, d_ref, js, ks):
    return mapped_each(d_ref, nr + mapped(js, c_before) + mapped(ks, s_before))


def pair_corrected(nr, s_lo, c_lo, bnd_lo, d_hi_ref, js, ks):
    return corrected(nr, taken(c_lo, bnd_lo), taken(s_lo, bnd_lo), d_hi_ref, js, ks)


def correct_both(
    s_lo, s_hi, halo_lo, halo_hi, small_ref, maps_ref, d_lo, d_hi, nr_ref, c_ref, msg_ref
):
    lo_maps, hi_maps = [maps_ref[i] for i in range(3)], [maps_ref[i] for i in range(3, 6)]
    points = s_lo.shape[0]
    inj_lo, cap_lo, gain_lo, bnd_lo = vectors(small_ref, 0, points)
    inj_hi, cap_hi, gain_hi, bnd_hi = vectors(small_ref, 1, points)
    nr_lo = negative_residual(s_lo, halo_lo, inj_lo, cap_lo, gain_lo, lo_maps[0])
    nr_hi = negative_residual(s_hi, halo_hi, inj_hi, cap_hi, gain_hi, hi_maps[0])
    c_lo = mapped_each(d_lo, nr_lo)
    c_hi = pair_corrected(nr_hi, s_lo, c_lo, bnd_lo, d_hi, hi_maps[2], hi_maps[1])
    nr_ref[:points], nr_ref[points:] = nr_lo, nr_hi
    c_ref[:points], c_ref[points:] = c_lo, c_hi
    msg_ref[:points] = taken(c_hi, bnd_hi)
    msg_ref[points:] = taken(s_hi, bnd_hi)


def early_kernel(
    s_lo, s_hi, pack_lo, pack_hi, d_lo, d_hi, _, maps_ref, small_ref, nr_ref, c_ref, msg_ref
):
    points, width = s_lo.shape
    for i in range(3):
        rows = slice(i * width, (i + 1) * width)
        maps_ref[i] = split_cols(pack_lo[rows])
        maps_ref[3 + i] = split_cols(pack_hi[rows])
    small_ref[: points + 24] = pack_lo[3 * width :]
    small_ref[points + 24 :] = pack_hi[3 * width :]
    none = jnp.zeros((1, width), F32)
    correct_both(
        s_lo[...], s_hi[...], none, none, small_ref, maps_ref, d_lo, d_hi, nr_ref, c_ref, msg_ref
    )


def first_kernel(
    halo_ref, s_lo, s_hi, small_ref, maps_ref, d_lo, d_hi, old_nr, old_c, old_msg,
    s_ref, nr_ref, c_ref, msg_ref,
):
    points = s_lo.shape[0]
    _, cap_lo, _, bnd_lo = vectors(small_ref, 0, points)
    _, cap_hi, _, bnd_hi = vectors(small_ref, 1, points)
    s_ref[:points], s_ref[points:] = s_lo[...], s_hi[...]
    nr_ref[...], c_ref[...], msg_ref[...] = old_nr[...], old_c[...], old_msg[...]
    nr_lo = old_nr[:1] + cap_lo * halo_ref[:1]
    nr_hi = old_nr[points : points + 1] + cap_hi * halo_ref[4:5]
    c_lo = mapped_each(d_lo, nr_lo)
    came = mapped(maps_ref[5], taken(jnp.broadcast_to(c_lo, (8, c_lo.shape[1])), bnd_lo))
    came = came + mapped(maps_ref[4], taken(s_lo[:8], bnd_lo))
    c_hi = mapped_each(d_hi, nr_hi + came[:1])
    nr_ref[:1], nr_ref[points : points + 1] = nr_lo, nr_hi
    c_ref[:1], c_ref[points : points + 1] = c_lo, c_hi
    msg_ref[:1] = taken(jnp.broadcast_to(c_hi, (8, c_hi.shape[1])), bnd_hi)[:1]


def second_kernel(
    got_ref, s_ref, nr_ref, c_ref, small_ref, maps_ref, d_lo, d_hi, ss_ref, new_c_ref, f_ref
):
    points, width = got_ref.shape[0] // 2, got_ref.shape[1]
    second_pair = lax.axis_index("dom") >= PAIR

    @pl.when(second_pair)
    def _():
        bnd_lo = vectors(small_ref, 0, points)[3]
        c_lo = corrected(
            nr_ref[:points], got_ref[:points], got_ref[points:], d_lo, maps_ref[2], maps_ref[1]
        )
        new_c_ref[:points] = c_lo
        c_hi = pair_corrected(
            nr_ref[points:], s_ref[:points], c_lo, bnd_lo, d_hi, maps_ref[5], maps_ref[4]
        )
        new_c_ref[points:] = c_hi
        for g, c in enumerate((c_lo, c_hi)):
            whole = mapped_sum(ss_ref[g * points : (g + 1) * points], c)
            f_ref[8 * g : 8 * g + 8] = jnp.broadcast_to(whole, (8, width))

    @pl.when(jnp.logical_not(second_pair))
    def _():
        new_c_ref[...] = c_ref[...]
        for g in range(PAIR):
            rows = slice(g * points, (g + 1) * points)
            whole = mapped_sum(ss_ref[rows], c_ref[rows])
            f_ref[8 * g : 8 * g + 8] = jnp.broadcast_to(whole, (8, width))


def tail_kernel(c_ref, ss_ref, tail_ref):
    points, width = c_ref.shape[0] // PAIR, c_ref.shape[1]
    each = mapped_each(ss_ref, c_ref[...])
    for g in range(PAIR):
        total = each[g * points : (g + 1) * points]
        shift = 1
        while shift < points:
            total = total + jnp.concatenate(
                [total[shift:], jnp.zeros((shift, width), F32)], axis=0
            )
            shift *= 2
        at = g * (points + 8)
        tail_ref[at : at + points] = jnp.concatenate(
            [total[1:], jnp.zeros((1, width), F32)], axis=0
        )
        tail_ref[at + points : at + points + 8] = jnp.broadcast_to(total[:1], (8, width))


def is_later(distance):
    return (lax.axis_index("tm") // distance) % 2 == 1


def sections(width):
    return [
        (slice(g * width, (g + 1) * width), slice(8 * g, 8 * g + 8)) for g in range(PAIR)
    ]


def first_maps_kernel(distance, mw_ref, gw_ref, _, tw_ref, a_ref, bw_ref, aw_ref):
    width = mw_ref.shape[1]
    later = is_later(distance)
    eye = identity(width)
    for wide, _ in sections(width):
        mw, gw = mw_ref[wide], gw_ref[wide]
        a = jnp.where(later, mw, gw)
        tw_ref[wide] = times(a, jnp.where(later, gw, mw))
        a_ref[wide] = split_cols(a)
        bw_ref[wide] = jnp.where(later, gw, eye)
        aw_ref[wide] = jnp.where(later, eye, gw)


def next_maps_kernel(
    distance, mw_ref, gw_ref, bw_ref, aw_ref, _, tw_ref, a_ref, x_ref, nbw_ref, naw_ref
):
    width = mw_ref.shape[1]
    later = is_later(distance)
    for wide, _ in sections(width):
        mw, gw, bw, aw = mw_ref[wide], gw_ref[wide], bw_ref[wide], aw_ref[wide]
        a = jnp.where(later, mw, gw)
        tw_ref[wide] = times(a, jnp.where(later, gw, mw))
        a_ref[wide] = split_cols(a)
        x = jnp.where(later, bw, gw)
        joined = times(x, jnp.where(later, gw, aw))
        x_ref[wide] = split_cols(x)
        nbw_ref[wide] = jnp.where(later, joined, bw)
        naw_ref[wide] = jnp.where(later, aw, joined)


def first_sums_kernel(distance, mf_ref, gf_ref, a_ref, _, __, tf_ref, bf_ref, af_ref):
    later = is_later(distance)
    for wide, short in sections(a_ref.shape[0] // PAIR):
        mf, gf = mf_ref[short], gf_ref[short]
        tf_ref[short] = mapped(a_ref[wide], jnp.where(later, gf, mf)) + jnp.where(later, mf, gf)
        bf_ref[short] = jnp.where(later, gf, 0.0)
        af_ref[short] = jnp.where(later, 0.0, gf)


def next_sums_kernel(
    distance, mf_ref, gf_ref, bf_ref, af_ref, a_ref, x_ref, tf_ref, nbf_ref, naf_ref
):
    later = is_later(distance)
    for wide, short in sections(a_ref.shape[0] // PAIR):
        mf, gf, bf, af = mf_ref[short], gf_ref[short], bf_ref[short], af_ref[short]
        tf_ref[short] = mapped(a_ref[wide], jnp.where(later, gf, mf)) + jnp.where(later, mf, gf)
        sums = mapped(x_ref[wide], jnp.where(later, gf, af)) + jnp.where(later, bf, gf)
        nbf_ref[short] = jnp.where(later, sums, bf)
        naf_ref[short] = jnp.where(later, af, sums)


def local_kernel(c_ref, l_lo, l_hi, tail_ref, aw_ref, af_ref, s_ref, base_ref, v_ref):
    points, width = s_ref.shape[0] // PAIR, s_ref.shape[1]
    for g, (wide, short) in enumerate(sections(width)):
        rows = slice(g * points, (g + 1) * points)
        long = slice(g * (points + 8), (g + 1) * (points + 8))
        base_ref[rows] = s_ref[rows] + scanned(c_ref[rows], (l_lo, l_hi)[g])
        v_ref[long] = mapped(split_cols(aw_ref[wide]), tail_ref[long]) + af_ref[short][:1]


def turn_kernel(
    v_ref, gw_ref, gf_ref, bw_ref, bf_ref, p_lo, p_hi, base_ref, halo_ref, small_ref, maps_ref,
    d_lo, d_hi, s_ref, nr_ref, c_ref, msg_ref,
):
    points, width = s_ref.shape[0] // PAIR, s_ref.shape[1]
    came = []
    for g, (wide, short) in enumerate(sections(width)):
        long = slice(g * (points + 8), (g + 1) * (points + 8))
        v = mapped(split_cols(gw_ref[wide]), v_ref[long]) + gf_ref[short][:1]
        came.append(mapped(split_cols(bw_ref[wide]), v) + bf_ref[short][:1])
    moved = [
        mapped_each(p_lo, came[0][:points]),
        mapped_each_split(p_hi[...], came[1][:points]),
    ]
    s = base_ref[...] + jnp.concatenate(moved, axis=0)
    s_ref[...] = s
    correct_both(
        s[:points], s[points:],
        halo_ref[:1] + came[0][points : points + 1],
        halo_ref[4:5] + came[1][points : points + 1],
        small_ref, maps_ref, d_lo, d_hi, nr_ref, c_ref, msg_ref,
    )


def last_local_kernel(
    c_ref, l_lo, l_hi, tail_ref, aw_ref, af_ref, gw_ref, bw_ref, bf_ref, p_lo, p_hi, s_ref, base_ref
):
    points, width = s_ref.shape[0] // PAIR, s_ref.shape[1]
    came = []
    for g, (wide, short) in enumerate(sections(width)):
        at = g * (points + 8)
        v = mapped(split_cols(aw_ref[wide]), tail_ref[at : at + points]) + af_ref[short][:1]
        v = mapped(split_cols(gw_ref[wide]), v)
        came.append(mapped(split_cols(bw_ref[wide]), v) + bf_ref[short][:1])
    for g in range(PAIR):
        rows = slice(g * points, (g + 1) * points)
        moved = mapped_each_split(p_hi[...], came[g]) if g else mapped_each(p_lo, came[g])
        base_ref[rows] = s_ref[rows] + moved + scanned(c_ref[rows], (l_lo, l_hi)[g])


def end_kernel(gf_ref, bw_ref, p_lo, p_hi, base_ref, s_ref):
    points, width = s_ref.shape[0] // PAIR, s_ref.shape[1]
    for g, (wide, short) in enumerate(sections(width)):
        rows = slice(g * points, (g + 1) * points)
        v = mapped(split_cols(bw_ref[wide]), gf_ref[short])
        if g:
            both = dot_nt(split_rows(v), p_hi[...])
            both = both[:1] + both[8:9]
            moved = [both[:, i * width : (i + 1) * width] for i in range(points)]
            moved = jnp.concatenate(moved, axis=0)
        else:
            moved = mapped_each(p_lo, jnp.broadcast_to(v[:1], (points, width)))
        s_ref[rows] = base_ref[rows] + moved


def choose_kernel(both_ref, got_ref, s_ref):
    points = s_ref.shape[0]
    odd = lax.axis_index("dom") % 2 == 1
    s_ref[...] = jnp.where(odd, both_ref[points:], got_ref[:points])


def exchanged(value, distance):
    return lax.ppermute(
        value, "tm", [(i, i ^ distance) for i in range(lax.axis_size("tm"))]
    )


def swapped(value, distance):
    return lax.ppermute(value, "dom", [(i, i ^ distance) for i in range(lax.axis_size("dom"))])


def both_partitions(
    s, nr, c, msg, halo, small, maps, d_lo, d_hi, r_lo, r_hi, w
):
    points, width = s.shape[0] // PAIR, s.shape[1]
    vec, square = ((PAIR * points, width), F32), ((PAIR * width, width), F32)
    square_split = ((PAIR * width, 2 * width), BF16)
    eight = ((PAIR * 8, width), F32)
    longer = ((PAIR * (points + 8), width), F32)
    many = ((PAIR * points, width, width), F32)
    steps = (points.bit_length() - 1) * points // 2
    distances = [2**k for k in range(lax.axis_size("tm").bit_length() - 1)]

    def sums_level(level, f, bf, af, beside):
        got = exchanged(f, distances[level])
        if level == 0:
            return call(
                functools.partial(first_sums_kernel, distances[0]), [eight] * 3,
                f, got, *kept[0], *beside,
            )
        return call(
            functools.partial(next_sums_kernel, distances[level]), [eight] * 3,
            f, got, bf, af, *kept[level],
            cost=pl.CostEstimate(flops=2**33, bytes_accessed=2**25, transcendentals=0),
        )

    got = swapped(msg, 2)
    got_w = exchanged(w, distances[0])
    ss, r_lo, r_hi = call(
        suffix_kernel, [many] + [((points, width, width), F32)] * 2, r_lo, r_hi,
        in_hbm=2, scratch=[pltpu.SemaphoreType.DMA((2,))],
    )
    l_shape = ((steps, width, width), F32)
    p_lo, l_lo = call(
        functools.partial(prefix_kernel, False), [((points, width, width), F32), l_shape], r_lo
    )
    p_hi, l_hi = call(
        functools.partial(prefix_kernel, True), [((points * width, 2 * width), BF16), l_shape], r_hi
    )
    c, f = call(
        second_kernel, [vec, eight], got, s, nr, c, small, maps, d_lo, d_hi, ss
    )
    (tail,) = call(tail_kernel, [longer], c, ss)
    kept, bf, af = [], None, None
    for level, distance in enumerate(distances[:-1]):
        if level == 0:
            w, a, bw, aw = call(
                functools.partial(first_maps_kernel, distance),
                [square, square_split, square, square], w, got_w, f,
            )
            kept.append((a,))
        else:
            w, a, x, bw, aw = call(
                functools.partial(next_maps_kernel, distance),
                [square, square_split, square_split, square, square], w, got_w, bw, aw, f,
            )
            kept.append((a, x))
        got_w = exchanged(w, distances[level + 1])
        f, bf, af = sums_level(level, f, bf, af, (p_lo, p_hi))
    got, last = exchanged(f, distances[-1]), got_w
    base, v = call(local_kernel, [vec, longer], c, l_lo, l_hi, tail, aw, af, s)
    s, nr, c, msg = call(
        turn_kernel, [vec] * 4,
        v, last, got, bw, bf, p_lo, p_hi, base, halo, small, maps, d_lo, d_hi,
    )
    got = swapped(msg, 2)
    c, f = call(
        second_kernel, [vec, eight], got, s, nr, c, small, maps, d_lo, d_hi, ss
    )
    (tail,) = call(tail_kernel, [longer], c, ss)
    for level in range(len(distances) - 1):
        f, bf, af = sums_level(level, f, bf, af, (tail, tail))
    got = exchanged(f, distances[-1])
    (base,) = call(last_local_kernel, [vec], c, l_lo, l_hi, tail, aw, af, last, bw, bf, p_lo, p_hi, s)
    return call(end_kernel, [vec], got, bw, p_lo, p_hi, base)[0]


def per_device(
    starting_voltage_guess,
    injected_amperes,
    capacitance,
    conductance,
    block_pattern,
    device_gain,
    link_weight,
    boundary_vertex_list,
    diagonal_reciprocals,
    boundary_jacobian,
    transfer,
):
    points, _, width = starting_voltage_guess.shape
    segments = lax.axis_size("tm")
    (one,) = call(
        ones_kernel, [((1, width), F32)],
        cost=pl.CostEstimate(flops=2**33, bytes_accessed=2**25, transcendentals=0),
    )
    mask = jnp.broadcast_to(block_pattern[0].astype(F32), (1, width))
    s = starting_voltage_guess[:, 0]
    near_s = swapped(starting_voltage_guess, 1)[:, 0]
    d, r, near_s, mask, one = lax.optimization_barrier(
        (diagonal_reciprocals, transfer, near_s, mask, one)
    )
    d, near_d = d[:, 0, 0], swapped(d, 1)[:, 0, 0]
    r, near_r = r[:, 0, 0], swapped(r, 1)[:, 0, 0]
    (rows,) = call(halo_kernel, [((8, width), F32)], s, near_s)
    halo = lax.ppermute(rows, "tm", [(i, (i + 1) % segments) for i in range(segments)])
    (pack,) = call(
        pack_kernel, [((3 * width + points + 24, width), F32)],
        one, conductance[0], mask, link_weight[0], boundary_jacobian[0],
        injected_amperes[:, 0], capacitance, device_gain, boundary_vertex_list,
    )
    near_pack = swapped(pack, 1)
    vec = ((PAIR * points, width), F32)
    (w,) = call(
        whole_kernel, [((PAIR * width, width), F32)], near_r, r, in_hbm=2,
        scratch=[pltpu.VMEM((points, width, width), F32)] * 2 + [pltpu.SemaphoreType.DMA((2,))],
    )
    maps, small, nr, c, msg = call(
        early_kernel,
        [((6, width, 2 * width), BF16), ((PAIR * (points + 24), width), F32), vec, vec, vec],
        near_s, s, near_pack, pack, near_d, d, w,
    )
    s, nr, c, msg = call(
        first_kernel, [vec] * 4,
        halo, near_s, s, small, maps, near_d, d, nr, c, msg,
    )
    odd = lax.axis_index("dom") % 2 == 1
    both = lax.cond(
        odd,
        both_partitions,
        lambda s, *rest: s,
        s, nr, c, msg, halo, small, maps, near_d, d, near_r, r, w,
    )
    (s,) = call(choose_kernel, [((points, width), F32)], both, swapped(both, 1))
    return s[:, None]


def solution(mesh):
    in_specs = (
        P("tm", "dom", None),
        P("tm", "dom", None),
        P("dom", None),
        P("dom", None, None),
        P("dom", None, None),
        P("dom", None),
        P("dom", None, None),
        P("dom", None),
        P("tm", "dom", None, None, None),
        P("dom", None, None),
        P("tm", "dom", None, None, None),
    )
    out_specs = P("tm", "dom", None)
    return jax.shard_map(
        per_device, mesh=mesh, in_specs=in_specs, out_specs=out_specs, check_vma=False
    )
```

```python
import functools

import jax
import jax.numpy as jnp
from jax import lax
from jax.experimental import pallas as pl
from jax.experimental.pallas import tpu as pltpu
from jax.sharding import PartitionSpec as P

F32 = jnp.float32
BF16 = jnp.bfloat16
PAIR = 2


def halves(x):
    hi = x.astype(BF16)
    return hi, (x - hi.astype(F32)).astype(BF16)


def split_cols(matrix):
    return jnp.concatenate(halves(matrix), axis=1)


def split_rows(vectors):
    hi, lo = halves(vectors)
    hi, lo = hi.astype(F32), lo.astype(F32)
    top = jnp.concatenate([hi, hi], axis=1)
    low = jnp.concatenate([lo, jnp.zeros_like(lo)], axis=1)
    return jnp.concatenate([top, low], axis=0).astype(BF16)


def dot_nt(a, b):
    return lax.dot_general(a, b, (((1,), (1,)), ((), ())), preferred_element_type=F32)


def times(a, b):
    ah, al = halves(a)
    bh, bl = halves(b)
    left = jnp.concatenate([ah, al, ah], axis=1)
    right = jnp.concatenate([bh, bh, bl], axis=0)
    return jnp.dot(left, right, preferred_element_type=F32)


def mapped(matrix_split, vectors):
    count = vectors.shape[0]
    both = dot_nt(split_rows(vectors), matrix_split)
    return both[:count] + both[count:]


def mapped_each(matrices, vectors):
    rows = []
    for r in range(vectors.shape[0]):
        products = matrices[r] * vectors[r : r + 1, :]
        rows.append(jnp.sum(products.T, axis=0, keepdims=True))
    return jnp.concatenate(rows, axis=0)


def mapped_each_split(matrices_split, vectors):
    count, width = vectors.shape
    both = dot_nt(split_rows(vectors), matrices_split)
    row = lax.broadcasted_iota(jnp.int32, (2 * count, width), 0) % count
    picked = [
        jnp.where(row == r, both[:, r * width : (r + 1) * width], 0.0) for r in range(count)
    ]
    while len(picked) > 1:
        picked = [a + b for a, b in zip(picked[::2], picked[1::2])]
    return picked[0][:count] + picked[0][count:]


def mapped_sum(matrices, vectors):
    products = matrices[0] * vectors[:1, :]
    for r in range(1, vectors.shape[0]):
        products = products + matrices[r] * vectors[r : r + 1, :]
    return jnp.sum(products.T, axis=0, keepdims=True)


def call(kernel, outs, *args, cost=None, in_hbm=0, scratch=()):
    vmem = pl.BlockSpec(memory_space=pltpu.VMEM)
    return pl.pallas_call(
        kernel,
        out_shape=[jax.ShapeDtypeStruct(s, d) for s, d in outs],
        in_specs=[vmem] * (len(args) - in_hbm) + [pl.BlockSpec(memory_space=pltpu.HBM)] * in_hbm,
        out_specs=[vmem] * len(outs),
        scratch_shapes=list(scratch),
        cost_estimate=cost,
        compiler_params=pltpu.CompilerParams(vmem_limit_bytes=24 * 2**20),
    )(*args)


def identity(width):
    return (
        lax.broadcasted_iota(jnp.int32, (width, width), 0)
        == lax.broadcasted_iota(jnp.int32, (width, width), 1)
    ).astype(F32)


def halo_kernel(s_ref, near_ref, msg_ref):
    points, width = s_ref.shape
    msg_ref[:4] = jnp.broadcast_to(near_ref[points - 1 :], (4, width))
    msg_ref[4:] = jnp.broadcast_to(s_ref[points - 1 :], (4, width))


def ones_kernel(one_ref):
    one_ref[...] = jnp.ones(one_ref.shape, F32)


def pack_kernel(one_ref, g_ref, mask_ref, k_ref, j_ref, inj_ref, cap_ref, gain_ref, bnd_ref, pack_ref):
    points, width = inj_ref.shape
    pack_ref[:width] = g_ref[...] * (mask_ref[...] * one_ref[...])
    pack_ref[width : 2 * width] = k_ref[...]
    pack_ref[2 * width : 3 * width] = j_ref[...]
    at = 3 * width
    pack_ref[at : at + points] = inj_ref[...]
    at += points
    for one in (cap_ref[...], gain_ref[...], bnd_ref[...].astype(F32)):
        pack_ref[at : at + 8] = jnp.broadcast_to(one, (8, width))
        at += 8


def vectors(small_ref, g, points):
    at = g * (points + 24)
    inj = small_ref[at : at + points]
    at += points
    cap, gain, bnd = (small_ref[at + 8 * i : at + 8 * i + 1] for i in range(3))
    return inj, cap, gain, bnd.astype(jnp.int32)


def fetched(sources, targets, sems):
    moves = [
        pltpu.make_async_copy(source, target, sems.at[i])
        for i, (source, target) in enumerate(zip(sources, targets))
    ]
    for move in moves:
        move.start()
    return moves


def whole_kernel(lo_ref, hi_ref, w_ref, r_lo, r_hi, sems):
    points, width = lo_ref.shape[0], lo_ref.shape[1]
    moves = fetched((lo_ref, hi_ref), (r_lo, r_hi), sems)
    u = []
    for move, r_ref in zip(moves, (r_lo, r_hi)):
        move.wait()
        u += [times(r_ref[i + 1], r_ref[i]) for i in range(0, points, 2)]
    while len(u) > PAIR:
        u = [times(u[i + 1], u[i]) for i in range(0, len(u), 2)]
    for g in range(PAIR):
        w_ref[g * width : (g + 1) * width] = u[g]


def suffix_kernel(r_lo, r_hi, lo_ref, hi_ref, s_ref, d_lo, d_hi, sems):
    points, width = r_lo.shape[0], r_lo.shape[1]
    moves = fetched((lo_ref, hi_ref), (d_lo, d_hi), sems)
    for g, r_ref in enumerate((r_lo, r_hi)):
        u = [r_ref[i] for i in range(points)]
        span = 1
        while span < points:
            for base in range(0, points, 2 * span):
                prod = times(u[base + span], jnp.concatenate(u[base : base + span], axis=1))
                for i in range(span):
                    u[base + i] = prod[:, i * width : (i + 1) * width]
            span *= 2
        for i in range(points - 1):
            s_ref[g * points + i] = u[i + 1]
        s_ref[(g + 1) * points - 1] = identity(width)
    for move in moves:
        move.wait()


def prefix_kernel(split, r_ref, p_ref, l_ref):
    points, width = r_ref.shape[0], r_ref.shape[1]
    q = [r_ref[i] for i in range(points)]
    span, slot = 1, 0
    while span < points:
        for base in range(0, points, 2 * span):
            upper = q[base + span : base + 2 * span]
            for matrix in upper:
                l_ref[slot] = matrix
                slot += 1
            prod = times(jnp.concatenate(upper, axis=0), q[base + span - 1])
            for i in range(span):
                q[base + span + i] = prod[i * width : (i + 1) * width]
        span *= 2
    for i in range(points):
        if split:
            p_ref[i * width : (i + 1) * width] = split_cols(q[i])
        else:
            p_ref[i] = q[i]


def scanned(c, l_ref):
    points = c.shape[0]
    x = [c[i : i + 1, :] for i in range(points)]
    span, slot = 1, 0
    while span < points:
        for base in range(0, points, 2 * span):
            head = x[base + span - 1]
            for i in range(base + span, base + 2 * span):
                x[i] = x[i] + mapped_each(l_ref[slot : slot + 1], head)
                slot += 1
        span *= 2
    return jnp.concatenate(x, axis=0)


def taken(rows, lanes):
    return jnp.take_along_axis(rows, jnp.broadcast_to(lanes, rows.shape), axis=1)


def negative_residual(s, halo, inj, cap, gain, gs):
    before = jnp.concatenate([halo, s[: s.shape[0] - 1]], axis=0)
    return inj - cap * (s - before) - mapped(gs, s) - gain * jnp.tanh(s)


def corrected(nr, c_before, s_before, d_ref, js, ks):
    return mapped_each(d_ref, nr + mapped(js, c_before) + mapped(ks, s_before))


def pair_corrected(nr, s_lo, c_lo, bnd_lo, d_hi_ref, js, ks):
    return corrected(nr, taken(c_lo, bnd_lo), taken(s_lo, bnd_lo), d_hi_ref, js, ks)


def correct_both(
    s_lo, s_hi, halo_lo, halo_hi, small_ref, maps_ref, d_lo, d_hi, nr_ref, c_ref, msg_ref
):
    lo_maps, hi_maps = [maps_ref[i] for i in range(3)], [maps_ref[i] for i in range(3, 6)]
    points = s_lo.shape[0]
    inj_lo, cap_lo, gain_lo, bnd_lo = vectors(small_ref, 0, points)
    inj_hi, cap_hi, gain_hi, bnd_hi = vectors(small_ref, 1, points)
    nr_lo = negative_residual(s_lo, halo_lo, inj_lo, cap_lo, gain_lo, lo_maps[0])
    nr_hi = negative_residual(s_hi, halo_hi, inj_hi, cap_hi, gain_hi, hi_maps[0])
    nr_ref[:points], nr_ref[points:] = nr_lo, nr_hi
    msg_ref[points:] = taken(s_hi, bnd_hi)

    @pl.when(in_first_pair())
    def _():
        c_lo = mapped_each(d_lo, nr_lo)
        c_hi = pair_corrected(nr_hi, s_lo, c_lo, bnd_lo, d_hi, hi_maps[2], hi_maps[1])
        c_ref[:points], c_ref[points:] = c_lo, c_hi
        msg_ref[:points] = taken(c_hi, bnd_hi)

    @pl.when(jnp.logical_not(in_first_pair()))
    def _():
        c_ref[...] = jnp.zeros(c_ref.shape, F32)
        msg_ref[:points] = jnp.zeros((points, c_ref.shape[1]), F32)


def early_kernel(s_lo, s_hi, pack_lo, pack_hi, _, maps_ref, small_ref, nr_ref):
    points, width = s_lo.shape
    for i in range(3):
        rows = slice(i * width, (i + 1) * width)
        maps_ref[i] = split_cols(pack_lo[rows])
        maps_ref[3 + i] = split_cols(pack_hi[rows])
    none = jnp.zeros((1, width), F32)
    for g, (s_ref, pack) in enumerate(((s_lo, pack_lo), (s_hi, pack_hi))):
        at = g * (points + 24)
        small_ref[at : at + points + 24] = pack[3 * width :]
        inj, cap, gain, _ = vectors(small_ref, g, points)
        nr_ref[g * points : (g + 1) * points] = negative_residual(
            s_ref[...], none, inj, cap, gain, maps_ref[3 * g]
        )


def diagonal_kernel(lo_ref, hi_ref, d_lo, d_hi, sems):
    for move in fetched((lo_ref, hi_ref), (d_lo, d_hi), sems):
        move.wait()


def in_first_pair():
    return lax.axis_index("dom") < PAIR


def first_kernel(
    halo_ref, s_lo, s_hi, small_ref, maps_ref, d_lo, d_hi, old_nr, s_ref, nr_ref, c_ref, msg_ref
):
    points = s_lo.shape[0]
    bnd_lo, bnd_hi = (vectors(small_ref, g, points)[3] for g in range(PAIR))
    s_ref[:points], s_ref[points:] = s_lo[...], s_hi[...]
    msg_ref[points:] = taken(s_hi[...], bnd_hi)
    nr_ref[...] = old_nr[...]
    for g in range(PAIR):
        at = g * points
        cap = vectors(small_ref, g, points)[1]
        nr_ref[at : at + 1] = old_nr[at : at + 1] + cap * halo_ref[4 * g : 4 * g + 1]

    @pl.when(in_first_pair())
    def _():
        c_lo = mapped_each(d_lo, nr_ref[:points])
        linked = mapped(maps_ref[4], taken(s_lo[...], bnd_lo))
        c_hi = mapped_each(
            d_hi, nr_ref[points:] + linked + mapped(maps_ref[5], taken(c_lo, bnd_lo))
        )
        c_ref[:points], c_ref[points:] = c_lo, c_hi
        msg_ref[:points] = taken(c_hi, bnd_hi)

    @pl.when(jnp.logical_not(in_first_pair()))
    def _():
        c_ref[...] = jnp.zeros(c_ref.shape, F32)
        msg_ref[:points] = jnp.zeros((points, c_ref.shape[1]), F32)


def second_kernel(
    got_ref, s_ref, nr_ref, c_ref, small_ref, maps_ref, d_lo, d_hi, ss_ref, new_c_ref, f_ref
):
    points, width = got_ref.shape[0] // 2, got_ref.shape[1]
    second_pair = lax.axis_index("dom") >= PAIR

    @pl.when(second_pair)
    def _():
        bnd_lo = vectors(small_ref, 0, points)[3]
        c_lo = corrected(
            nr_ref[:points], got_ref[:points], got_ref[points:], d_lo, maps_ref[2], maps_ref[1]
        )
        new_c_ref[:points] = c_lo
        c_hi = pair_corrected(
            nr_ref[points:], s_ref[:points], c_lo, bnd_lo, d_hi, maps_ref[5], maps_ref[4]
        )
        new_c_ref[points:] = c_hi
        for g, c in enumerate((c_lo, c_hi)):
            whole = mapped_sum(ss_ref[g * points : (g + 1) * points], c)
            f_ref[8 * g : 8 * g + 8] = jnp.broadcast_to(whole, (8, width))

    @pl.when(jnp.logical_not(second_pair))
    def _():
        new_c_ref[...] = c_ref[...]
        for g in range(PAIR):
            rows = slice(g * points, (g + 1) * points)
            whole = mapped_sum(ss_ref[rows], c_ref[rows])
            f_ref[8 * g : 8 * g + 8] = jnp.broadcast_to(whole, (8, width))


def tail_kernel(c_ref, ss_ref, tail_ref):
    points, width = c_ref.shape[0] // PAIR, c_ref.shape[1]
    each = mapped_each(ss_ref, c_ref[...])
    for g in range(PAIR):
        total = each[g * points : (g + 1) * points]
        shift = 1
        while shift < points:
            total = total + jnp.concatenate(
                [total[shift:], jnp.zeros((shift, width), F32)], axis=0
            )
            shift *= 2
        at = g * (points + 8)
        tail_ref[at : at + points] = jnp.concatenate(
            [total[1:], jnp.zeros((1, width), F32)], axis=0
        )
        tail_ref[at + points : at + points + 8] = jnp.broadcast_to(total[:1], (8, width))


def is_later(distance):
    return (lax.axis_index("tm") // distance) % 2 == 1


def sections(width):
    return [
        (slice(g * width, (g + 1) * width), slice(8 * g, 8 * g + 8)) for g in range(PAIR)
    ]


def first_maps_kernel(distance, mw_ref, gw_ref, _, tw_ref, a_ref, bw_ref, aw_ref):
    width = mw_ref.shape[1]
    later = is_later(distance)
    eye = identity(width)
    for wide, _ in sections(width):
        mw, gw = mw_ref[wide], gw_ref[wide]
        a = jnp.where(later, mw, gw)
        tw_ref[wide] = times(a, jnp.where(later, gw, mw))
        a_ref[wide] = split_cols(a)
        bw_ref[wide] = jnp.where(later, gw, eye)
        aw_ref[wide] = jnp.where(later, eye, gw)


def next_maps_kernel(
    distance, mw_ref, gw_ref, bw_ref, aw_ref, _, tw_ref, a_ref, x_ref, nbw_ref, naw_ref
):
    width = mw_ref.shape[1]
    later = is_later(distance)
    for wide, _ in sections(width):
        mw, gw, bw, aw = mw_ref[wide], gw_ref[wide], bw_ref[wide], aw_ref[wide]
        a = jnp.where(later, mw, gw)
        tw_ref[wide] = times(a, jnp.where(later, gw, mw))
        a_ref[wide] = split_cols(a)
        x = jnp.where(later, bw, gw)
        joined = times(x, jnp.where(later, gw, aw))
        x_ref[wide] = split_cols(x)
        nbw_ref[wide] = jnp.where(later, joined, bw)
        naw_ref[wide] = jnp.where(later, aw, joined)


def first_sums_kernel(distance, mf_ref, gf_ref, a_ref, _, __, tf_ref, bf_ref, af_ref):
    later = is_later(distance)
    for wide, short in sections(a_ref.shape[0] // PAIR):
        mf, gf = mf_ref[short], gf_ref[short]
        tf_ref[short] = mapped(a_ref[wide], jnp.where(later, gf, mf)) + jnp.where(later, mf, gf)
        bf_ref[short] = jnp.where(later, gf, 0.0)
        af_ref[short] = jnp.where(later, 0.0, gf)


def next_sums_kernel(
    distance, mf_ref, gf_ref, bf_ref, af_ref, a_ref, x_ref, _, tf_ref, nbf_ref, naf_ref
):
    later = is_later(distance)
    for wide, short in sections(a_ref.shape[0] // PAIR):
        mf, gf, bf, af = mf_ref[short], gf_ref[short], bf_ref[short], af_ref[short]
        tf_ref[short] = mapped(a_ref[wide], jnp.where(later, gf, mf)) + jnp.where(later, mf, gf)
        sums = mapped(x_ref[wide], jnp.where(later, gf, af)) + jnp.where(later, bf, gf)
        nbf_ref[short] = jnp.where(later, sums, bf)
        naf_ref[short] = jnp.where(later, af, sums)


def local_kernel(c_ref, l_lo, l_hi, tail_ref, aw_ref, af_ref, s_ref, base_ref, v_ref):
    points, width = s_ref.shape[0] // PAIR, s_ref.shape[1]
    for g, (wide, short) in enumerate(sections(width)):
        rows = slice(g * points, (g + 1) * points)
        long = slice(g * (points + 8), (g + 1) * (points + 8))
        base_ref[rows] = s_ref[rows] + scanned(c_ref[rows], (l_lo, l_hi)[g])
        v_ref[long] = mapped(split_cols(aw_ref[wide]), tail_ref[long]) + af_ref[short][:1]


def turn_kernel(
    v_ref, gw_ref, gf_ref, bw_ref, bf_ref, p_lo, p_hi, base_ref, halo_ref, small_ref, maps_ref,
    d_lo, d_hi, s_ref, nr_ref, c_ref, msg_ref,
):
    points, width = s_ref.shape[0] // PAIR, s_ref.shape[1]
    came = []
    for g, (wide, short) in enumerate(sections(width)):
        long = slice(g * (points + 8), (g + 1) * (points + 8))
        v = mapped(split_cols(gw_ref[wide]), v_ref[long]) + gf_ref[short][:1]
        came.append(mapped(split_cols(bw_ref[wide]), v) + bf_ref[short][:1])
    moved = [
        mapped_each(p_lo, came[0][:points]),
        mapped_each_split(p_hi[...], came[1][:points]),
    ]
    s = base_ref[...] + jnp.concatenate(moved, axis=0)
    s_ref[...] = s
    correct_both(
        s[:points], s[points:],
        halo_ref[:1] + came[0][points : points + 1],
        halo_ref[4:5] + came[1][points : points + 1],
        small_ref, maps_ref, d_lo, d_hi, nr_ref, c_ref, msg_ref,
    )


def scan_kernel(c_ref, l_lo, l_hi, s_ref, base_ref):
    points = s_ref.shape[0] // PAIR
    for g, l_ref in enumerate((l_lo, l_hi)):
        rows = slice(g * points, (g + 1) * points)
        base_ref[rows] = s_ref[rows] + scanned(c_ref[rows], l_ref)


def last_local_kernel(
    tail_ref, aw_ref, af_ref, gw_ref, bw_ref, bf_ref, p_lo, p_hi, old_ref, base_ref
):
    points, width = old_ref.shape[0] // PAIR, old_ref.shape[1]
    came = []
    for g, (wide, short) in enumerate(sections(width)):
        at = g * (points + 8)
        v = mapped(split_cols(aw_ref[wide]), tail_ref[at : at + points]) + af_ref[short][:1]
        v = mapped(split_cols(gw_ref[wide]), v)
        came.append(mapped(split_cols(bw_ref[wide]), v) + bf_ref[short][:1])
    for g in range(PAIR):
        rows = slice(g * points, (g + 1) * points)
        moved = mapped_each_split(p_hi[...], came[g]) if g else mapped_each(p_lo, came[g])
        base_ref[rows] = old_ref[rows] + moved


def end_kernel(gf_ref, bw_ref, p_lo, p_hi, base_ref, s_ref):
    points, width = s_ref.shape[0] // PAIR, s_ref.shape[1]
    for g, (wide, short) in enumerate(sections(width)):
        rows = slice(g * points, (g + 1) * points)
        v = mapped(split_cols(bw_ref[wide]), gf_ref[short])
        if g:
            both = dot_nt(split_rows(v), p_hi[...])
            both = both[:1] + both[8:9]
            moved = [both[:, i * width : (i + 1) * width] for i in range(points)]
            moved = jnp.concatenate(moved, axis=0)
        else:
            moved = mapped_each(p_lo, jnp.broadcast_to(v[:1], (points, width)))
        s_ref[rows] = base_ref[rows] + moved


def choose_kernel(both_ref, got_ref, s_ref):
    points = s_ref.shape[0]
    odd = lax.axis_index("dom") % 2 == 1
    s_ref[...] = jnp.where(odd, both_ref[points:], got_ref[:points])


def exchanged(value, distance):
    return lax.ppermute(
        value, "tm", [(i, i ^ distance) for i in range(lax.axis_size("tm"))]
    )


def swapped(value, distance):
    return lax.ppermute(value, "dom", [(i, i ^ distance) for i in range(lax.axis_size("dom"))])


def both_partitions(
    s, nr, c, msg, halo, small, maps, d_lo, d_hi, r_lo, r_hi, w
):
    points, width = s.shape[0] // PAIR, s.shape[1]
    vec, square = ((PAIR * points, width), F32), ((PAIR * width, width), F32)
    square_split = ((PAIR * width, 2 * width), BF16)
    eight = ((PAIR * 8, width), F32)
    longer = ((PAIR * (points + 8), width), F32)
    many = ((PAIR * points, width, width), F32)
    steps = (points.bit_length() - 1) * points // 2
    distances = [2**k for k in range(lax.axis_size("tm").bit_length() - 1)]

    def sums_level(level, f, bf, af, beside):
        got = exchanged(f, distances[level])
        if level == 0:
            return call(
                functools.partial(first_sums_kernel, distances[0]), [eight] * 3,
                f, got, *kept[0], *beside,
            )
        return call(
            functools.partial(next_sums_kernel, distances[level]), [eight] * 3,
            f, got, bf, af, *kept[level], beside[1],
            cost=pl.CostEstimate(flops=2**33, bytes_accessed=2**25, transcendentals=0),
        )

    got = swapped(msg, 2)
    got_w = exchanged(w, distances[0])
    ss, d_lo, d_hi = call(
        suffix_kernel, [many] + [((points, width, width), F32)] * 2, r_lo, r_hi, d_lo, d_hi,
        in_hbm=2, scratch=[pltpu.SemaphoreType.DMA((2,))],
    )
    l_shape = ((steps, width, width), F32)
    p_lo, l_lo = call(
        functools.partial(prefix_kernel, False), [((points, width, width), F32), l_shape], r_lo
    )
    p_hi, l_hi = call(
        functools.partial(prefix_kernel, True), [((points * width, 2 * width), BF16), l_shape], r_hi
    )
    c, f = call(
        second_kernel, [vec, eight], got, s, nr, c, small, maps, d_lo, d_hi, ss
    )
    (tail,) = call(tail_kernel, [longer], c, ss)
    kept, bf, af = [], None, None
    for level, distance in enumerate(distances[:-1]):
        if level == 0:
            w, a, bw, aw = call(
                functools.partial(first_maps_kernel, distance),
                [square, square_split, square, square], w, got_w, f,
            )
            kept.append((a,))
        else:
            w, a, x, bw, aw = call(
                functools.partial(next_maps_kernel, distance),
                [square, square_split, square_split, square, square], w, got_w, bw, aw, f,
            )
            kept.append((a, x))
        got_w = exchanged(w, distances[level + 1])
        f, bf, af = sums_level(level, f, bf, af, (p_lo, p_hi))
    got, last = exchanged(f, distances[-1]), got_w
    base, v = call(local_kernel, [vec, longer], c, l_lo, l_hi, tail, aw, af, s)
    s, nr, c, msg = call(
        turn_kernel, [vec] * 4,
        v, last, got, bw, bf, p_lo, p_hi, base, halo, small, maps, d_lo, d_hi,
    )
    got = swapped(msg, 2)
    c, f = call(
        second_kernel, [vec, eight], got, s, nr, c, small, maps, d_lo, d_hi, ss
    )
    (tail,) = call(tail_kernel, [longer], c, ss)
    (base,) = call(scan_kernel, [vec], c, l_lo, l_hi, s)
    for level in range(len(distances) - 1):
        f, bf, af = sums_level(level, f, bf, af, (tail, base))
    got = exchanged(f, distances[-1])
    (base,) = call(last_local_kernel, [vec], tail, aw, af, last, bw, bf, p_lo, p_hi, base)
    return call(end_kernel, [vec], got, bw, p_lo, p_hi, base)[0]


def per_device(
    starting_voltage_guess,
    injected_amperes,
    capacitance,
    conductance,
    block_pattern,
    device_gain,
    link_weight,
    boundary_vertex_list,
    diagonal_reciprocals,
    boundary_jacobian,
    transfer,
):
    points, _, width = starting_voltage_guess.shape
    segments = lax.axis_size("tm")
    (one,) = call(
        ones_kernel, [((1, width), F32)],
        cost=pl.CostEstimate(flops=2**33, bytes_accessed=2**25, transcendentals=0),
    )
    mask = jnp.broadcast_to(block_pattern[0].astype(F32), (1, width))
    s = starting_voltage_guess[:, 0]
    near_s = swapped(starting_voltage_guess, 1)[:, 0]
    d, r, near_s, mask, one = lax.optimization_barrier(
        (diagonal_reciprocals, transfer, near_s, mask, one)
    )
    d, near_d = d[:, 0, 0], swapped(d, 1)[:, 0, 0]
    r, near_r = r[:, 0, 0], swapped(r, 1)[:, 0, 0]
    (rows,) = call(halo_kernel, [((8, width), F32)], s, near_s)
    halo = lax.ppermute(rows, "tm", [(i, (i + 1) % segments) for i in range(segments)])
    (pack,) = call(
        pack_kernel, [((3 * width + points + 24, width), F32)],
        one, conductance[0], mask, link_weight[0], boundary_jacobian[0],
        injected_amperes[:, 0], capacitance, device_gain, boundary_vertex_list,
    )
    near_pack = swapped(pack, 1)
    vec = ((PAIR * points, width), F32)
    (w,) = call(
        whole_kernel, [((PAIR * width, width), F32)], near_r, r, in_hbm=2,
        scratch=[pltpu.VMEM((points, width, width), F32)] * 2 + [pltpu.SemaphoreType.DMA((2,))],
    )
    maps, small, nr = call(
        early_kernel,
        [((6, width, 2 * width), BF16), ((PAIR * (points + 24), width), F32), vec],
        near_s, s, near_pack, pack, w,
    )
    d_lo, d_hi = call(
        diagonal_kernel, [((points, width, width), F32)] * 2, near_d, d,
        in_hbm=2, scratch=[pltpu.SemaphoreType.DMA((2,))],
    )
    s, nr, c, msg = call(
        first_kernel, [vec] * 4, halo, near_s, s, small, maps, d_lo, d_hi, nr
    )
    odd = lax.axis_index("dom") % 2 == 1
    both = lax.cond(
        odd,
        both_partitions,
        lambda s, *rest: s,
        s, nr, c, msg, halo, small, maps, near_d, d, near_r, r, w,
    )
    (s,) = call(choose_kernel, [((points, width), F32)], both, swapped(both, 1))
    return s[:, None]


def solution(mesh):
    in_specs = (
        P("tm", "dom", None),
        P("tm", "dom", None),
        P("dom", None),
        P("dom", None, None),
        P("dom", None, None),
        P("dom", None),
        P("dom", None, None),
        P("dom", None),
        P("tm", "dom", None, None, None),
        P("dom", None, None),
        P("tm", "dom", None, None, None),
    )
    out_specs = P("tm", "dom", None)
    return jax.shard_map(
        per_device, mesh=mesh, in_specs=in_specs, out_specs=out_specs, check_vma=False
    )
```

```python
import functools

import jax
import jax.numpy as jnp
from jax import lax
from jax.experimental import pallas as pl
from jax.experimental.pallas import tpu as pltpu
from jax.sharding import PartitionSpec as P

F32 = jnp.float32
BF16 = jnp.bfloat16
PAIR = 2


def halves(x):
    hi = x.astype(BF16)
    return hi, (x - hi.astype(F32)).astype(BF16)


def split_cols(matrix):
    return jnp.concatenate(halves(matrix), axis=1)


def split_rows(vectors):
    hi, lo = halves(vectors)
    hi, lo = hi.astype(F32), lo.astype(F32)
    top = jnp.concatenate([hi, hi], axis=1)
    low = jnp.concatenate([lo, jnp.zeros_like(lo)], axis=1)
    return jnp.concatenate([top, low], axis=0).astype(BF16)


def dot_nt(a, b):
    return lax.dot_general(a, b, (((1,), (1,)), ((), ())), preferred_element_type=F32)


def times(a, b):
    ah, al = halves(a)
    bh, bl = halves(b)
    left = jnp.concatenate([ah, al, ah], axis=1)
    right = jnp.concatenate([bh, bh, bl], axis=0)
    return jnp.dot(left, right, preferred_element_type=F32)


def mapped(matrix_split, vectors):
    count = vectors.shape[0]
    both = dot_nt(split_rows(vectors), matrix_split)
    return both[:count] + both[count:]


def mapped_each(matrices, vectors):
    rows = []
    for r in range(vectors.shape[0]):
        products = matrices[r] * vectors[r : r + 1, :]
        rows.append(jnp.sum(products.T, axis=0, keepdims=True))
    return jnp.concatenate(rows, axis=0)


def mapped_each_split(matrices_split, vectors):
    count, width = vectors.shape
    both = dot_nt(split_rows(vectors), matrices_split)
    row = lax.broadcasted_iota(jnp.int32, (2 * count, width), 0) % count
    picked = [
        jnp.where(row == r, both[:, r * width : (r + 1) * width], 0.0) for r in range(count)
    ]
    while len(picked) > 1:
        picked = [a + b for a, b in zip(picked[::2], picked[1::2])]
    return picked[0][:count] + picked[0][count:]


def mapped_sum(matrices, vectors):
    products = matrices[0] * vectors[:1, :]
    for r in range(1, vectors.shape[0]):
        products = products + matrices[r] * vectors[r : r + 1, :]
    return jnp.sum(products.T, axis=0, keepdims=True)


def call(kernel, outs, *args, cost=None, in_hbm=0, scratch=()):
    vmem = pl.BlockSpec(memory_space=pltpu.VMEM)
    return pl.pallas_call(
        kernel,
        out_shape=[jax.ShapeDtypeStruct(s, d) for s, d in outs],
        in_specs=[vmem] * (len(args) - in_hbm) + [pl.BlockSpec(memory_space=pltpu.HBM)] * in_hbm,
        out_specs=[vmem] * len(outs),
        scratch_shapes=list(scratch),
        cost_estimate=cost,
        compiler_params=pltpu.CompilerParams(vmem_limit_bytes=24 * 2**20),
    )(*args)


def identity(width):
    return (
        lax.broadcasted_iota(jnp.int32, (width, width), 0)
        == lax.broadcasted_iota(jnp.int32, (width, width), 1)
    ).astype(F32)


def halo_kernel(s_ref, near_ref, msg_ref):
    points, width = s_ref.shape
    msg_ref[:4] = jnp.broadcast_to(near_ref[points - 1 :], (4, width))
    msg_ref[4:] = jnp.broadcast_to(s_ref[points - 1 :], (4, width))


def ones_kernel(one_ref):
    one_ref[...] = jnp.ones(one_ref.shape, F32)


def pack_kernel(one_ref, g_ref, mask_ref, k_ref, j_ref, inj_ref, cap_ref, gain_ref, bnd_ref, pack_ref):
    points, width = inj_ref.shape
    pack_ref[:width] = g_ref[...] * (mask_ref[...] * one_ref[...])
    pack_ref[width : 2 * width] = k_ref[...]
    pack_ref[2 * width : 3 * width] = j_ref[...]
    at = 3 * width
    pack_ref[at : at + points] = inj_ref[...]
    at += points
    for one in (cap_ref[...], gain_ref[...], bnd_ref[...].astype(F32)):
        pack_ref[at : at + 8] = jnp.broadcast_to(one, (8, width))
        at += 8


def vectors(small_ref, g, points):
    at = g * (points + 24)
    inj = small_ref[at : at + points]
    at += points
    cap, gain, bnd = (small_ref[at + 8 * i : at + 8 * i + 1] for i in range(3))
    return inj, cap, gain, bnd.astype(jnp.int32)


def fetched(sources, targets, sems):
    moves = [
        pltpu.make_async_copy(source, target, sems.at[i])
        for i, (source, target) in enumerate(zip(sources, targets))
    ]
    for move in moves:
        move.start()
    return moves


def whole_kernel(lo_ref, hi_ref, w_ref, r_lo, r_hi, sems):
    points, width = lo_ref.shape[0], lo_ref.shape[1]
    moves = fetched((lo_ref, hi_ref), (r_lo, r_hi), sems)
    u = []
    for move, r_ref in zip(moves, (r_lo, r_hi)):
        move.wait()
        u += [times(r_ref[i + 1], r_ref[i]) for i in range(0, points, 2)]
    while len(u) > PAIR:
        u = [times(u[i + 1], u[i]) for i in range(0, len(u), 2)]
    for g in range(PAIR):
        w_ref[g * width : (g + 1) * width] = u[g]


def suffix_kernel(r_lo, r_hi, lo_ref, hi_ref, s_ref, d_lo, d_hi, sems):
    points, width = r_lo.shape[0], r_lo.shape[1]
    moves = fetched((lo_ref, hi_ref), (d_lo, d_hi), sems)
    both = [[r_ref[i] for i in range(points)] for r_ref in (r_lo, r_hi)]
    span = 1
    while span < points:
        for base in range(0, points, 2 * span):
            first = max(base, 1)
            if first == base + span:
                continue
            for u in both:
                prod = times(u[base + span], jnp.concatenate(u[first : base + span], axis=1))
                for i in range(first, base + span):
                    at = (i - first) * width
                    u[i] = prod[:, at : at + width]
        span *= 2
    for g, u in enumerate(both):
        for i in range(points - 1):
            s_ref[g * points + i] = u[i + 1]
        s_ref[(g + 1) * points - 1] = identity(width)
    for move in moves:
        move.wait()


def prefix_kernel(r_lo, r_hi, p_lo, l_lo, p_hi, l_hi):
    points, width = r_lo.shape[0], r_lo.shape[1]
    both = [[r_ref[i] for i in range(points)] for r_ref in (r_lo, r_hi)]
    span, slot = 1, 0
    while span < points:
        for base in range(0, points, 2 * span):
            for q, l_ref in zip(both, (l_lo, l_hi)):
                upper = q[base + span : base + 2 * span]
                for i, matrix in enumerate(upper):
                    if l_ref is l_hi:
                        at = (slot + i) * width
                        l_ref[at : at + width] = split_cols(matrix)
                    else:
                        l_ref[slot + i] = matrix
                prod = times(jnp.concatenate(upper, axis=0), q[base + span - 1])
                for i in range(span):
                    q[base + span + i] = prod[i * width : (i + 1) * width]
            slot += span
        span *= 2
    for i in range(points):
        p_lo[i] = both[0][i]
        p_hi[i * width : (i + 1) * width] = split_cols(both[1][i])


def scanned(c, l_ref):
    points = c.shape[0]
    x = [c[i : i + 1, :] for i in range(points)]
    span, slot = 1, 0
    while span < points:
        for base in range(0, points, 2 * span):
            head = x[base + span - 1]
            for i in range(base + span, base + 2 * span):
                x[i] = x[i] + mapped_each(l_ref[slot : slot + 1], head)
                slot += 1
        span *= 2
    return jnp.concatenate(x, axis=0)


def scanned_split(c, l_ref):
    points, width = c.shape
    half = points // 2
    x = [c[i : i + 1, :] for i in range(points)]
    span, level = 1, 0
    while span < points:
        later = [i for i in range(points) if i & span]
        heads = jnp.concatenate([x[(i & ~(2 * span - 1)) + span - 1] for i in later], axis=0)
        rows = slice(level * half * width, (level + 1) * half * width)
        moved = mapped_each_split(l_ref[rows], heads)
        for slot, i in enumerate(later):
            x[i] = x[i] + moved[slot : slot + 1]
        span *= 2
        level += 1
    return jnp.concatenate(x, axis=0)


def taken(rows, lanes):
    return jnp.take_along_axis(rows, jnp.broadcast_to(lanes, rows.shape), axis=1)


def negative_residual(s, halo, inj, cap, gain, gs):
    before = jnp.concatenate([halo, s[: s.shape[0] - 1]], axis=0)
    return inj - cap * (s - before) - mapped(gs, s) - gain * jnp.tanh(s)


def corrected(nr, c_before, s_before, d_ref, js, ks):
    return mapped_each(d_ref, nr + mapped(js, c_before) + mapped(ks, s_before))


def pair_corrected(nr, s_lo, c_lo, bnd_lo, d_hi_ref, js, ks):
    return corrected(nr, taken(c_lo, bnd_lo), taken(s_lo, bnd_lo), d_hi_ref, js, ks)


def correct_both(
    s_lo, s_hi, halo_lo, halo_hi, small_ref, maps_ref, d_lo, d_hi, nr_ref, c_ref, msg_ref
):
    lo_maps, hi_maps = [maps_ref[i] for i in range(3)], [maps_ref[i] for i in range(3, 6)]
    points = s_lo.shape[0]
    inj_lo, cap_lo, gain_lo, bnd_lo = vectors(small_ref, 0, points)
    inj_hi, cap_hi, gain_hi, bnd_hi = vectors(small_ref, 1, points)
    nr_lo = negative_residual(s_lo, halo_lo, inj_lo, cap_lo, gain_lo, lo_maps[0])
    nr_hi = negative_residual(s_hi, halo_hi, inj_hi, cap_hi, gain_hi, hi_maps[0])
    nr_ref[:points], nr_ref[points:] = nr_lo, nr_hi
    msg_ref[points:] = taken(s_hi, bnd_hi)

    @pl.when(in_first_pair())
    def _():
        c_lo = mapped_each(d_lo, nr_lo)
        c_hi = pair_corrected(nr_hi, s_lo, c_lo, bnd_lo, d_hi, hi_maps[2], hi_maps[1])
        c_ref[:points], c_ref[points:] = c_lo, c_hi
        msg_ref[:points] = taken(c_hi, bnd_hi)

    @pl.when(jnp.logical_not(in_first_pair()))
    def _():
        c_ref[...] = jnp.zeros(c_ref.shape, F32)
        msg_ref[:points] = jnp.zeros((points, c_ref.shape[1]), F32)


def early_kernel(s_lo, s_hi, pack_lo, pack_hi, _, maps_ref, small_ref, nr_ref):
    points, width = s_lo.shape
    for i in range(3):
        rows = slice(i * width, (i + 1) * width)
        maps_ref[i] = split_cols(pack_lo[rows])
        maps_ref[3 + i] = split_cols(pack_hi[rows])
    none = jnp.zeros((1, width), F32)
    for g, (s_ref, pack) in enumerate(((s_lo, pack_lo), (s_hi, pack_hi))):
        at = g * (points + 24)
        small_ref[at : at + points + 24] = pack[3 * width :]
        inj, cap, gain, _ = vectors(small_ref, g, points)
        nr_ref[g * points : (g + 1) * points] = negative_residual(
            s_ref[...], none, inj, cap, gain, maps_ref[3 * g]
        )


def diagonal_kernel(_, lo_ref, hi_ref, d_lo, d_hi, sems):
    for move in fetched((lo_ref, hi_ref), (d_lo, d_hi), sems):
        move.wait()


def in_first_pair():
    return lax.axis_index("dom") < PAIR


def first_kernel(
    halo_ref, s_lo, s_hi, small_ref, maps_ref, d_lo, d_hi, old_nr, s_ref, nr_ref, c_ref, msg_ref
):
    points = s_lo.shape[0]
    bnd_lo, bnd_hi = (vectors(small_ref, g, points)[3] for g in range(PAIR))
    s_ref[:points], s_ref[points:] = s_lo[...], s_hi[...]
    msg_ref[points:] = taken(s_hi[...], bnd_hi)
    nr_ref[...] = old_nr[...]
    for g in range(PAIR):
        at = g * points
        cap = vectors(small_ref, g, points)[1]
        nr_ref[at : at + 1] = old_nr[at : at + 1] + cap * halo_ref[4 * g : 4 * g + 1]

    @pl.when(in_first_pair())
    def _():
        c_lo = mapped_each(d_lo, nr_ref[:points])
        linked = mapped(maps_ref[4], taken(s_lo[...], bnd_lo))
        c_hi = mapped_each(
            d_hi, nr_ref[points:] + linked + mapped(maps_ref[5], taken(c_lo, bnd_lo))
        )
        c_ref[:points], c_ref[points:] = c_lo, c_hi
        msg_ref[:points] = taken(c_hi, bnd_hi)

    @pl.when(jnp.logical_not(in_first_pair()))
    def _():
        c_ref[...] = jnp.zeros(c_ref.shape, F32)
        msg_ref[:points] = jnp.zeros((points, c_ref.shape[1]), F32)


def second_kernel(
    got_ref, s_ref, nr_ref, c_ref, small_ref, maps_ref, d_lo, d_hi, ss_ref, new_c_ref, f_ref
):
    points, width = got_ref.shape[0] // 2, got_ref.shape[1]
    second_pair = lax.axis_index("dom") >= PAIR

    @pl.when(second_pair)
    def _():
        bnd_lo = vectors(small_ref, 0, points)[3]
        c_lo = corrected(
            nr_ref[:points], got_ref[:points], got_ref[points:], d_lo, maps_ref[2], maps_ref[1]
        )
        new_c_ref[:points] = c_lo
        c_hi = pair_corrected(
            nr_ref[points:], s_ref[:points], c_lo, bnd_lo, d_hi, maps_ref[5], maps_ref[4]
        )
        new_c_ref[points:] = c_hi
        for g, c in enumerate((c_lo, c_hi)):
            whole = mapped_sum(ss_ref[g * points : (g + 1) * points], c)
            f_ref[8 * g : 8 * g + 8] = jnp.broadcast_to(whole, (8, width))

    @pl.when(jnp.logical_not(second_pair))
    def _():
        new_c_ref[...] = c_ref[...]
        for g in range(PAIR):
            rows = slice(g * points, (g + 1) * points)
            whole = mapped_sum(ss_ref[rows], c_ref[rows])
            f_ref[8 * g : 8 * g + 8] = jnp.broadcast_to(whole, (8, width))


def tail_kernel(c_ref, ss_ref, tail_ref):
    points, width = c_ref.shape[0] // PAIR, c_ref.shape[1]
    each = mapped_each(ss_ref, c_ref[...])
    for g in range(PAIR):
        total = each[g * points : (g + 1) * points]
        shift = 1
        while shift < points:
            total = total + jnp.concatenate(
                [total[shift:], jnp.zeros((shift, width), F32)], axis=0
            )
            shift *= 2
        at = g * (points + 8)
        tail_ref[at : at + points] = jnp.concatenate(
            [total[1:], jnp.zeros((1, width), F32)], axis=0
        )
        tail_ref[at + points : at + points + 8] = jnp.broadcast_to(total[:1], (8, width))


def is_later(distance):
    return (lax.axis_index("tm") // distance) % 2 == 1


def sections(width):
    return [
        (slice(g * width, (g + 1) * width), slice(8 * g, 8 * g + 8)) for g in range(PAIR)
    ]


def first_maps_kernel(distance, mw_ref, gw_ref, _, tw_ref, a_ref, bw_ref, aw_ref):
    width = mw_ref.shape[1]
    later = is_later(distance)
    eye = identity(width)
    for wide, _ in sections(width):
        mw, gw = mw_ref[wide], gw_ref[wide]
        a = jnp.where(later, mw, gw)
        tw_ref[wide] = times(a, jnp.where(later, gw, mw))
        a_ref[wide] = split_cols(a)
        bw_ref[wide] = jnp.where(later, gw, eye)
        aw_ref[wide] = jnp.where(later, eye, gw)


def next_maps_kernel(
    distance, mw_ref, gw_ref, bw_ref, aw_ref, _, tw_ref, a_ref, x_ref, nbw_ref, naw_ref
):
    width = mw_ref.shape[1]
    later = is_later(distance)
    for wide, _ in sections(width):
        mw, gw, bw, aw = mw_ref[wide], gw_ref[wide], bw_ref[wide], aw_ref[wide]
        a = jnp.where(later, mw, gw)
        tw_ref[wide] = times(a, jnp.where(later, gw, mw))
        a_ref[wide] = split_cols(a)
        x = jnp.where(later, bw, gw)
        joined = times(x, jnp.where(later, gw, aw))
        x_ref[wide] = split_cols(x)
        nbw_ref[wide] = jnp.where(later, joined, bw)
        naw_ref[wide] = jnp.where(later, aw, joined)


def first_sums_kernel(distance, mf_ref, gf_ref, a_ref, _, __, tf_ref, bf_ref, af_ref):
    later = is_later(distance)
    for wide, short in sections(a_ref.shape[0] // PAIR):
        mf, gf = mf_ref[short], gf_ref[short]
        tf_ref[short] = mapped(a_ref[wide], jnp.where(later, gf, mf)) + jnp.where(later, mf, gf)
        bf_ref[short] = jnp.where(later, gf, 0.0)
        af_ref[short] = jnp.where(later, 0.0, gf)


def next_sums_kernel(
    distance, mf_ref, gf_ref, bf_ref, af_ref, a_ref, x_ref, _, tf_ref, nbf_ref, naf_ref
):
    later = is_later(distance)
    for wide, short in sections(a_ref.shape[0] // PAIR):
        mf, gf, bf, af = mf_ref[short], gf_ref[short], bf_ref[short], af_ref[short]
        tf_ref[short] = mapped(a_ref[wide], jnp.where(later, gf, mf)) + jnp.where(later, mf, gf)
        sums = mapped(x_ref[wide], jnp.where(later, gf, af)) + jnp.where(later, bf, gf)
        nbf_ref[short] = jnp.where(later, sums, bf)
        naf_ref[short] = jnp.where(later, af, sums)


def local_kernel(c_ref, l_lo, l_hi, tail_ref, aw_ref, af_ref, s_ref, base_ref, v_ref):
    points, width = s_ref.shape[0] // PAIR, s_ref.shape[1]
    for g, (wide, short) in enumerate(sections(width)):
        rows = slice(g * points, (g + 1) * points)
        long = slice(g * (points + 8), (g + 1) * (points + 8))
        scan = scanned_split if g else scanned
        base_ref[rows] = s_ref[rows] + scan(c_ref[rows], (l_lo, l_hi)[g])
        v_ref[long] = mapped(split_cols(aw_ref[wide]), tail_ref[long]) + af_ref[short][:1]


def turn_kernel(
    v_ref, gw_ref, gf_ref, bw_ref, bf_ref, p_lo, p_hi, base_ref, halo_ref, small_ref, maps_ref,
    d_lo, d_hi, s_ref, nr_ref, c_ref, msg_ref,
):
    points, width = s_ref.shape[0] // PAIR, s_ref.shape[1]
    came = []
    for g, (wide, short) in enumerate(sections(width)):
        long = slice(g * (points + 8), (g + 1) * (points + 8))
        v = mapped(split_cols(gw_ref[wide]), v_ref[long]) + gf_ref[short][:1]
        came.append(mapped(split_cols(bw_ref[wide]), v) + bf_ref[short][:1])
    moved = [
        mapped_each(p_lo, came[0][:points]),
        mapped_each_split(p_hi[...], came[1][:points]),
    ]
    s = base_ref[...] + jnp.concatenate(moved, axis=0)
    s_ref[...] = s
    correct_both(
        s[:points], s[points:],
        halo_ref[:1] + came[0][points : points + 1],
        halo_ref[4:5] + came[1][points : points + 1],
        small_ref, maps_ref, d_lo, d_hi, nr_ref, c_ref, msg_ref,
    )


def scan_kernel(c_ref, l_lo, l_hi, s_ref, base_ref):
    points = s_ref.shape[0] // PAIR
    for g, (scan, l_ref) in enumerate(((scanned, l_lo), (scanned_split, l_hi))):
        rows = slice(g * points, (g + 1) * points)
        base_ref[rows] = s_ref[rows] + scan(c_ref[rows], l_ref)


def last_local_kernel(
    tail_ref, aw_ref, af_ref, gw_ref, bw_ref, bf_ref, p_lo, p_hi, old_ref, base_ref
):
    points, width = old_ref.shape[0] // PAIR, old_ref.shape[1]
    came = []
    for g, (wide, short) in enumerate(sections(width)):
        at = g * (points + 8)
        v = mapped(split_cols(aw_ref[wide]), tail_ref[at : at + points]) + af_ref[short][:1]
        v = mapped(split_cols(gw_ref[wide]), v)
        came.append(mapped(split_cols(bw_ref[wide]), v) + bf_ref[short][:1])
    for g in range(PAIR):
        rows = slice(g * points, (g + 1) * points)
        moved = mapped_each_split(p_hi[...], came[g]) if g else mapped_each(p_lo, came[g])
        base_ref[rows] = old_ref[rows] + moved


def end_kernel(gf_ref, bw_ref, p_lo, p_hi, base_ref, s_ref):
    points, width = s_ref.shape[0] // PAIR, s_ref.shape[1]
    for g, (wide, short) in enumerate(sections(width)):
        rows = slice(g * points, (g + 1) * points)
        v = mapped(split_cols(bw_ref[wide]), gf_ref[short])
        if g:
            both = dot_nt(split_rows(v), p_hi[...])
            both = both[:1] + both[8:9]
            moved = [both[:, i * width : (i + 1) * width] for i in range(points)]
            moved = jnp.concatenate(moved, axis=0)
        else:
            moved = mapped_each(p_lo, jnp.broadcast_to(v[:1], (points, width)))
        s_ref[rows] = base_ref[rows] + moved


def choose_kernel(both_ref, got_ref, s_ref):
    points = s_ref.shape[0]
    odd = lax.axis_index("dom") % 2 == 1
    s_ref[...] = jnp.where(odd, both_ref[points:], got_ref[:points])


def exchanged(value, distance):
    return lax.ppermute(
        value, "tm", [(i, i ^ distance) for i in range(lax.axis_size("tm"))]
    )


def swapped(value, distance):
    return lax.ppermute(value, "dom", [(i, i ^ distance) for i in range(lax.axis_size("dom"))])


def both_partitions(
    s, nr, c, msg, halo, small, maps, d_lo, d_hi, r_lo, r_hi, w
):
    points, width = s.shape[0] // PAIR, s.shape[1]
    vec, square = ((PAIR * points, width), F32), ((PAIR * width, width), F32)
    square_split = ((PAIR * width, 2 * width), BF16)
    eight = ((PAIR * 8, width), F32)
    longer = ((PAIR * (points + 8), width), F32)
    many = ((PAIR * points, width, width), F32)
    steps = (points.bit_length() - 1) * points // 2
    distances = [2**k for k in range(lax.axis_size("tm").bit_length() - 1)]

    def sums_level(level, f, bf, af, beside):
        got = exchanged(f, distances[level])
        if level == 0:
            return call(
                functools.partial(first_sums_kernel, distances[0]), [eight] * 3,
                f, got, *kept[0], *beside,
            )
        return call(
            functools.partial(next_sums_kernel, distances[level]), [eight] * 3,
            f, got, bf, af, *kept[level], beside[1],
            cost=pl.CostEstimate(flops=2**33, bytes_accessed=2**25, transcendentals=0),
        )

    got = swapped(msg, 2)
    got_w = exchanged(w, distances[0])
    ss, d_lo, d_hi = call(
        suffix_kernel, [many] + [((points, width, width), F32)] * 2, r_lo, r_hi, d_lo, d_hi,
        in_hbm=2, scratch=[pltpu.SemaphoreType.DMA((2,))],
    )
    p_lo, l_lo, p_hi, l_hi = call(
        prefix_kernel,
        [((points, width, width), F32), ((steps, width, width), F32)]
        + [((points * width, 2 * width), BF16), ((steps * width, 2 * width), BF16)],
        r_lo, r_hi,
    )
    c, f = call(
        second_kernel, [vec, eight], got, s, nr, c, small, maps, d_lo, d_hi, ss
    )
    (tail,) = call(tail_kernel, [longer], c, ss)
    kept, bf, af = [], None, None
    for level, distance in enumerate(distances[:-1]):
        if level == 0:
            w, a, bw, aw = call(
                functools.partial(first_maps_kernel, distance),
                [square, square_split, square, square], w, got_w, f,
            )
            kept.append((a,))
        else:
            w, a, x, bw, aw = call(
                functools.partial(next_maps_kernel, distance),
                [square, square_split, square_split, square, square], w, got_w, bw, aw, f,
            )
            kept.append((a, x))
        got_w = exchanged(w, distances[level + 1])
        f, bf, af = sums_level(level, f, bf, af, (p_lo, p_hi))
    got, last = exchanged(f, distances[-1]), got_w
    base, v = call(local_kernel, [vec, longer], c, l_lo, l_hi, tail, aw, af, s)
    s, nr, c, msg = call(
        turn_kernel, [vec] * 4,
        v, last, got, bw, bf, p_lo, p_hi, base, halo, small, maps, d_lo, d_hi,
    )
    got = swapped(msg, 2)
    c, f = call(
        second_kernel, [vec, eight], got, s, nr, c, small, maps, d_lo, d_hi, ss
    )
    (tail,) = call(tail_kernel, [longer], c, ss)
    (base,) = call(scan_kernel, [vec], c, l_lo, l_hi, s)
    for level in range(len(distances) - 1):
        f, bf, af = sums_level(level, f, bf, af, (tail, base))
    got = exchanged(f, distances[-1])
    (base,) = call(last_local_kernel, [vec], tail, aw, af, last, bw, bf, p_lo, p_hi, base)
    return call(end_kernel, [vec], got, bw, p_lo, p_hi, base)[0]


def per_device(
    starting_voltage_guess,
    injected_amperes,
    capacitance,
    conductance,
    block_pattern,
    device_gain,
    link_weight,
    boundary_vertex_list,
    diagonal_reciprocals,
    boundary_jacobian,
    transfer,
):
    points, _, width = starting_voltage_guess.shape
    segments = lax.axis_size("tm")
    (one,) = call(
        ones_kernel, [((1, width), F32)],
        cost=pl.CostEstimate(flops=2**33, bytes_accessed=2**25, transcendentals=0),
    )
    mask = jnp.broadcast_to(block_pattern[0].astype(F32), (1, width))
    s = starting_voltage_guess[:, 0]
    near_s = swapped(starting_voltage_guess, 1)[:, 0]
    d, r, near_s, mask, one = lax.optimization_barrier(
        (diagonal_reciprocals, transfer, near_s, mask, one)
    )
    d, near_d = d[:, 0, 0], swapped(d, 1)[:, 0, 0]
    r, near_r = r[:, 0, 0], swapped(r, 1)[:, 0, 0]
    (rows,) = call(halo_kernel, [((8, width), F32)], s, near_s)
    halo = lax.ppermute(rows, "tm", [(i, (i + 1) % segments) for i in range(segments)])
    (pack,) = call(
        pack_kernel, [((3 * width + points + 24, width), F32)],
        one, conductance[0], mask, link_weight[0], boundary_jacobian[0],
        injected_amperes[:, 0], capacitance, device_gain, boundary_vertex_list,
    )
    near_pack = swapped(pack, 1)
    vec = ((PAIR * points, width), F32)
    (w,) = call(
        whole_kernel, [((PAIR * width, width), F32)], near_r, r, in_hbm=2,
        scratch=[pltpu.VMEM((points, width, width), F32)] * 2 + [pltpu.SemaphoreType.DMA((2,))],
    )
    maps, small, nr = call(
        early_kernel,
        [((6, width, 2 * width), BF16), ((PAIR * (points + 24), width), F32), vec],
        near_s, s, near_pack, pack, w,
    )
    d_lo, d_hi = call(
        diagonal_kernel, [((points, width, width), F32)] * 2, nr, near_d, d,
        in_hbm=2, scratch=[pltpu.SemaphoreType.DMA((2,))],
    )
    s, nr, c, msg = call(
        first_kernel, [vec] * 4, halo, near_s, s, small, maps, d_lo, d_hi, nr
    )
    odd = lax.axis_index("dom") % 2 == 1
    both = lax.cond(
        odd,
        both_partitions,
        lambda s, *rest: s,
        s, nr, c, msg, halo, small, maps, near_d, d, near_r, r, w,
    )
    (s,) = call(choose_kernel, [((points, width), F32)], both, swapped(both, 1))
    return s[:, None]


def solution(mesh):
    in_specs = (
        P("tm", "dom", None),
        P("tm", "dom", None),
        P("dom", None),
        P("dom", None, None),
        P("dom", None, None),
        P("dom", None),
        P("dom", None, None),
        P("dom", None),
        P("tm", "dom", None, None, None),
        P("dom", None, None),
        P("tm", "dom", None, None, None),
    )
    out_specs = P("tm", "dom", None)
    return jax.shard_map(
        per_device, mesh=mesh, in_specs=in_specs, out_specs=out_specs, check_vma=False
    )
```

```python
import functools

import jax
import jax.numpy as jnp
from jax import lax
from jax.experimental import pallas as pl
from jax.experimental.pallas import tpu as pltpu
from jax.sharding import PartitionSpec as P

F32 = jnp.float32
BF16 = jnp.bfloat16
PAIR = 2


def halves(x):
    hi = x.astype(BF16)
    return hi, (x - hi.astype(F32)).astype(BF16)


def split_cols(matrix):
    return jnp.concatenate(halves(matrix), axis=1)


def split_rows(vectors):
    hi, lo = halves(vectors)
    hi, lo = hi.astype(F32), lo.astype(F32)
    top = jnp.concatenate([hi, hi], axis=1)
    low = jnp.concatenate([lo, jnp.zeros_like(lo)], axis=1)
    return jnp.concatenate([top, low], axis=0).astype(BF16)


def dot_nt(a, b):
    return lax.dot_general(a, b, (((1,), (1,)), ((), ())), preferred_element_type=F32)


def times(a, b):
    ah, al = halves(a)
    bh, bl = halves(b)
    left = jnp.concatenate([ah, al, ah], axis=1)
    right = jnp.concatenate([bh, bh, bl], axis=0)
    return jnp.dot(left, right, preferred_element_type=F32)


def mapped(matrix_split, vectors):
    count = vectors.shape[0]
    both = dot_nt(split_rows(vectors), matrix_split)
    return both[:count] + both[count:]


def mapped_each(matrices, vectors):
    rows = []
    for r in range(vectors.shape[0]):
        products = matrices[r] * vectors[r : r + 1, :]
        rows.append(jnp.sum(products.T, axis=0, keepdims=True))
    return jnp.concatenate(rows, axis=0)


def mapped_each_split(matrices_split, vectors):
    count, width = vectors.shape
    both = dot_nt(split_rows(vectors), matrices_split)
    row = lax.broadcasted_iota(jnp.int32, (2 * count, width), 0) % count
    picked = [
        jnp.where(row == r, both[:, r * width : (r + 1) * width], 0.0) for r in range(count)
    ]
    while len(picked) > 1:
        picked = [a + b for a, b in zip(picked[::2], picked[1::2])]
    return picked[0][:count] + picked[0][count:]


def mapped_sum(matrices, vectors):
    products = matrices[0] * vectors[:1, :]
    for r in range(1, vectors.shape[0]):
        products = products + matrices[r] * vectors[r : r + 1, :]
    return jnp.sum(products.T, axis=0, keepdims=True)


def call(kernel, outs, *args, cost=None, in_hbm=0, scratch=()):
    vmem = pl.BlockSpec(memory_space=pltpu.VMEM)
    return pl.pallas_call(
        kernel,
        out_shape=[jax.ShapeDtypeStruct(s, d) for s, d in outs],
        in_specs=[vmem] * (len(args) - in_hbm) + [pl.BlockSpec(memory_space=pltpu.HBM)] * in_hbm,
        out_specs=[vmem] * len(outs),
        scratch_shapes=list(scratch),
        cost_estimate=cost,
        compiler_params=pltpu.CompilerParams(vmem_limit_bytes=24 * 2**20),
    )(*args)


def identity(width):
    return (
        lax.broadcasted_iota(jnp.int32, (width, width), 0)
        == lax.broadcasted_iota(jnp.int32, (width, width), 1)
    ).astype(F32)


def halo_kernel(s_ref, near_ref, msg_ref):
    points, width = s_ref.shape
    msg_ref[:4] = jnp.broadcast_to(near_ref[points - 1 :], (4, width))
    msg_ref[4:] = jnp.broadcast_to(s_ref[points - 1 :], (4, width))


def ones_kernel(one_ref):
    one_ref[...] = jnp.ones(one_ref.shape, F32)


def pack_kernel(one_ref, g_ref, mask_ref, k_ref, j_ref, inj_ref, cap_ref, gain_ref, bnd_ref, pack_ref):
    points, width = inj_ref.shape
    pack_ref[:width] = g_ref[...] * (mask_ref[...] * one_ref[...])
    pack_ref[width : 2 * width] = k_ref[...]
    pack_ref[2 * width : 3 * width] = j_ref[...]
    at = 3 * width
    pack_ref[at : at + points] = inj_ref[...]
    at += points
    for one in (cap_ref[...], gain_ref[...], bnd_ref[...].astype(F32)):
        pack_ref[at : at + 8] = jnp.broadcast_to(one, (8, width))
        at += 8


def vectors(small_ref, g, points):
    at = g * (points + 24)
    inj = small_ref[at : at + points]
    at += points
    cap, gain, bnd = (small_ref[at + 8 * i : at + 8 * i + 1] for i in range(3))
    return inj, cap, gain, bnd.astype(jnp.int32)


def fetched(sources, targets, sems):
    moves = [
        pltpu.make_async_copy(source, target, sems.at[i])
        for i, (source, target) in enumerate(zip(sources, targets))
    ]
    for move in moves:
        move.start()
    return moves


def whole_kernel(lo_ref, hi_ref, diag_ref, w_ref, d_hi, r_lo, r_hi, sems):
    points, width = lo_ref.shape[0], lo_ref.shape[1]
    moves = fetched((lo_ref, hi_ref, diag_ref), (r_lo, r_hi, d_hi), sems)
    u = []
    for move, r_ref in zip(moves, (r_lo, r_hi)):
        move.wait()
        u += [times(r_ref[i + 1], r_ref[i]) for i in range(0, points, 2)]
    while len(u) > PAIR:
        u = [times(u[i + 1], u[i]) for i in range(0, len(u), 2)]
    for g in range(PAIR):
        w_ref[g * width : (g + 1) * width] = u[g]
    moves[-1].wait()


def suffix_kernel(r_lo, r_hi, lo_ref, hi_ref, s_ref, d_lo, d_hi, sems):
    points, width = r_lo.shape[0], r_lo.shape[1]
    moves = fetched((lo_ref, hi_ref), (d_lo, d_hi), sems)
    both = [[r_ref[i] for i in range(points)] for r_ref in (r_lo, r_hi)]
    span = 1
    while span < points:
        for base in range(0, points, 2 * span):
            first = max(base, 1)
            if first == base + span:
                continue
            for u in both:
                prod = times(u[base + span], jnp.concatenate(u[first : base + span], axis=1))
                for i in range(first, base + span):
                    at = (i - first) * width
                    u[i] = prod[:, at : at + width]
        span *= 2
    for g, u in enumerate(both):
        for i in range(points - 1):
            s_ref[g * points + i] = u[i + 1]
        s_ref[(g + 1) * points - 1] = identity(width)
    for move in moves:
        move.wait()


def prefix_kernel(r_lo, r_hi, p_lo, l_lo, p_hi, l_hi):
    points, width = r_lo.shape[0], r_lo.shape[1]
    both = [[r_ref[i] for i in range(points)] for r_ref in (r_lo, r_hi)]
    span, slot = 1, 0
    while span < points:
        for base in range(0, points, 2 * span):
            for q, l_ref in zip(both, (l_lo, l_hi)):
                upper = q[base + span : base + 2 * span]
                for i, matrix in enumerate(upper):
                    if l_ref is l_hi:
                        at = (slot + i) * width
                        l_ref[at : at + width] = split_cols(matrix)
                    else:
                        l_ref[slot + i] = matrix
                prod = times(jnp.concatenate(upper, axis=0), q[base + span - 1])
                for i in range(span):
                    q[base + span + i] = prod[i * width : (i + 1) * width]
            slot += span
        span *= 2
    for i in range(points):
        p_lo[i] = both[0][i]
        p_hi[i * width : (i + 1) * width] = split_cols(both[1][i])


def scanned(c, l_ref):
    points = c.shape[0]
    x = [c[i : i + 1, :] for i in range(points)]
    span, slot = 1, 0
    while span < points:
        for base in range(0, points, 2 * span):
            head = x[base + span - 1]
            for i in range(base + span, base + 2 * span):
                x[i] = x[i] + mapped_each(l_ref[slot : slot + 1], head)
                slot += 1
        span *= 2
    return jnp.concatenate(x, axis=0)


def scanned_split(c, l_ref):
    points, width = c.shape
    half = points // 2
    x = [c[i : i + 1, :] for i in range(points)]
    span, level = 1, 0
    while span < points:
        later = [i for i in range(points) if i & span]
        heads = jnp.concatenate([x[(i & ~(2 * span - 1)) + span - 1] for i in later], axis=0)
        rows = slice(level * half * width, (level + 1) * half * width)
        moved = mapped_each_split(l_ref[rows], heads)
        for slot, i in enumerate(later):
            x[i] = x[i] + moved[slot : slot + 1]
        span *= 2
        level += 1
    return jnp.concatenate(x, axis=0)


def taken(rows, lanes):
    return jnp.take_along_axis(rows, jnp.broadcast_to(lanes, rows.shape), axis=1)


def negative_residual(s, halo, inj, cap, gain, gs):
    before = jnp.concatenate([halo, s[: s.shape[0] - 1]], axis=0)
    return inj - cap * (s - before) - mapped(gs, s) - gain * jnp.tanh(s)


def corrected(nr, c_before, s_before, d_ref, js, ks):
    return mapped_each(d_ref, nr + mapped(js, c_before) + mapped(ks, s_before))


def pair_corrected(nr, s_lo, c_lo, bnd_lo, d_hi_ref, js, ks):
    return corrected(nr, taken(c_lo, bnd_lo), taken(s_lo, bnd_lo), d_hi_ref, js, ks)


def correct_both(
    s_lo, s_hi, halo_lo, halo_hi, small_ref, maps_ref, d_lo, d_hi, nr_ref, c_ref, msg_ref
):
    lo_maps, hi_maps = [maps_ref[i] for i in range(3)], [maps_ref[i] for i in range(3, 6)]
    points = s_lo.shape[0]
    inj_lo, cap_lo, gain_lo, bnd_lo = vectors(small_ref, 0, points)
    inj_hi, cap_hi, gain_hi, bnd_hi = vectors(small_ref, 1, points)
    nr_lo = negative_residual(s_lo, halo_lo, inj_lo, cap_lo, gain_lo, lo_maps[0])
    nr_hi = negative_residual(s_hi, halo_hi, inj_hi, cap_hi, gain_hi, hi_maps[0])
    nr_ref[:points], nr_ref[points:] = nr_lo, nr_hi
    msg_ref[points:] = taken(s_hi, bnd_hi)

    @pl.when(in_first_pair())
    def _():
        c_lo = mapped_each(d_lo, nr_lo)
        c_hi = pair_corrected(nr_hi, s_lo, c_lo, bnd_lo, d_hi, hi_maps[2], hi_maps[1])
        c_ref[:points], c_ref[points:] = c_lo, c_hi
        msg_ref[:points] = taken(c_hi, bnd_hi)

    @pl.when(jnp.logical_not(in_first_pair()))
    def _():
        c_ref[...] = jnp.zeros(c_ref.shape, F32)
        msg_ref[:points] = jnp.zeros((points, c_ref.shape[1]), F32)


def early_kernel(s_lo, s_hi, pack_lo, pack_hi, _, maps_ref, small_ref, nr_ref):
    points, width = s_lo.shape
    for i in range(3):
        rows = slice(i * width, (i + 1) * width)
        maps_ref[i] = split_cols(pack_lo[rows])
        maps_ref[3 + i] = split_cols(pack_hi[rows])
    none = jnp.zeros((1, width), F32)
    for g, (s_ref, pack) in enumerate(((s_lo, pack_lo), (s_hi, pack_hi))):
        at = g * (points + 24)
        small_ref[at : at + points + 24] = pack[3 * width :]
        inj, cap, gain, _ = vectors(small_ref, g, points)
        nr_ref[g * points : (g + 1) * points] = negative_residual(
            s_ref[...], none, inj, cap, gain, maps_ref[3 * g]
        )


def diagonal_kernel(_, lo_ref, d_lo, sems):
    for move in fetched((lo_ref,), (d_lo,), sems):
        move.wait()


def in_first_pair():
    return lax.axis_index("dom") < PAIR


def first_kernel(
    halo_ref, s_lo, s_hi, small_ref, maps_ref, d_lo, d_hi, old_nr, s_ref, nr_ref, c_ref, msg_ref
):
    points = s_lo.shape[0]
    bnd_lo, bnd_hi = (vectors(small_ref, g, points)[3] for g in range(PAIR))
    s_ref[:points], s_ref[points:] = s_lo[...], s_hi[...]
    msg_ref[points:] = taken(s_hi[...], bnd_hi)
    nr_ref[...] = old_nr[...]
    for g in range(PAIR):
        at = g * points
        cap = vectors(small_ref, g, points)[1]
        nr_ref[at : at + 1] = old_nr[at : at + 1] + cap * halo_ref[4 * g : 4 * g + 1]

    @pl.when(in_first_pair())
    def _():
        c_lo = mapped_each(d_lo, nr_ref[:points])
        linked = mapped(maps_ref[4], taken(s_lo[...], bnd_lo))
        c_hi = mapped_each(
            d_hi, nr_ref[points:] + linked + mapped(maps_ref[5], taken(c_lo, bnd_lo))
        )
        c_ref[:points], c_ref[points:] = c_lo, c_hi
        msg_ref[:points] = taken(c_hi, bnd_hi)

    @pl.when(jnp.logical_not(in_first_pair()))
    def _():
        c_ref[...] = jnp.zeros(c_ref.shape, F32)
        msg_ref[:points] = jnp.zeros((points, c_ref.shape[1]), F32)


def second_kernel(
    got_ref, s_ref, nr_ref, c_ref, small_ref, maps_ref, d_lo, d_hi, ss_ref, new_c_ref, f_ref
):
    points, width = got_ref.shape[0] // 2, got_ref.shape[1]
    second_pair = lax.axis_index("dom") >= PAIR

    @pl.when(second_pair)
    def _():
        bnd_lo = vectors(small_ref, 0, points)[3]
        c_lo = corrected(
            nr_ref[:points], got_ref[:points], got_ref[points:], d_lo, maps_ref[2], maps_ref[1]
        )
        new_c_ref[:points] = c_lo
        c_hi = pair_corrected(
            nr_ref[points:], s_ref[:points], c_lo, bnd_lo, d_hi, maps_ref[5], maps_ref[4]
        )
        new_c_ref[points:] = c_hi
        for g, c in enumerate((c_lo, c_hi)):
            whole = mapped_sum(ss_ref[g * points : (g + 1) * points], c)
            f_ref[8 * g : 8 * g + 8] = jnp.broadcast_to(whole, (8, width))

    @pl.when(jnp.logical_not(second_pair))
    def _():
        new_c_ref[...] = c_ref[...]
        for g in range(PAIR):
            rows = slice(g * points, (g + 1) * points)
            whole = mapped_sum(ss_ref[rows], c_ref[rows])
            f_ref[8 * g : 8 * g + 8] = jnp.broadcast_to(whole, (8, width))


def tail_kernel(c_ref, ss_ref, tail_ref):
    points, width = c_ref.shape[0] // PAIR, c_ref.shape[1]
    each = mapped_each(ss_ref, c_ref[...])
    for g in range(PAIR):
        total = each[g * points : (g + 1) * points]
        shift = 1
        while shift < points:
            total = total + jnp.concatenate(
                [total[shift:], jnp.zeros((shift, width), F32)], axis=0
            )
            shift *= 2
        at = g * (points + 8)
        tail_ref[at : at + points] = jnp.concatenate(
            [total[1:], jnp.zeros((1, width), F32)], axis=0
        )
        tail_ref[at + points : at + points + 8] = jnp.broadcast_to(total[:1], (8, width))


def is_later(distance):
    return (lax.axis_index("tm") // distance) % 2 == 1


def sections(width):
    return [
        (slice(g * width, (g + 1) * width), slice(8 * g, 8 * g + 8)) for g in range(PAIR)
    ]


def first_maps_kernel(distance, mw_ref, gw_ref, _, tw_ref, a_ref, bw_ref, aw_ref):
    width = mw_ref.shape[1]
    later = is_later(distance)
    eye = identity(width)
    for wide, _ in sections(width):
        mw, gw = mw_ref[wide], gw_ref[wide]
        a = jnp.where(later, mw, gw)
        tw_ref[wide] = times(a, jnp.where(later, gw, mw))
        a_ref[wide] = split_cols(a)
        bw_ref[wide] = jnp.where(later, gw, eye)
        aw_ref[wide] = jnp.where(later, eye, gw)


def next_maps_kernel(
    distance, mw_ref, gw_ref, bw_ref, aw_ref, _, tw_ref, a_ref, x_ref, nbw_ref, naw_ref
):
    width = mw_ref.shape[1]
    later = is_later(distance)
    for wide, _ in sections(width):
        mw, gw, bw, aw = mw_ref[wide], gw_ref[wide], bw_ref[wide], aw_ref[wide]
        a = jnp.where(later, mw, gw)
        tw_ref[wide] = times(a, jnp.where(later, gw, mw))
        a_ref[wide] = split_cols(a)
        x = jnp.where(later, bw, gw)
        joined = times(x, jnp.where(later, gw, aw))
        x_ref[wide] = split_cols(x)
        nbw_ref[wide] = jnp.where(later, joined, bw)
        naw_ref[wide] = jnp.where(later, aw, joined)


def first_sums_kernel(distance, mf_ref, gf_ref, a_ref, _, __, tf_ref, bf_ref, af_ref):
    later = is_later(distance)
    for wide, short in sections(a_ref.shape[0] // PAIR):
        mf, gf = mf_ref[short], gf_ref[short]
        tf_ref[short] = mapped(a_ref[wide], jnp.where(later, gf, mf)) + jnp.where(later, mf, gf)
        bf_ref[short] = jnp.where(later, gf, 0.0)
        af_ref[short] = jnp.where(later, 0.0, gf)


def next_sums_kernel(
    distance, mf_ref, gf_ref, bf_ref, af_ref, a_ref, x_ref, _, tf_ref, nbf_ref, naf_ref
):
    later = is_later(distance)
    for wide, short in sections(a_ref.shape[0] // PAIR):
        mf, gf, bf, af = mf_ref[short], gf_ref[short], bf_ref[short], af_ref[short]
        tf_ref[short] = mapped(a_ref[wide], jnp.where(later, gf, mf)) + jnp.where(later, mf, gf)
        sums = mapped(x_ref[wide], jnp.where(later, gf, af)) + jnp.where(later, bf, gf)
        nbf_ref[short] = jnp.where(later, sums, bf)
        naf_ref[short] = jnp.where(later, af, sums)


def local_kernel(c_ref, l_lo, l_hi, tail_ref, aw_ref, af_ref, s_ref, base_ref, v_ref):
    points, width = s_ref.shape[0] // PAIR, s_ref.shape[1]
    for g, (wide, short) in enumerate(sections(width)):
        rows = slice(g * points, (g + 1) * points)
        long = slice(g * (points + 8), (g + 1) * (points + 8))
        scan = scanned_split if g else scanned
        base_ref[rows] = s_ref[rows] + scan(c_ref[rows], (l_lo, l_hi)[g])
        v_ref[long] = mapped(split_cols(aw_ref[wide]), tail_ref[long]) + af_ref[short][:1]


def turn_kernel(
    v_ref, gw_ref, gf_ref, bw_ref, bf_ref, p_lo, p_hi, base_ref, halo_ref, small_ref, maps_ref,
    d_lo, d_hi, s_ref, nr_ref, c_ref, msg_ref,
):
    points, width = s_ref.shape[0] // PAIR, s_ref.shape[1]
    came = []
    for g, (wide, short) in enumerate(sections(width)):
        long = slice(g * (points + 8), (g + 1) * (points + 8))
        v = mapped(split_cols(gw_ref[wide]), v_ref[long]) + gf_ref[short][:1]
        came.append(mapped(split_cols(bw_ref[wide]), v) + bf_ref[short][:1])
    moved = [
        mapped_each(p_lo, came[0][:points]),
        mapped_each_split(p_hi[...], came[1][:points]),
    ]
    s = base_ref[...] + jnp.concatenate(moved, axis=0)
    s_ref[...] = s
    correct_both(
        s[:points], s[points:],
        halo_ref[:1] + came[0][points : points + 1],
        halo_ref[4:5] + came[1][points : points + 1],
        small_ref, maps_ref, d_lo, d_hi, nr_ref, c_ref, msg_ref,
    )


def scan_kernel(c_ref, l_lo, l_hi, s_ref, base_ref):
    points = s_ref.shape[0] // PAIR
    for g, (scan, l_ref) in enumerate(((scanned, l_lo), (scanned_split, l_hi))):
        rows = slice(g * points, (g + 1) * points)
        base_ref[rows] = s_ref[rows] + scan(c_ref[rows], l_ref)


def last_local_kernel(
    tail_ref, aw_ref, af_ref, gw_ref, bw_ref, bf_ref, p_lo, p_hi, old_ref, base_ref
):
    points, width = old_ref.shape[0] // PAIR, old_ref.shape[1]
    came = []
    for g, (wide, short) in enumerate(sections(width)):
        at = g * (points + 8)
        v = mapped(split_cols(aw_ref[wide]), tail_ref[at : at + points]) + af_ref[short][:1]
        v = mapped(split_cols(gw_ref[wide]), v)
        came.append(mapped(split_cols(bw_ref[wide]), v) + bf_ref[short][:1])
    for g in range(PAIR):
        rows = slice(g * points, (g + 1) * points)
        moved = mapped_each_split(p_hi[...], came[g]) if g else mapped_each(p_lo, came[g])
        base_ref[rows] = old_ref[rows] + moved


def end_kernel(gf_ref, bw_ref, p_lo, p_hi, base_ref, s_ref):
    points, width = s_ref.shape[0] // PAIR, s_ref.shape[1]
    for g, (wide, short) in enumerate(sections(width)):
        rows = slice(g * points, (g + 1) * points)
        v = mapped(split_cols(bw_ref[wide]), gf_ref[short])
        if g:
            both = dot_nt(split_rows(v), p_hi[...])
            both = both[:1] + both[8:9]
            moved = [both[:, i * width : (i + 1) * width] for i in range(points)]
            moved = jnp.concatenate(moved, axis=0)
        else:
            moved = mapped_each(p_lo, jnp.broadcast_to(v[:1], (points, width)))
        s_ref[rows] = base_ref[rows] + moved


def choose_kernel(both_ref, got_ref, s_ref):
    points = s_ref.shape[0]
    odd = lax.axis_index("dom") % 2 == 1
    s_ref[...] = jnp.where(odd, both_ref[points:], got_ref[:points])


def exchanged(value, distance):
    return lax.ppermute(
        value, "tm", [(i, i ^ distance) for i in range(lax.axis_size("tm"))]
    )


def swapped(value, distance):
    return lax.ppermute(value, "dom", [(i, i ^ distance) for i in range(lax.axis_size("dom"))])


def both_partitions(
    s, nr, c, msg, halo, small, maps, d_lo, d_hi, r_lo, r_hi, w
):
    points, width = s.shape[0] // PAIR, s.shape[1]
    vec, square = ((PAIR * points, width), F32), ((PAIR * width, width), F32)
    square_split = ((PAIR * width, 2 * width), BF16)
    eight = ((PAIR * 8, width), F32)
    longer = ((PAIR * (points + 8), width), F32)
    many = ((PAIR * points, width, width), F32)
    steps = (points.bit_length() - 1) * points // 2
    distances = [2**k for k in range(lax.axis_size("tm").bit_length() - 1)]

    def sums_level(level, f, bf, af, beside):
        got = exchanged(f, distances[level])
        if level == 0:
            return call(
                functools.partial(first_sums_kernel, distances[0]), [eight] * 3,
                f, got, *kept[0], *beside,
            )
        return call(
            functools.partial(next_sums_kernel, distances[level]), [eight] * 3,
            f, got, bf, af, *kept[level], beside[1],
            cost=pl.CostEstimate(flops=2**33, bytes_accessed=2**25, transcendentals=0),
        )

    got = swapped(msg, 2)
    got_w = exchanged(w, distances[0])
    ss, d_lo, d_hi = call(
        suffix_kernel, [many] + [((points, width, width), F32)] * 2, r_lo, r_hi, d_lo, d_hi,
        in_hbm=2, scratch=[pltpu.SemaphoreType.DMA((2,))],
    )
    p_lo, l_lo, p_hi, l_hi = call(
        prefix_kernel,
        [((points, width, width), F32), ((steps, width, width), F32)]
        + [((points * width, 2 * width), BF16), ((steps * width, 2 * width), BF16)],
        r_lo, r_hi,
    )
    c, f = call(
        second_kernel, [vec, eight], got, s, nr, c, small, maps, d_lo, d_hi, ss
    )
    (tail,) = call(tail_kernel, [longer], c, ss)
    kept, bf, af = [], None, None
    for level, distance in enumerate(distances[:-1]):
        if level == 0:
            w, a, bw, aw = call(
                functools.partial(first_maps_kernel, distance),
                [square, square_split, square, square], w, got_w, f,
            )
            kept.append((a,))
        else:
            w, a, x, bw, aw = call(
                functools.partial(next_maps_kernel, distance),
                [square, square_split, square_split, square, square], w, got_w, bw, aw, f,
            )
            kept.append((a, x))
        got_w = exchanged(w, distances[level + 1])
        f, bf, af = sums_level(level, f, bf, af, (p_lo, p_hi))
    got, last = exchanged(f, distances[-1]), got_w
    base, v = call(local_kernel, [vec, longer], c, l_lo, l_hi, tail, aw, af, s)
    s, nr, c, msg = call(
        turn_kernel, [vec] * 4,
        v, last, got, bw, bf, p_lo, p_hi, base, halo, small, maps, d_lo, d_hi,
    )
    got = swapped(msg, 2)
    c, f = call(
        second_kernel, [vec, eight], got, s, nr, c, small, maps, d_lo, d_hi, ss
    )
    (tail,) = call(tail_kernel, [longer], c, ss)
    (base,) = call(scan_kernel, [vec], c, l_lo, l_hi, s)
    for level in range(len(distances) - 1):
        f, bf, af = sums_level(level, f, bf, af, (tail, base))
    got = exchanged(f, distances[-1])
    (base,) = call(last_local_kernel, [vec], tail, aw, af, last, bw, bf, p_lo, p_hi, base)
    return call(end_kernel, [vec], got, bw, p_lo, p_hi, base)[0]


def per_device(
    starting_voltage_guess,
    injected_amperes,
    capacitance,
    conductance,
    block_pattern,
    device_gain,
    link_weight,
    boundary_vertex_list,
    diagonal_reciprocals,
    boundary_jacobian,
    transfer,
):
    points, _, width = starting_voltage_guess.shape
    segments = lax.axis_size("tm")
    (one,) = call(
        ones_kernel, [((1, width), F32)],
        cost=pl.CostEstimate(flops=2**33, bytes_accessed=2**25, transcendentals=0),
    )
    mask = jnp.broadcast_to(block_pattern[0].astype(F32), (1, width))
    s = starting_voltage_guess[:, 0]
    near_s = swapped(starting_voltage_guess, 1)[:, 0]
    d, r, near_s, mask, one = lax.optimization_barrier(
        (diagonal_reciprocals, transfer, near_s, mask, one)
    )
    d, near_d = d[:, 0, 0], swapped(d, 1)[:, 0, 0]
    r, near_r = r[:, 0, 0], swapped(r, 1)[:, 0, 0]
    (rows,) = call(halo_kernel, [((8, width), F32)], s, near_s)
    halo = lax.ppermute(rows, "tm", [(i, (i + 1) % segments) for i in range(segments)])
    (pack,) = call(
        pack_kernel, [((3 * width + points + 24, width), F32)],
        one, conductance[0], mask, link_weight[0], boundary_jacobian[0],
        injected_amperes[:, 0], capacitance, device_gain, boundary_vertex_list,
    )
    near_pack = swapped(pack, 1)
    vec = ((PAIR * points, width), F32)
    w, d_hi = call(
        whole_kernel, [((PAIR * width, width), F32), ((points, width, width), F32)],
        near_r, r, d, in_hbm=3,
        scratch=[pltpu.VMEM((points, width, width), F32)] * 2 + [pltpu.SemaphoreType.DMA((3,))],
    )
    maps, small, nr = call(
        early_kernel,
        [((6, width, 2 * width), BF16), ((PAIR * (points + 24), width), F32), vec],
        near_s, s, near_pack, pack, w,
    )
    (d_lo,) = call(
        diagonal_kernel, [((points, width, width), F32)], nr, near_d,
        in_hbm=1, scratch=[pltpu.SemaphoreType.DMA((1,))],
    )
    s, nr, c, msg = call(
        first_kernel, [vec] * 4, halo, near_s, s, small, maps, d_lo, d_hi, nr
    )
    odd = lax.axis_index("dom") % 2 == 1
    both = lax.cond(
        odd,
        both_partitions,
        lambda s, *rest: s,
        s, nr, c, msg, halo, small, maps, near_d, d, near_r, r, w,
    )
    (s,) = call(choose_kernel, [((points, width), F32)], both, swapped(both, 1))
    return s[:, None]


def solution(mesh):
    in_specs = (
        P("tm", "dom", None),
        P("tm", "dom", None),
        P("dom", None),
        P("dom", None, None),
        P("dom", None, None),
        P("dom", None),
        P("dom", None, None),
        P("dom", None),
        P("tm", "dom", None, None, None),
        P("dom", None, None),
        P("tm", "dom", None, None, None),
    )
    out_specs = P("tm", "dom", None)
    return jax.shard_map(
        per_device, mesh=mesh, in_specs=in_specs, out_specs=out_specs, check_vma=False
    )
```

```python
import functools

import jax
import jax.numpy as jnp
from jax import lax
from jax.experimental import pallas as pl
from jax.experimental.pallas import tpu as pltpu
from jax.sharding import PartitionSpec as P

F32 = jnp.float32
BF16 = jnp.bfloat16
PAIR = 2


def halves(x):
    hi = x.astype(BF16)
    return hi, (x - hi.astype(F32)).astype(BF16)


def split_cols(matrix):
    return jnp.concatenate(halves(matrix), axis=1)


def split_rows(vectors):
    hi, lo = halves(vectors)
    hi, lo = hi.astype(F32), lo.astype(F32)
    top = jnp.concatenate([hi, hi], axis=1)
    low = jnp.concatenate([lo, jnp.zeros_like(lo)], axis=1)
    return jnp.concatenate([top, low], axis=0).astype(BF16)


def dot_nt(a, b):
    return lax.dot_general(a, b, (((1,), (1,)), ((), ())), preferred_element_type=F32)


def times(a, b):
    ah, al = halves(a)
    bh, bl = halves(b)
    left = jnp.concatenate([ah, al, ah], axis=1)
    right = jnp.concatenate([bh, bh, bl], axis=0)
    return jnp.dot(left, right, preferred_element_type=F32)


def mapped(matrix_split, vectors):
    count = vectors.shape[0]
    both = dot_nt(split_rows(vectors), matrix_split)
    return both[:count] + both[count:]


def mapped_each(matrices, vectors):
    if isinstance(matrices, tuple):
        half = vectors.shape[0] // 2
        near = mapped_each(matrices[0], vectors[:half])
        return jnp.concatenate([near, mapped_each_split(matrices[1], vectors[half:])], axis=0)
    rows = []
    for r in range(vectors.shape[0]):
        products = matrices[r] * vectors[r : r + 1, :]
        rows.append(jnp.sum(products.T, axis=0, keepdims=True))
    return jnp.concatenate(rows, axis=0)


def mapped_each_split(matrices_split, vectors):
    count, width = vectors.shape
    both = dot_nt(split_rows(vectors), matrices_split)
    row = lax.broadcasted_iota(jnp.int32, (2 * count, width), 0) % count
    picked = [
        jnp.where(row == r, both[:, r * width : (r + 1) * width], 0.0) for r in range(count)
    ]
    while len(picked) > 1:
        picked = [a + b for a, b in zip(picked[::2], picked[1::2])]
    return picked[0][:count] + picked[0][count:]


def mapped_sum(matrices, vectors):
    products = matrices[0] * vectors[:1, :]
    for r in range(1, vectors.shape[0]):
        products = products + matrices[r] * vectors[r : r + 1, :]
    return jnp.sum(products.T, axis=0, keepdims=True)


def call(kernel, outs, *args, cost=None, in_hbm=0, scratch=()):
    vmem = pl.BlockSpec(memory_space=pltpu.VMEM)
    return pl.pallas_call(
        kernel,
        out_shape=[jax.ShapeDtypeStruct(s, d) for s, d in outs],
        in_specs=[vmem] * (len(args) - in_hbm) + [pl.BlockSpec(memory_space=pltpu.HBM)] * in_hbm,
        out_specs=[vmem] * len(outs),
        scratch_shapes=list(scratch),
        cost_estimate=cost,
        compiler_params=pltpu.CompilerParams(vmem_limit_bytes=24 * 2**20),
    )(*args)


def identity(width):
    return (
        lax.broadcasted_iota(jnp.int32, (width, width), 0)
        == lax.broadcasted_iota(jnp.int32, (width, width), 1)
    ).astype(F32)


def halo_kernel(s_ref, near_ref, msg_ref):
    points, width = s_ref.shape
    msg_ref[:4] = jnp.broadcast_to(near_ref[points - 1 :], (4, width))
    msg_ref[4:] = jnp.broadcast_to(s_ref[points - 1 :], (4, width))


def ones_kernel(one_ref):
    one_ref[...] = jnp.ones(one_ref.shape, F32)


def pack_kernel(one_ref, g_ref, mask_ref, k_ref, j_ref, inj_ref, cap_ref, gain_ref, bnd_ref, pack_ref):
    points, width = inj_ref.shape
    pack_ref[:width] = g_ref[...] * (mask_ref[...] * one_ref[...])
    pack_ref[width : 2 * width] = k_ref[...]
    pack_ref[2 * width : 3 * width] = j_ref[...]
    at = 3 * width
    pack_ref[at : at + points] = inj_ref[...]
    at += points
    for one in (cap_ref[...], gain_ref[...], bnd_ref[...].astype(F32)):
        pack_ref[at : at + 8] = jnp.broadcast_to(one, (8, width))
        at += 8


def vectors(small_ref, g, points):
    at = g * (points + 24)
    inj = small_ref[at : at + points]
    at += points
    cap, gain, bnd = (small_ref[at + 8 * i : at + 8 * i + 1] for i in range(3))
    return inj, cap, gain, bnd.astype(jnp.int32)


def fetched(sources, targets, sems):
    moves = [
        pltpu.make_async_copy(source, target, sems.at[i])
        for i, (source, target) in enumerate(zip(sources, targets))
    ]
    for move in moves:
        move.start()
    return moves


def whole_kernel(lo_ref, hi_ref, diag_ref, w_ref, d_hi, r_lo, r_hi, sems):
    points, width = lo_ref.shape[0], lo_ref.shape[1]
    moves = fetched((lo_ref, hi_ref, diag_ref), (r_lo, r_hi, d_hi), sems)
    u = []
    for move, r_ref in zip(moves, (r_lo, r_hi)):
        move.wait()
        u += [times(r_ref[i + 1], r_ref[i]) for i in range(0, points, 2)]
    while len(u) > PAIR:
        u = [times(u[i + 1], u[i]) for i in range(0, len(u), 2)]
    for g in range(PAIR):
        w_ref[g * width : (g + 1) * width] = u[g]
    moves[-1].wait()


def suffix_kernel(r_lo, r_hi, lo_ref, hi_ref, s_ref, d_lo, d_hi, sems):
    points, width = r_lo.shape[0], r_lo.shape[1]
    moves = fetched((lo_ref, hi_ref), (d_lo, d_hi), sems)
    both = [[r_ref[i] for i in range(points)] for r_ref in (r_lo, r_hi)]
    span = 1
    while span < points:
        for base in range(0, points, 2 * span):
            first = max(base, 1)
            if first == base + span:
                continue
            for u in both:
                prod = times(u[base + span], jnp.concatenate(u[first : base + span], axis=1))
                for i in range(first, base + span):
                    at = (i - first) * width
                    u[i] = prod[:, at : at + width]
        span *= 2
    for g, u in enumerate(both):
        for i in range(points - 1):
            s_ref[g * points + i] = u[i + 1]
        s_ref[(g + 1) * points - 1] = identity(width)
    for move in moves:
        move.wait()


def prefix_kernel(r_lo, r_hi, d_lo, d_hi, p_lo, l_lo, p_hi, l_hi, ds_lo, ds_hi):
    points, width = r_lo.shape[0], r_lo.shape[1]
    both = [[r_ref[i] for i in range(points)] for r_ref in (r_lo, r_hi)]
    span, slot = 1, 0
    while span < points:
        for base in range(0, points, 2 * span):
            for q, l_ref in zip(both, (l_lo, l_hi)):
                upper = q[base + span : base + 2 * span]
                for i, matrix in enumerate(upper):
                    if l_ref is l_hi:
                        at = (slot + i) * width
                        l_ref[at : at + width] = split_cols(matrix)
                    else:
                        l_ref[slot + i] = matrix
                prod = times(jnp.concatenate(upper, axis=0), q[base + span - 1])
                for i in range(span):
                    q[base + span + i] = prod[i * width : (i + 1) * width]
            slot += span
        span *= 2
    for i in range(points):
        p_lo[i] = both[0][i]
        p_hi[i * width : (i + 1) * width] = split_cols(both[1][i])
    for i in range(points // 2):
        rows = slice(i * width, (i + 1) * width)
        ds_lo[rows] = split_cols(d_lo[points // 2 + i])
        ds_hi[rows] = split_cols(d_hi[points // 2 + i])


def scanned(c, l_ref):
    points = c.shape[0]
    x = [c[i : i + 1, :] for i in range(points)]
    span, slot = 1, 0
    while span < points:
        for base in range(0, points, 2 * span):
            head = x[base + span - 1]
            for i in range(base + span, base + 2 * span):
                x[i] = x[i] + mapped_each(l_ref[slot : slot + 1], head)
                slot += 1
        span *= 2
    return jnp.concatenate(x, axis=0)


def scanned_split(c, l_ref):
    points, width = c.shape
    half = points // 2
    x = [c[i : i + 1, :] for i in range(points)]
    span, level = 1, 0
    while span < points:
        later = [i for i in range(points) if i & span]
        heads = jnp.concatenate([x[(i & ~(2 * span - 1)) + span - 1] for i in later], axis=0)
        rows = slice(level * half * width, (level + 1) * half * width)
        moved = mapped_each_split(l_ref[rows], heads)
        for slot, i in enumerate(later):
            x[i] = x[i] + moved[slot : slot + 1]
        span *= 2
        level += 1
    return jnp.concatenate(x, axis=0)


def taken(rows, lanes):
    return jnp.take_along_axis(rows, jnp.broadcast_to(lanes, rows.shape), axis=1)


def negative_residual(s, halo, inj, cap, gain, gs):
    before = jnp.concatenate([halo, s[: s.shape[0] - 1]], axis=0)
    return inj - cap * (s - before) - mapped(gs, s) - gain * jnp.tanh(s)


def corrected(nr, c_before, s_before, d_ref, js, ks):
    return mapped_each(d_ref, nr + mapped(js, c_before) + mapped(ks, s_before))


def pair_corrected(nr, s_lo, c_lo, bnd_lo, d_hi_ref, js, ks):
    return corrected(nr, taken(c_lo, bnd_lo), taken(s_lo, bnd_lo), d_hi_ref, js, ks)


def correct_both(
    s_lo, s_hi, halo_lo, halo_hi, small_ref, maps_ref, d_lo, d_hi, nr_ref, c_ref, msg_ref
):
    lo_maps, hi_maps = [maps_ref[i] for i in range(3)], [maps_ref[i] for i in range(3, 6)]
    points = s_lo.shape[0]
    inj_lo, cap_lo, gain_lo, bnd_lo = vectors(small_ref, 0, points)
    inj_hi, cap_hi, gain_hi, bnd_hi = vectors(small_ref, 1, points)
    nr_lo = negative_residual(s_lo, halo_lo, inj_lo, cap_lo, gain_lo, lo_maps[0])
    nr_hi = negative_residual(s_hi, halo_hi, inj_hi, cap_hi, gain_hi, hi_maps[0])
    nr_ref[:points], nr_ref[points:] = nr_lo, nr_hi
    msg_ref[points:] = taken(s_hi, bnd_hi)

    @pl.when(in_first_pair())
    def _():
        c_lo = mapped_each(d_lo, nr_lo)
        c_hi = pair_corrected(nr_hi, s_lo, c_lo, bnd_lo, d_hi, hi_maps[2], hi_maps[1])
        c_ref[:points], c_ref[points:] = c_lo, c_hi
        msg_ref[:points] = taken(c_hi, bnd_hi)

    @pl.when(jnp.logical_not(in_first_pair()))
    def _():
        c_ref[...] = jnp.zeros(c_ref.shape, F32)
        msg_ref[:points] = jnp.zeros((points, c_ref.shape[1]), F32)


def early_kernel(s_lo, s_hi, pack_lo, pack_hi, _, maps_ref, small_ref, nr_ref):
    points, width = s_lo.shape
    for i in range(3):
        rows = slice(i * width, (i + 1) * width)
        maps_ref[i] = split_cols(pack_lo[rows])
        maps_ref[3 + i] = split_cols(pack_hi[rows])
    none = jnp.zeros((1, width), F32)
    for g, (s_ref, pack) in enumerate(((s_lo, pack_lo), (s_hi, pack_hi))):
        at = g * (points + 24)
        small_ref[at : at + points + 24] = pack[3 * width :]
        inj, cap, gain, _ = vectors(small_ref, g, points)
        nr_ref[g * points : (g + 1) * points] = negative_residual(
            s_ref[...], none, inj, cap, gain, maps_ref[3 * g]
        )


def diagonal_kernel(_, lo_ref, d_lo, sems):
    for move in fetched((lo_ref,), (d_lo,), sems):
        move.wait()


def in_first_pair():
    return lax.axis_index("dom") < PAIR


def first_kernel(
    halo_ref, s_lo, s_hi, small_ref, maps_ref, d_lo, d_hi, old_nr, s_ref, nr_ref, c_ref, msg_ref
):
    points = s_lo.shape[0]
    bnd_lo, bnd_hi = (vectors(small_ref, g, points)[3] for g in range(PAIR))
    s_ref[:points], s_ref[points:] = s_lo[...], s_hi[...]
    msg_ref[points:] = taken(s_hi[...], bnd_hi)
    nr_ref[...] = old_nr[...]
    for g in range(PAIR):
        at = g * points
        cap = vectors(small_ref, g, points)[1]
        nr_ref[at : at + 1] = old_nr[at : at + 1] + cap * halo_ref[4 * g : 4 * g + 1]

    @pl.when(in_first_pair())
    def _():
        c_lo = mapped_each(d_lo, nr_ref[:points])
        linked = mapped(maps_ref[4], taken(s_lo[...], bnd_lo))
        c_hi = mapped_each(
            d_hi, nr_ref[points:] + linked + mapped(maps_ref[5], taken(c_lo, bnd_lo))
        )
        c_ref[:points], c_ref[points:] = c_lo, c_hi
        msg_ref[:points] = taken(c_hi, bnd_hi)

    @pl.when(jnp.logical_not(in_first_pair()))
    def _():
        c_ref[...] = jnp.zeros(c_ref.shape, F32)
        msg_ref[:points] = jnp.zeros((points, c_ref.shape[1]), F32)


def second_kernel(
    got_ref, s_ref, nr_ref, c_ref, small_ref, maps_ref, d_lo, d_hi, ss_ref, *refs
):
    new_c_ref, f_ref = refs[-2:]
    if len(refs) == 4:
        d_lo, d_hi = (d_lo, refs[0][...]), (d_hi, refs[1][...])
    points, width = got_ref.shape[0] // 2, got_ref.shape[1]
    second_pair = lax.axis_index("dom") >= PAIR

    @pl.when(second_pair)
    def _():
        bnd_lo = vectors(small_ref, 0, points)[3]
        c_lo = corrected(
            nr_ref[:points], got_ref[:points], got_ref[points:], d_lo, maps_ref[2], maps_ref[1]
        )
        new_c_ref[:points] = c_lo
        c_hi = pair_corrected(
            nr_ref[points:], s_ref[:points], c_lo, bnd_lo, d_hi, maps_ref[5], maps_ref[4]
        )
        new_c_ref[points:] = c_hi
        for g, c in enumerate((c_lo, c_hi)):
            whole = mapped_sum(ss_ref[g * points : (g + 1) * points], c)
            f_ref[8 * g : 8 * g + 8] = jnp.broadcast_to(whole, (8, width))

    @pl.when(jnp.logical_not(second_pair))
    def _():
        new_c_ref[...] = c_ref[...]
        for g in range(PAIR):
            rows = slice(g * points, (g + 1) * points)
            whole = mapped_sum(ss_ref[rows], c_ref[rows])
            f_ref[8 * g : 8 * g + 8] = jnp.broadcast_to(whole, (8, width))


def tail_kernel(c_ref, ss_ref, tail_ref):
    points, width = c_ref.shape[0] // PAIR, c_ref.shape[1]
    each = mapped_each(ss_ref, c_ref[...])
    for g in range(PAIR):
        total = each[g * points : (g + 1) * points]
        shift = 1
        while shift < points:
            total = total + jnp.concatenate(
                [total[shift:], jnp.zeros((shift, width), F32)], axis=0
            )
            shift *= 2
        at = g * (points + 8)
        tail_ref[at : at + points] = jnp.concatenate(
            [total[1:], jnp.zeros((1, width), F32)], axis=0
        )
        tail_ref[at + points : at + points + 8] = jnp.broadcast_to(total[:1], (8, width))


def is_later(distance):
    return (lax.axis_index("tm") // distance) % 2 == 1


def sections(width):
    return [
        (slice(g * width, (g + 1) * width), slice(8 * g, 8 * g + 8)) for g in range(PAIR)
    ]


def first_maps_kernel(distance, mw_ref, gw_ref, _, tw_ref, a_ref, bw_ref, aw_ref):
    width = mw_ref.shape[1]
    later = is_later(distance)
    eye = identity(width)
    for wide, _ in sections(width):
        mw, gw = mw_ref[wide], gw_ref[wide]
        a = jnp.where(later, mw, gw)
        tw_ref[wide] = times(a, jnp.where(later, gw, mw))
        a_ref[wide] = split_cols(a)
        bw_ref[wide] = jnp.where(later, gw, eye)
        aw_ref[wide] = jnp.where(later, eye, gw)


def next_maps_kernel(
    distance, mw_ref, gw_ref, bw_ref, aw_ref, _, tw_ref, a_ref, x_ref, nbw_ref, naw_ref
):
    width = mw_ref.shape[1]
    later = is_later(distance)
    for wide, _ in sections(width):
        mw, gw, bw, aw = mw_ref[wide], gw_ref[wide], bw_ref[wide], aw_ref[wide]
        a = jnp.where(later, mw, gw)
        tw_ref[wide] = times(a, jnp.where(later, gw, mw))
        a_ref[wide] = split_cols(a)
        x = jnp.where(later, bw, gw)
        joined = times(x, jnp.where(later, gw, aw))
        x_ref[wide] = split_cols(x)
        nbw_ref[wide] = jnp.where(later, joined, bw)
        naw_ref[wide] = jnp.where(later, aw, joined)


def first_sums_kernel(distance, mf_ref, gf_ref, a_ref, _, __, tf_ref, bf_ref, af_ref):
    later = is_later(distance)
    for wide, short in sections(a_ref.shape[0] // PAIR):
        mf, gf = mf_ref[short], gf_ref[short]
        tf_ref[short] = mapped(a_ref[wide], jnp.where(later, gf, mf)) + jnp.where(later, mf, gf)
        bf_ref[short] = jnp.where(later, gf, 0.0)
        af_ref[short] = jnp.where(later, 0.0, gf)


def next_sums_kernel(
    distance, mf_ref, gf_ref, bf_ref, af_ref, a_ref, x_ref, _, tf_ref, nbf_ref, naf_ref
):
    later = is_later(distance)
    for wide, short in sections(a_ref.shape[0] // PAIR):
        mf, gf, bf, af = mf_ref[short], gf_ref[short], bf_ref[short], af_ref[short]
        tf_ref[short] = mapped(a_ref[wide], jnp.where(later, gf, mf)) + jnp.where(later, mf, gf)
        sums = mapped(x_ref[wide], jnp.where(later, gf, af)) + jnp.where(later, bf, gf)
        nbf_ref[short] = jnp.where(later, sums, bf)
        naf_ref[short] = jnp.where(later, af, sums)


def local_kernel(c_ref, l_lo, l_hi, tail_ref, aw_ref, af_ref, s_ref, base_ref, v_ref):
    points, width = s_ref.shape[0] // PAIR, s_ref.shape[1]
    for g, (wide, short) in enumerate(sections(width)):
        rows = slice(g * points, (g + 1) * points)
        long = slice(g * (points + 8), (g + 1) * (points + 8))
        scan = scanned_split if g else scanned
        base_ref[rows] = s_ref[rows] + scan(c_ref[rows], (l_lo, l_hi)[g])
        v_ref[long] = mapped(split_cols(aw_ref[wide]), tail_ref[long]) + af_ref[short][:1]


def turn_kernel(
    v_ref, gw_ref, gf_ref, bw_ref, bf_ref, p_lo, p_hi, base_ref, halo_ref, small_ref, maps_ref,
    d_lo, d_hi, ds_lo, ds_hi, s_ref, nr_ref, c_ref, msg_ref,
):
    points, width = s_ref.shape[0] // PAIR, s_ref.shape[1]
    came = []
    for g, (wide, short) in enumerate(sections(width)):
        long = slice(g * (points + 8), (g + 1) * (points + 8))
        v = mapped(split_cols(gw_ref[wide]), v_ref[long]) + gf_ref[short][:1]
        came.append(mapped(split_cols(bw_ref[wide]), v) + bf_ref[short][:1])
    moved = [
        mapped_each(p_lo, came[0][:points]),
        mapped_each_split(p_hi[...], came[1][:points]),
    ]
    s = base_ref[...] + jnp.concatenate(moved, axis=0)
    s_ref[...] = s
    correct_both(
        s[:points], s[points:],
        halo_ref[:1] + came[0][points : points + 1],
        halo_ref[4:5] + came[1][points : points + 1],
        small_ref, maps_ref, (d_lo, ds_lo[...]), (d_hi, ds_hi[...]), nr_ref, c_ref, msg_ref,
    )


def scan_kernel(c_ref, l_lo, l_hi, s_ref, base_ref):
    points = s_ref.shape[0] // PAIR
    for g, (scan, l_ref) in enumerate(((scanned, l_lo), (scanned_split, l_hi))):
        rows = slice(g * points, (g + 1) * points)
        base_ref[rows] = s_ref[rows] + scan(c_ref[rows], l_ref)


def last_local_kernel(
    tail_ref, aw_ref, af_ref, gw_ref, bw_ref, bf_ref, p_lo, p_hi, old_ref, base_ref
):
    points, width = old_ref.shape[0] // PAIR, old_ref.shape[1]
    came = []
    for g, (wide, short) in enumerate(sections(width)):
        at = g * (points + 8)
        v = mapped(split_cols(aw_ref[wide]), tail_ref[at : at + points]) + af_ref[short][:1]
        v = mapped(split_cols(gw_ref[wide]), v)
        came.append(mapped(split_cols(bw_ref[wide]), v) + bf_ref[short][:1])
    for g in range(PAIR):
        rows = slice(g * points, (g + 1) * points)
        moved = mapped_each_split(p_hi[...], came[g]) if g else mapped_each(p_lo, came[g])
        base_ref[rows] = old_ref[rows] + moved


def end_kernel(gf_ref, bw_ref, p_lo, p_hi, base_ref, s_ref):
    points, width = s_ref.shape[0] // PAIR, s_ref.shape[1]
    for g, (wide, short) in enumerate(sections(width)):
        rows = slice(g * points, (g + 1) * points)
        v = mapped(split_cols(bw_ref[wide]), gf_ref[short])
        if g:
            both = dot_nt(split_rows(v), p_hi[...])
            both = both[:1] + both[8:9]
            moved = [both[:, i * width : (i + 1) * width] for i in range(points)]
            moved = jnp.concatenate(moved, axis=0)
        else:
            moved = mapped_each(p_lo, jnp.broadcast_to(v[:1], (points, width)))
        s_ref[rows] = base_ref[rows] + moved


def choose_kernel(both_ref, got_ref, s_ref):
    points = s_ref.shape[0]
    odd = lax.axis_index("dom") % 2 == 1
    s_ref[...] = jnp.where(odd, both_ref[points:], got_ref[:points])


def exchanged(value, distance):
    return lax.ppermute(
        value, "tm", [(i, i ^ distance) for i in range(lax.axis_size("tm"))]
    )


def swapped(value, distance):
    return lax.ppermute(value, "dom", [(i, i ^ distance) for i in range(lax.axis_size("dom"))])


def both_partitions(
    s, nr, c, msg, halo, small, maps, d_lo, d_hi, r_lo, r_hi, w
):
    points, width = s.shape[0] // PAIR, s.shape[1]
    vec, square = ((PAIR * points, width), F32), ((PAIR * width, width), F32)
    square_split = ((PAIR * width, 2 * width), BF16)
    eight = ((PAIR * 8, width), F32)
    longer = ((PAIR * (points + 8), width), F32)
    many = ((PAIR * points, width, width), F32)
    steps = (points.bit_length() - 1) * points // 2
    distances = [2**k for k in range(lax.axis_size("tm").bit_length() - 1)]

    def sums_level(level, f, bf, af, beside):
        got = exchanged(f, distances[level])
        if level == 0:
            return call(
                functools.partial(first_sums_kernel, distances[0]), [eight] * 3,
                f, got, *kept[0], *beside,
            )
        return call(
            functools.partial(next_sums_kernel, distances[level]), [eight] * 3,
            f, got, bf, af, *kept[level], beside[1],
            cost=pl.CostEstimate(flops=2**33, bytes_accessed=2**25, transcendentals=0),
        )

    got = swapped(msg, 2)
    got_w = exchanged(w, distances[0])
    ss, d_lo, d_hi = call(
        suffix_kernel, [many] + [((points, width, width), F32)] * 2, r_lo, r_hi, d_lo, d_hi,
        in_hbm=2, scratch=[pltpu.SemaphoreType.DMA((2,))],
    )
    p_lo, l_lo, p_hi, l_hi, ds_lo, ds_hi = call(
        prefix_kernel,
        [((points, width, width), F32), ((steps, width, width), F32)]
        + [((points * width, 2 * width), BF16), ((steps * width, 2 * width), BF16)]
        + [((points // 2 * width, 2 * width), BF16)] * 2,
        r_lo, r_hi, d_lo, d_hi,
    )
    c, f = call(
        second_kernel, [vec, eight], got, s, nr, c, small, maps, d_lo, d_hi, ss
    )
    (tail,) = call(tail_kernel, [longer], c, ss)
    kept, bf, af = [], None, None
    for level, distance in enumerate(distances[:-1]):
        if level == 0:
            w, a, bw, aw = call(
                functools.partial(first_maps_kernel, distance),
                [square, square_split, square, square], w, got_w, f,
            )
            kept.append((a,))
        else:
            w, a, x, bw, aw = call(
                functools.partial(next_maps_kernel, distance),
                [square, square_split, square_split, square, square], w, got_w, bw, aw, f,
            )
            kept.append((a, x))
        got_w = exchanged(w, distances[level + 1])
        f, bf, af = sums_level(level, f, bf, af, (p_lo, p_hi))
    got, last = exchanged(f, distances[-1]), got_w
    base, v = call(local_kernel, [vec, longer], c, l_lo, l_hi, tail, aw, af, s)
    s, nr, c, msg = call(
        turn_kernel, [vec] * 4,
        v, last, got, bw, bf, p_lo, p_hi, base, halo, small, maps, d_lo, d_hi, ds_lo, ds_hi,
    )
    got = swapped(msg, 2)
    c, f = call(
        second_kernel, [vec, eight], got, s, nr, c, small, maps, d_lo, d_hi, ss, ds_lo, ds_hi
    )
    (tail,) = call(tail_kernel, [longer], c, ss)
    (base,) = call(scan_kernel, [vec], c, l_lo, l_hi, s)
    for level in range(len(distances) - 1):
        f, bf, af = sums_level(level, f, bf, af, (tail, base))
    got = exchanged(f, distances[-1])
    (base,) = call(last_local_kernel, [vec], tail, aw, af, last, bw, bf, p_lo, p_hi, base)
    return call(end_kernel, [vec], got, bw, p_lo, p_hi, base)[0]


def per_device(
    starting_voltage_guess,
    injected_amperes,
    capacitance,
    conductance,
    block_pattern,
    device_gain,
    link_weight,
    boundary_vertex_list,
    diagonal_reciprocals,
    boundary_jacobian,
    transfer,
):
    points, _, width = starting_voltage_guess.shape
    segments = lax.axis_size("tm")
    (one,) = call(
        ones_kernel, [((1, width), F32)],
        cost=pl.CostEstimate(flops=2**33, bytes_accessed=2**25, transcendentals=0),
    )
    mask = jnp.broadcast_to(block_pattern[0].astype(F32), (1, width))
    s = starting_voltage_guess[:, 0]
    near_s = swapped(starting_voltage_guess, 1)[:, 0]
    d, r, near_s, mask, one = lax.optimization_barrier(
        (diagonal_reciprocals, transfer, near_s, mask, one)
    )
    d, near_d = d[:, 0, 0], swapped(d, 1)[:, 0, 0]
    r, near_r = r[:, 0, 0], swapped(r, 1)[:, 0, 0]
    (rows,) = call(halo_kernel, [((8, width), F32)], s, near_s)
    halo = lax.ppermute(rows, "tm", [(i, (i + 1) % segments) for i in range(segments)])
    (pack,) = call(
        pack_kernel, [((3 * width + points + 24, width), F32)],
        one, conductance[0], mask, link_weight[0], boundary_jacobian[0],
        injected_amperes[:, 0], capacitance, device_gain, boundary_vertex_list,
    )
    near_pack = swapped(pack, 1)
    vec = ((PAIR * points, width), F32)
    w, d_hi = call(
        whole_kernel, [((PAIR * width, width), F32), ((points, width, width), F32)],
        near_r, r, d, in_hbm=3,
        scratch=[pltpu.VMEM((points, width, width), F32)] * 2 + [pltpu.SemaphoreType.DMA((3,))],
    )
    maps, small, nr = call(
        early_kernel,
        [((6, width, 2 * width), BF16), ((PAIR * (points + 24), width), F32), vec],
        near_s, s, near_pack, pack, w,
    )
    (d_lo,) = call(
        diagonal_kernel, [((points, width, width), F32)], nr, near_d,
        in_hbm=1, scratch=[pltpu.SemaphoreType.DMA((1,))],
    )
    s, nr, c, msg = call(
        first_kernel, [vec] * 4, halo, near_s, s, small, maps, d_lo, d_hi, nr
    )
    odd = lax.axis_index("dom") % 2 == 1
    both = lax.cond(
        odd,
        both_partitions,
        lambda s, *rest: s,
        s, nr, c, msg, halo, small, maps, near_d, d, near_r, r, w,
    )
    (s,) = call(choose_kernel, [((points, width), F32)], both, swapped(both, 1))
    return s[:, None]


def solution(mesh):
    in_specs = (
        P("tm", "dom", None),
        P("tm", "dom", None),
        P("dom", None),
        P("dom", None, None),
        P("dom", None, None),
        P("dom", None),
        P("dom", None, None),
        P("dom", None),
        P("tm", "dom", None, None, None),
        P("dom", None, None),
        P("tm", "dom", None, None, None),
    )
    out_specs = P("tm", "dom", None)
    return jax.shard_map(
        per_device, mesh=mesh, in_specs=in_specs, out_specs=out_specs, check_vma=False
    )
```

```python
import functools

import jax
import jax.numpy as jnp
from jax import lax
from jax.experimental import pallas as pl
from jax.experimental.pallas import tpu as pltpu
from jax.sharding import PartitionSpec as P

F32 = jnp.float32
BF16 = jnp.bfloat16
PAIR = 2


def halves(x):
    hi = x.astype(BF16)
    return hi, (x - hi.astype(F32)).astype(BF16)


def split_cols(matrix):
    return jnp.concatenate(halves(matrix), axis=1)


def split_rows(vectors):
    hi, lo = halves(vectors)
    hi, lo = hi.astype(F32), lo.astype(F32)
    top = jnp.concatenate([hi, hi], axis=1)
    low = jnp.concatenate([lo, jnp.zeros_like(lo)], axis=1)
    return jnp.concatenate([top, low], axis=0).astype(BF16)


def dot_nt(a, b):
    return lax.dot_general(a, b, (((1,), (1,)), ((), ())), preferred_element_type=F32)


def times(a, b):
    ah, al = halves(a)
    bh, bl = halves(b)
    left = jnp.concatenate([ah, al, ah], axis=1)
    right = jnp.concatenate([bh, bh, bl], axis=0)
    return jnp.dot(left, right, preferred_element_type=F32)


def mapped(matrix_split, vectors):
    count = vectors.shape[0]
    both = dot_nt(split_rows(vectors), matrix_split)
    return both[:count] + both[count:]


def mapped_each(matrices, vectors):
    if isinstance(matrices, tuple):
        half = vectors.shape[0] // 2
        near = mapped_each(matrices[0], vectors[:half])
        return jnp.concatenate([near, mapped_each_split(matrices[1], vectors[half:])], axis=0)
    rows = []
    for r in range(vectors.shape[0]):
        products = matrices[r] * vectors[r : r + 1, :]
        rows.append(jnp.sum(products.T, axis=0, keepdims=True))
    return jnp.concatenate(rows, axis=0)


def mapped_each_split(matrices_split, vectors):
    count, width = vectors.shape
    both = dot_nt(split_rows(vectors), matrices_split)
    row = lax.broadcasted_iota(jnp.int32, (2 * count, width), 0) % count
    picked = [
        jnp.where(row == r, both[:, r * width : (r + 1) * width], 0.0) for r in range(count)
    ]
    while len(picked) > 1:
        picked = [a + b for a, b in zip(picked[::2], picked[1::2])]
    return picked[0][:count] + picked[0][count:]


def mapped_sum(matrices, vectors):
    products = matrices[0] * vectors[:1, :]
    for r in range(1, vectors.shape[0]):
        products = products + matrices[r] * vectors[r : r + 1, :]
    return jnp.sum(products.T, axis=0, keepdims=True)


def call(kernel, outs, *args, cost=None, in_hbm=0, scratch=()):
    vmem = pl.BlockSpec(memory_space=pltpu.VMEM)
    return pl.pallas_call(
        kernel,
        out_shape=[jax.ShapeDtypeStruct(s, d) for s, d in outs],
        in_specs=[vmem] * (len(args) - in_hbm) + [pl.BlockSpec(memory_space=pltpu.HBM)] * in_hbm,
        out_specs=[vmem] * len(outs),
        scratch_shapes=list(scratch),
        cost_estimate=cost,
        compiler_params=pltpu.CompilerParams(vmem_limit_bytes=24 * 2**20),
    )(*args)


def identity(width):
    return (
        lax.broadcasted_iota(jnp.int32, (width, width), 0)
        == lax.broadcasted_iota(jnp.int32, (width, width), 1)
    ).astype(F32)


def halo_kernel(s_ref, near_ref, msg_ref):
    points, width = s_ref.shape
    msg_ref[:4] = jnp.broadcast_to(near_ref[points - 1 :], (4, width))
    msg_ref[4:] = jnp.broadcast_to(s_ref[points - 1 :], (4, width))


def ones_kernel(one_ref):
    one_ref[...] = jnp.ones(one_ref.shape, F32)


def pack_kernel(one_ref, g_ref, mask_ref, k_ref, j_ref, inj_ref, cap_ref, gain_ref, bnd_ref, pack_ref):
    points, width = inj_ref.shape
    pack_ref[:width] = g_ref[...] * (mask_ref[...] * one_ref[...])
    pack_ref[width : 2 * width] = k_ref[...]
    pack_ref[2 * width : 3 * width] = j_ref[...]
    at = 3 * width
    pack_ref[at : at + points] = inj_ref[...]
    at += points
    for one in (cap_ref[...], gain_ref[...], bnd_ref[...].astype(F32)):
        pack_ref[at : at + 8] = jnp.broadcast_to(one, (8, width))
        at += 8


def vectors(small_ref, g, points):
    at = g * (points + 24)
    inj = small_ref[at : at + points]
    at += points
    cap, gain, bnd = (small_ref[at + 8 * i : at + 8 * i + 1] for i in range(3))
    return inj, cap, gain, bnd.astype(jnp.int32)


def fetched(sources, targets, sems):
    moves = [
        pltpu.make_async_copy(source, target, sems.at[i])
        for i, (source, target) in enumerate(zip(sources, targets))
    ]
    for move in moves:
        move.start()
    return moves


def whole_kernel(lo_ref, hi_ref, diag_ref, w_ref, d_hi, r_lo, r_hi, sems):
    points, width = lo_ref.shape[0], lo_ref.shape[1]
    moves = fetched((lo_ref, hi_ref, diag_ref), (r_lo, r_hi, d_hi), sems)
    u = []
    for move, r_ref in zip(moves, (r_lo, r_hi)):
        move.wait()
        u += [times(r_ref[i + 1], r_ref[i]) for i in range(0, points, 2)]
    while len(u) > PAIR:
        u = [times(u[i + 1], u[i]) for i in range(0, len(u), 2)]
    for g in range(PAIR):
        w_ref[g * width : (g + 1) * width] = u[g]
    moves[-1].wait()


def suffix_kernel(r_lo, r_hi, lo_ref, hi_ref, s_ref, d_lo, d_hi, sems):
    points, width = r_lo.shape[0], r_lo.shape[1]
    moves = fetched((lo_ref, hi_ref), (d_lo, d_hi), sems)
    both = [[r_ref[i] for i in range(points)] for r_ref in (r_lo, r_hi)]
    span = 1
    while span < points:
        for base in range(0, points, 2 * span):
            first = max(base, 1)
            if first == base + span:
                continue
            for u in both:
                prod = times(u[base + span], jnp.concatenate(u[first : base + span], axis=1))
                for i in range(first, base + span):
                    at = (i - first) * width
                    u[i] = prod[:, at : at + width]
        span *= 2
    for g, u in enumerate(both):
        for i in range(points - 1):
            s_ref[g * points + i] = u[i + 1]
        s_ref[(g + 1) * points - 1] = identity(width)
    for move in moves:
        move.wait()


def prefix_kernel(r_lo, r_hi, p_lo, l_lo, p_hi, l_hi):
    points, width = r_lo.shape[0], r_lo.shape[1]
    both = [[r_ref[i] for i in range(points)] for r_ref in (r_lo, r_hi)]
    span, slot = 1, 0
    while span < points:
        for base in range(0, points, 2 * span):
            for q, l_ref in zip(both, (l_lo, l_hi)):
                upper = q[base + span : base + 2 * span]
                for i, matrix in enumerate(upper):
                    if l_ref is l_hi:
                        at = (slot + i) * width
                        l_ref[at : at + width] = split_cols(matrix)
                    else:
                        l_ref[slot + i] = matrix
                prod = times(jnp.concatenate(upper, axis=0), q[base + span - 1])
                for i in range(span):
                    q[base + span + i] = prod[i * width : (i + 1) * width]
            slot += span
        span *= 2
    for i in range(points):
        p_lo[i] = both[0][i]
        p_hi[i * width : (i + 1) * width] = split_cols(both[1][i])


def scanned(c, l_ref):
    points = c.shape[0]
    x = [c[i : i + 1, :] for i in range(points)]
    span, slot = 1, 0
    while span < points:
        for base in range(0, points, 2 * span):
            head = x[base + span - 1]
            for i in range(base + span, base + 2 * span):
                x[i] = x[i] + mapped_each(l_ref[slot : slot + 1], head)
                slot += 1
        span *= 2
    return jnp.concatenate(x, axis=0)


def scanned_split(c, l_ref):
    points, width = c.shape
    half = points // 2
    x = [c[i : i + 1, :] for i in range(points)]
    span, level = 1, 0
    while span < points:
        later = [i for i in range(points) if i & span]
        heads = jnp.concatenate([x[(i & ~(2 * span - 1)) + span - 1] for i in later], axis=0)
        rows = slice(level * half * width, (level + 1) * half * width)
        moved = mapped_each_split(l_ref[rows], heads)
        for slot, i in enumerate(later):
            x[i] = x[i] + moved[slot : slot + 1]
        span *= 2
        level += 1
    return jnp.concatenate(x, axis=0)


def taken(rows, lanes):
    return jnp.take_along_axis(rows, jnp.broadcast_to(lanes, rows.shape), axis=1)


def negative_residual(s, halo, inj, cap, gain, gs):
    before = jnp.concatenate([halo, s[: s.shape[0] - 1]], axis=0)
    return inj - cap * (s - before) - mapped(gs, s) - gain * jnp.tanh(s)


def corrected(nr, c_before, s_before, d_ref, js, ks):
    return mapped_each(d_ref, nr + mapped(js, c_before) + mapped(ks, s_before))


def pair_corrected(nr, s_lo, c_lo, bnd_lo, d_hi_ref, js, ks):
    return corrected(nr, taken(c_lo, bnd_lo), taken(s_lo, bnd_lo), d_hi_ref, js, ks)


def correct_both(
    s_lo, s_hi, halo_lo, halo_hi, small_ref, maps_ref, d_lo, d_hi, nr_ref, c_ref, msg_ref
):
    lo_maps, hi_maps = [maps_ref[i] for i in range(3)], [maps_ref[i] for i in range(3, 6)]
    points = s_lo.shape[0]
    inj_lo, cap_lo, gain_lo, bnd_lo = vectors(small_ref, 0, points)
    inj_hi, cap_hi, gain_hi, bnd_hi = vectors(small_ref, 1, points)
    nr_lo = negative_residual(s_lo, halo_lo, inj_lo, cap_lo, gain_lo, lo_maps[0])
    nr_hi = negative_residual(s_hi, halo_hi, inj_hi, cap_hi, gain_hi, hi_maps[0])
    nr_ref[:points], nr_ref[points:] = nr_lo, nr_hi
    msg_ref[points:] = taken(s_hi, bnd_hi)

    @pl.when(in_first_pair())
    def _():
        c_lo = mapped_each(d_lo, nr_lo)
        c_hi = pair_corrected(nr_hi, s_lo, c_lo, bnd_lo, d_hi, hi_maps[2], hi_maps[1])
        c_ref[:points], c_ref[points:] = c_lo, c_hi
        msg_ref[:points] = taken(c_hi, bnd_hi)

    @pl.when(jnp.logical_not(in_first_pair()))
    def _():
        c_ref[...] = jnp.zeros(c_ref.shape, F32)
        msg_ref[:points] = jnp.zeros((points, c_ref.shape[1]), F32)


def early_kernel(s_lo, s_hi, pack_lo, pack_hi, _, maps_ref, small_ref, nr_ref):
    points, width = s_lo.shape
    for i in range(3):
        rows = slice(i * width, (i + 1) * width)
        maps_ref[i] = split_cols(pack_lo[rows])
        maps_ref[3 + i] = split_cols(pack_hi[rows])
    none = jnp.zeros((1, width), F32)
    for g, (s_ref, pack) in enumerate(((s_lo, pack_lo), (s_hi, pack_hi))):
        at = g * (points + 24)
        small_ref[at : at + points + 24] = pack[3 * width :]
        inj, cap, gain, _ = vectors(small_ref, g, points)
        nr_ref[g * points : (g + 1) * points] = negative_residual(
            s_ref[...], none, inj, cap, gain, maps_ref[3 * g]
        )


def diagonal_kernel(_, lo_ref, d_lo, sems):
    for move in fetched((lo_ref,), (d_lo,), sems):
        move.wait()


def in_first_pair():
    return lax.axis_index("dom") < PAIR


def first_kernel(
    halo_ref, s_lo, s_hi, small_ref, maps_ref, d_lo, d_hi, old_nr, s_ref, nr_ref, c_ref, msg_ref
):
    points = s_lo.shape[0]
    bnd_lo, bnd_hi = (vectors(small_ref, g, points)[3] for g in range(PAIR))
    s_ref[:points], s_ref[points:] = s_lo[...], s_hi[...]
    msg_ref[points:] = taken(s_hi[...], bnd_hi)
    nr_ref[...] = old_nr[...]
    for g in range(PAIR):
        at = g * points
        cap = vectors(small_ref, g, points)[1]
        nr_ref[at : at + 1] = old_nr[at : at + 1] + cap * halo_ref[4 * g : 4 * g + 1]

    @pl.when(in_first_pair())
    def _():
        c_lo = mapped_each(d_lo, nr_ref[:points])
        linked = mapped(maps_ref[4], taken(s_lo[...], bnd_lo))
        c_hi = mapped_each(
            d_hi, nr_ref[points:] + linked + mapped(maps_ref[5], taken(c_lo, bnd_lo))
        )
        c_ref[:points], c_ref[points:] = c_lo, c_hi
        msg_ref[:points] = taken(c_hi, bnd_hi)

    @pl.when(jnp.logical_not(in_first_pair()))
    def _():
        c_ref[...] = jnp.zeros(c_ref.shape, F32)
        msg_ref[:points] = jnp.zeros((points, c_ref.shape[1]), F32)


def second_kernel(
    got_ref, s_ref, nr_ref, c_ref, small_ref, maps_ref, d_lo, d_hi, ss_ref, *refs
):
    new_c_ref, f_ref = refs[-2:]
    if len(refs) == 4:
        d_lo, d_hi = (d_lo, refs[0][...]), (d_hi, refs[1][...])
    points, width = got_ref.shape[0] // 2, got_ref.shape[1]
    second_pair = lax.axis_index("dom") >= PAIR

    @pl.when(second_pair)
    def _():
        bnd_lo = vectors(small_ref, 0, points)[3]
        c_lo = corrected(
            nr_ref[:points], got_ref[:points], got_ref[points:], d_lo, maps_ref[2], maps_ref[1]
        )
        new_c_ref[:points] = c_lo
        c_hi = pair_corrected(
            nr_ref[points:], s_ref[:points], c_lo, bnd_lo, d_hi, maps_ref[5], maps_ref[4]
        )
        new_c_ref[points:] = c_hi
        for g, c in enumerate((c_lo, c_hi)):
            whole = mapped_sum(ss_ref[g * points : (g + 1) * points], c)
            f_ref[8 * g : 8 * g + 8] = jnp.broadcast_to(whole, (8, width))

    @pl.when(jnp.logical_not(second_pair))
    def _():
        new_c_ref[...] = c_ref[...]
        for g in range(PAIR):
            rows = slice(g * points, (g + 1) * points)
            whole = mapped_sum(ss_ref[rows], c_ref[rows])
            f_ref[8 * g : 8 * g + 8] = jnp.broadcast_to(whole, (8, width))


def tail_and_split_kernel(c_ref, ss_ref, d_lo, d_hi, tail_ref, ds_lo, ds_hi):
    points, width = d_lo.shape[0], d_lo.shape[1]
    for i in range(points // 2):
        rows = slice(i * width, (i + 1) * width)
        ds_lo[rows] = split_cols(d_lo[points // 2 + i])
        ds_hi[rows] = split_cols(d_hi[points // 2 + i])
    tail_kernel(c_ref, ss_ref, tail_ref)


def tail_kernel(c_ref, ss_ref, tail_ref):
    points, width = c_ref.shape[0] // PAIR, c_ref.shape[1]
    each = mapped_each(ss_ref, c_ref[...])
    for g in range(PAIR):
        total = each[g * points : (g + 1) * points]
        shift = 1
        while shift < points:
            total = total + jnp.concatenate(
                [total[shift:], jnp.zeros((shift, width), F32)], axis=0
            )
            shift *= 2
        at = g * (points + 8)
        tail_ref[at : at + points] = jnp.concatenate(
            [total[1:], jnp.zeros((1, width), F32)], axis=0
        )
        tail_ref[at + points : at + points + 8] = jnp.broadcast_to(total[:1], (8, width))


def is_later(distance):
    return (lax.axis_index("tm") // distance) % 2 == 1


def sections(width):
    return [
        (slice(g * width, (g + 1) * width), slice(8 * g, 8 * g + 8)) for g in range(PAIR)
    ]


def first_maps_kernel(distance, mw_ref, gw_ref, _, tw_ref, a_ref, bw_ref, aw_ref):
    width = mw_ref.shape[1]
    later = is_later(distance)
    eye = identity(width)
    for wide, _ in sections(width):
        mw, gw = mw_ref[wide], gw_ref[wide]
        a = jnp.where(later, mw, gw)
        tw_ref[wide] = times(a, jnp.where(later, gw, mw))
        a_ref[wide] = split_cols(a)
        bw_ref[wide] = jnp.where(later, gw, eye)
        aw_ref[wide] = jnp.where(later, eye, gw)


def next_maps_kernel(
    distance, mw_ref, gw_ref, bw_ref, aw_ref, _, tw_ref, a_ref, x_ref, nbw_ref, naw_ref
):
    width = mw_ref.shape[1]
    later = is_later(distance)
    for wide, _ in sections(width):
        mw, gw, bw, aw = mw_ref[wide], gw_ref[wide], bw_ref[wide], aw_ref[wide]
        a = jnp.where(later, mw, gw)
        tw_ref[wide] = times(a, jnp.where(later, gw, mw))
        a_ref[wide] = split_cols(a)
        x = jnp.where(later, bw, gw)
        joined = times(x, jnp.where(later, gw, aw))
        x_ref[wide] = split_cols(x)
        nbw_ref[wide] = jnp.where(later, joined, bw)
        naw_ref[wide] = jnp.where(later, aw, joined)


def first_sums_kernel(distance, mf_ref, gf_ref, a_ref, _, __, tf_ref, bf_ref, af_ref):
    later = is_later(distance)
    for wide, short in sections(a_ref.shape[0] // PAIR):
        mf, gf = mf_ref[short], gf_ref[short]
        tf_ref[short] = mapped(a_ref[wide], jnp.where(later, gf, mf)) + jnp.where(later, mf, gf)
        bf_ref[short] = jnp.where(later, gf, 0.0)
        af_ref[short] = jnp.where(later, 0.0, gf)


def next_sums_kernel(
    distance, mf_ref, gf_ref, bf_ref, af_ref, a_ref, x_ref, _, tf_ref, nbf_ref, naf_ref
):
    later = is_later(distance)
    for wide, short in sections(a_ref.shape[0] // PAIR):
        mf, gf, bf, af = mf_ref[short], gf_ref[short], bf_ref[short], af_ref[short]
        tf_ref[short] = mapped(a_ref[wide], jnp.where(later, gf, mf)) + jnp.where(later, mf, gf)
        sums = mapped(x_ref[wide], jnp.where(later, gf, af)) + jnp.where(later, bf, gf)
        nbf_ref[short] = jnp.where(later, sums, bf)
        naf_ref[short] = jnp.where(later, af, sums)


def local_kernel(c_ref, l_lo, l_hi, tail_ref, aw_ref, af_ref, s_ref, base_ref, v_ref):
    points, width = s_ref.shape[0] // PAIR, s_ref.shape[1]
    for g, (wide, short) in enumerate(sections(width)):
        rows = slice(g * points, (g + 1) * points)
        long = slice(g * (points + 8), (g + 1) * (points + 8))
        scan = scanned_split if g else scanned
        base_ref[rows] = s_ref[rows] + scan(c_ref[rows], (l_lo, l_hi)[g])
        v_ref[long] = mapped(split_cols(aw_ref[wide]), tail_ref[long]) + af_ref[short][:1]


def turn_kernel(
    v_ref, gw_ref, gf_ref, bw_ref, bf_ref, p_lo, p_hi, base_ref, halo_ref, small_ref, maps_ref,
    d_lo, d_hi, ds_lo, ds_hi, s_ref, nr_ref, c_ref, msg_ref,
):
    points, width = s_ref.shape[0] // PAIR, s_ref.shape[1]
    came = []
    for g, (wide, short) in enumerate(sections(width)):
        long = slice(g * (points + 8), (g + 1) * (points + 8))
        v = mapped(split_cols(gw_ref[wide]), v_ref[long]) + gf_ref[short][:1]
        came.append(mapped(split_cols(bw_ref[wide]), v) + bf_ref[short][:1])
    moved = [
        mapped_each(p_lo, came[0][:points]),
        mapped_each_split(p_hi[...], came[1][:points]),
    ]
    s = base_ref[...] + jnp.concatenate(moved, axis=0)
    s_ref[...] = s
    correct_both(
        s[:points], s[points:],
        halo_ref[:1] + came[0][points : points + 1],
        halo_ref[4:5] + came[1][points : points + 1],
        small_ref, maps_ref, (d_lo, ds_lo[...]), (d_hi, ds_hi[...]), nr_ref, c_ref, msg_ref,
    )


def scan_kernel(c_ref, l_lo, l_hi, s_ref, base_ref):
    points = s_ref.shape[0] // PAIR
    for g, (scan, l_ref) in enumerate(((scanned, l_lo), (scanned_split, l_hi))):
        rows = slice(g * points, (g + 1) * points)
        base_ref[rows] = s_ref[rows] + scan(c_ref[rows], l_ref)


def last_local_kernel(
    tail_ref, aw_ref, af_ref, gw_ref, bw_ref, bf_ref, p_lo, p_hi, old_ref, base_ref
):
    points, width = old_ref.shape[0] // PAIR, old_ref.shape[1]
    came = []
    for g, (wide, short) in enumerate(sections(width)):
        at = g * (points + 8)
        v = mapped(split_cols(aw_ref[wide]), tail_ref[at : at + points]) + af_ref[short][:1]
        v = mapped(split_cols(gw_ref[wide]), v)
        came.append(mapped(split_cols(bw_ref[wide]), v) + bf_ref[short][:1])
    for g in range(PAIR):
        rows = slice(g * points, (g + 1) * points)
        moved = mapped_each_split(p_hi[...], came[g]) if g else mapped_each(p_lo, came[g])
        base_ref[rows] = old_ref[rows] + moved


def end_kernel(gf_ref, bw_ref, p_lo, p_hi, base_ref, s_ref):
    points, width = s_ref.shape[0] // PAIR, s_ref.shape[1]
    for g, (wide, short) in enumerate(sections(width)):
        rows = slice(g * points, (g + 1) * points)
        v = mapped(split_cols(bw_ref[wide]), gf_ref[short])
        if g:
            both = dot_nt(split_rows(v), p_hi[...])
            both = both[:1] + both[8:9]
            moved = [both[:, i * width : (i + 1) * width] for i in range(points)]
            moved = jnp.concatenate(moved, axis=0)
        else:
            moved = mapped_each(p_lo, jnp.broadcast_to(v[:1], (points, width)))
        s_ref[rows] = base_ref[rows] + moved


def choose_kernel(both_ref, got_ref, s_ref):
    points = s_ref.shape[0]
    odd = lax.axis_index("dom") % 2 == 1
    s_ref[...] = jnp.where(odd, both_ref[points:], got_ref[:points])


def exchanged(value, distance):
    return lax.ppermute(
        value, "tm", [(i, i ^ distance) for i in range(lax.axis_size("tm"))]
    )


def swapped(value, distance):
    return lax.ppermute(value, "dom", [(i, i ^ distance) for i in range(lax.axis_size("dom"))])


def both_partitions(
    s, nr, c, msg, halo, small, maps, d_lo, d_hi, r_lo, r_hi, w
):
    points, width = s.shape[0] // PAIR, s.shape[1]
    vec, square = ((PAIR * points, width), F32), ((PAIR * width, width), F32)
    square_split = ((PAIR * width, 2 * width), BF16)
    eight = ((PAIR * 8, width), F32)
    longer = ((PAIR * (points + 8), width), F32)
    many = ((PAIR * points, width, width), F32)
    steps = (points.bit_length() - 1) * points // 2
    distances = [2**k for k in range(lax.axis_size("tm").bit_length() - 1)]

    def sums_level(level, f, bf, af, beside):
        got = exchanged(f, distances[level])
        if level == 0:
            return call(
                functools.partial(first_sums_kernel, distances[0]), [eight] * 3,
                f, got, *kept[0], *beside,
            )
        return call(
            functools.partial(next_sums_kernel, distances[level]), [eight] * 3,
            f, got, bf, af, *kept[level], beside[1],
            cost=pl.CostEstimate(flops=2**33, bytes_accessed=2**25, transcendentals=0),
        )

    got = swapped(msg, 2)
    got_w = exchanged(w, distances[0])
    ss, d_lo, d_hi = call(
        suffix_kernel, [many] + [((points, width, width), F32)] * 2, r_lo, r_hi, d_lo, d_hi,
        in_hbm=2, scratch=[pltpu.SemaphoreType.DMA((2,))],
    )
    p_lo, l_lo, p_hi, l_hi = call(
        prefix_kernel,
        [((points, width, width), F32), ((steps, width, width), F32)]
        + [((points * width, 2 * width), BF16), ((steps * width, 2 * width), BF16)],
        r_lo, r_hi,
    )
    c, f = call(
        second_kernel, [vec, eight], got, s, nr, c, small, maps, d_lo, d_hi, ss
    )
    tail, ds_lo, ds_hi = call(
        tail_and_split_kernel, [longer] + [((points // 2 * width, 2 * width), BF16)] * 2,
        c, ss, d_lo, d_hi,
    )
    kept, bf, af = [], None, None
    for level, distance in enumerate(distances[:-1]):
        if level == 0:
            w, a, bw, aw = call(
                functools.partial(first_maps_kernel, distance),
                [square, square_split, square, square], w, got_w, f,
            )
            kept.append((a,))
        else:
            w, a, x, bw, aw = call(
                functools.partial(next_maps_kernel, distance),
                [square, square_split, square_split, square, square], w, got_w, bw, aw, f,
            )
            kept.append((a, x))
        got_w = exchanged(w, distances[level + 1])
        f, bf, af = sums_level(level, f, bf, af, (p_lo, p_hi))
    got, last = exchanged(f, distances[-1]), got_w
    base, v = call(local_kernel, [vec, longer], c, l_lo, l_hi, tail, aw, af, s)
    s, nr, c, msg = call(
        turn_kernel, [vec] * 4,
        v, last, got, bw, bf, p_lo, p_hi, base, halo, small, maps, d_lo, d_hi, ds_lo, ds_hi,
    )
    got = swapped(msg, 2)
    c, f = call(
        second_kernel, [vec, eight], got, s, nr, c, small, maps, d_lo, d_hi, ss, ds_lo, ds_hi
    )
    (tail,) = call(tail_kernel, [longer], c, ss)
    (base,) = call(scan_kernel, [vec], c, l_lo, l_hi, s)
    for level in range(len(distances) - 1):
        f, bf, af = sums_level(level, f, bf, af, (tail, base))
    got = exchanged(f, distances[-1])
    (base,) = call(last_local_kernel, [vec], tail, aw, af, last, bw, bf, p_lo, p_hi, base)
    return call(end_kernel, [vec], got, bw, p_lo, p_hi, base)[0]


def per_device(
    starting_voltage_guess,
    injected_amperes,
    capacitance,
    conductance,
    block_pattern,
    device_gain,
    link_weight,
    boundary_vertex_list,
    diagonal_reciprocals,
    boundary_jacobian,
    transfer,
):
    points, _, width = starting_voltage_guess.shape
    segments = lax.axis_size("tm")
    (one,) = call(
        ones_kernel, [((1, width), F32)],
        cost=pl.CostEstimate(flops=2**33, bytes_accessed=2**25, transcendentals=0),
    )
    mask = jnp.broadcast_to(block_pattern[0].astype(F32), (1, width))
    s = starting_voltage_guess[:, 0]
    near_s = swapped(starting_voltage_guess, 1)[:, 0]
    d, r, near_s, mask, one = lax.optimization_barrier(
        (diagonal_reciprocals, transfer, near_s, mask, one)
    )
    d, near_d = d[:, 0, 0], swapped(d, 1)[:, 0, 0]
    r, near_r = r[:, 0, 0], swapped(r, 1)[:, 0, 0]
    (rows,) = call(halo_kernel, [((8, width), F32)], s, near_s)
    halo = lax.ppermute(rows, "tm", [(i, (i + 1) % segments) for i in range(segments)])
    (pack,) = call(
        pack_kernel, [((3 * width + points + 24, width), F32)],
        one, conductance[0], mask, link_weight[0], boundary_jacobian[0],
        injected_amperes[:, 0], capacitance, device_gain, boundary_vertex_list,
    )
    near_pack = swapped(pack, 1)
    vec = ((PAIR * points, width), F32)
    w, d_hi = call(
        whole_kernel, [((PAIR * width, width), F32), ((points, width, width), F32)],
        near_r, r, d, in_hbm=3,
        scratch=[pltpu.VMEM((points, width, width), F32)] * 2 + [pltpu.SemaphoreType.DMA((3,))],
    )
    maps, small, nr = call(
        early_kernel,
        [((6, width, 2 * width), BF16), ((PAIR * (points + 24), width), F32), vec],
        near_s, s, near_pack, pack, w,
    )
    (d_lo,) = call(
        diagonal_kernel, [((points, width, width), F32)], nr, near_d,
        in_hbm=1, scratch=[pltpu.SemaphoreType.DMA((1,))],
    )
    s, nr, c, msg = call(
        first_kernel, [vec] * 4, halo, near_s, s, small, maps, d_lo, d_hi, nr
    )
    odd = lax.axis_index("dom") % 2 == 1
    both = lax.cond(
        odd,
        both_partitions,
        lambda s, *rest: s,
        s, nr, c, msg, halo, small, maps, near_d, d, near_r, r, w,
    )
    (s,) = call(choose_kernel, [((points, width), F32)], both, swapped(both, 1))
    return s[:, None]


def solution(mesh):
    in_specs = (
        P("tm", "dom", None),
        P("tm", "dom", None),
        P("dom", None),
        P("dom", None, None),
        P("dom", None, None),
        P("dom", None),
        P("dom", None, None),
        P("dom", None),
        P("tm", "dom", None, None, None),
        P("dom", None, None),
        P("tm", "dom", None, None, None),
    )
    out_specs = P("tm", "dom", None)
    return jax.shard_map(
        per_device, mesh=mesh, in_specs=in_specs, out_specs=out_specs, check_vma=False
    )
```

```python
import functools

import jax
import jax.numpy as jnp
from jax import lax
from jax.experimental import pallas as pl
from jax.experimental.pallas import tpu as pltpu
from jax.sharding import PartitionSpec as P

F32 = jnp.float32
BF16 = jnp.bfloat16
PAIR = 2


def halves(x):
    hi = x.astype(BF16)
    return hi, (x - hi.astype(F32)).astype(BF16)


def split_cols(matrix):
    return jnp.concatenate(halves(matrix), axis=1)


def split_rows(vectors):
    hi, lo = halves(vectors)
    hi, lo = hi.astype(F32), lo.astype(F32)
    top = jnp.concatenate([hi, hi], axis=1)
    low = jnp.concatenate([lo, jnp.zeros_like(lo)], axis=1)
    return jnp.concatenate([top, low], axis=0).astype(BF16)


def dot_nt(a, b):
    return lax.dot_general(a, b, (((1,), (1,)), ((), ())), preferred_element_type=F32)


def times(a, b):
    ah, al = halves(a)
    bh, bl = halves(b)
    left = jnp.concatenate([ah, al, ah], axis=1)
    right = jnp.concatenate([bh, bh, bl], axis=0)
    return jnp.dot(left, right, preferred_element_type=F32)


def mapped(matrix_split, vectors):
    count = vectors.shape[0]
    both = dot_nt(split_rows(vectors), matrix_split)
    return both[:count] + both[count:]


def mapped_each(matrices, vectors):
    if isinstance(matrices, tuple):
        half = vectors.shape[0] // 2
        near = mapped_each(matrices[0], vectors[:half])
        return jnp.concatenate([near, mapped_each_split(matrices[1], vectors[half:])], axis=0)
    rows = []
    for r in range(vectors.shape[0]):
        products = matrices[r] * vectors[r : r + 1, :]
        rows.append(jnp.sum(products.T, axis=0, keepdims=True))
    return jnp.concatenate(rows, axis=0)


def mapped_each_split(matrices_split, vectors):
    count, width = vectors.shape
    both = dot_nt(split_rows(vectors), matrices_split)
    row = lax.broadcasted_iota(jnp.int32, (2 * count, width), 0) % count
    picked = [
        jnp.where(row == r, both[:, r * width : (r + 1) * width], 0.0) for r in range(count)
    ]
    while len(picked) > 1:
        picked = [a + b for a, b in zip(picked[::2], picked[1::2])]
    return picked[0][:count] + picked[0][count:]


def mapped_sum(matrices, vectors):
    products = matrices[0] * vectors[:1, :]
    for r in range(1, vectors.shape[0]):
        products = products + matrices[r] * vectors[r : r + 1, :]
    return jnp.sum(products.T, axis=0, keepdims=True)


def call(kernel, outs, *args, cost=None, in_hbm=0, scratch=()):
    vmem = pl.BlockSpec(memory_space=pltpu.VMEM)
    return pl.pallas_call(
        kernel,
        out_shape=[jax.ShapeDtypeStruct(s, d) for s, d in outs],
        in_specs=[vmem] * (len(args) - in_hbm) + [pl.BlockSpec(memory_space=pltpu.HBM)] * in_hbm,
        out_specs=[vmem] * len(outs),
        scratch_shapes=list(scratch),
        cost_estimate=cost,
        compiler_params=pltpu.CompilerParams(vmem_limit_bytes=24 * 2**20),
    )(*args)


def identity(width):
    return (
        lax.broadcasted_iota(jnp.int32, (width, width), 0)
        == lax.broadcasted_iota(jnp.int32, (width, width), 1)
    ).astype(F32)


def halo_kernel(s_ref, near_ref, msg_ref):
    points, width = s_ref.shape
    msg_ref[:4] = jnp.broadcast_to(near_ref[points - 1 :], (4, width))
    msg_ref[4:] = jnp.broadcast_to(s_ref[points - 1 :], (4, width))


def ones_kernel(one_ref):
    one_ref[...] = jnp.ones(one_ref.shape, F32)


def pack_kernel(one_ref, g_ref, mask_ref, k_ref, j_ref, inj_ref, cap_ref, gain_ref, bnd_ref, pack_ref):
    points, width = inj_ref.shape
    pack_ref[:width] = g_ref[...] * (mask_ref[...] * one_ref[...])
    pack_ref[width : 2 * width] = k_ref[...]
    pack_ref[2 * width : 3 * width] = j_ref[...]
    at = 3 * width
    pack_ref[at : at + points] = inj_ref[...]
    at += points
    for one in (cap_ref[...], gain_ref[...], bnd_ref[...].astype(F32)):
        pack_ref[at : at + 8] = jnp.broadcast_to(one, (8, width))
        at += 8


def vectors(small_ref, g, points):
    at = g * (points + 24)
    inj = small_ref[at : at + points]
    at += points
    cap, gain, bnd = (small_ref[at + 8 * i : at + 8 * i + 1] for i in range(3))
    return inj, cap, gain, bnd.astype(jnp.int32)


def fetched(sources, targets, sems):
    moves = [
        pltpu.make_async_copy(source, target, sems.at[i])
        for i, (source, target) in enumerate(zip(sources, targets))
    ]
    for move in moves:
        move.start()
    return moves


def whole_kernel(lo_ref, hi_ref, diag_ref, w_ref, d_hi, r_lo, r_hi, sems):
    points, width = lo_ref.shape[0], lo_ref.shape[1]
    moves = fetched((lo_ref, hi_ref, diag_ref), (r_lo, r_hi, d_hi), sems)
    u = []
    for move, r_ref in zip(moves, (r_lo, r_hi)):
        move.wait()
        u += [times(r_ref[i + 1], r_ref[i]) for i in range(0, points, 2)]
    while len(u) > PAIR:
        u = [times(u[i + 1], u[i]) for i in range(0, len(u), 2)]
    for g in range(PAIR):
        w_ref[g * width : (g + 1) * width] = u[g]
    moves[-1].wait()


def suffix_kernel(r_lo, r_hi, lo_ref, hi_ref, s_ref, d_lo, d_hi, sems):
    points, width = r_lo.shape[0], r_lo.shape[1]
    moves = fetched((lo_ref, hi_ref), (d_lo, d_hi), sems)
    both = [[r_ref[i] for i in range(points)] for r_ref in (r_lo, r_hi)]
    span = 1
    while span < points:
        for base in range(0, points, 2 * span):
            first = max(base, 1)
            if first == base + span:
                continue
            for u in both:
                prod = times(u[base + span], jnp.concatenate(u[first : base + span], axis=1))
                for i in range(first, base + span):
                    at = (i - first) * width
                    u[i] = prod[:, at : at + width]
        span *= 2
    for g, u in enumerate(both):
        for i in range(points - 1):
            s_ref[g * points + i] = u[i + 1]
        s_ref[(g + 1) * points - 1] = identity(width)
    for move in moves:
        move.wait()


def prefix_kernel(r_lo, r_hi, p_lo, l_lo, p_hi, l_hi):
    points, width = r_lo.shape[0], r_lo.shape[1]
    both = [[r_ref[i] for i in range(points)] for r_ref in (r_lo, r_hi)]
    span, slot = 1, 0
    while span < points:
        for base in range(0, points, 2 * span):
            for q, l_ref in zip(both, (l_lo, l_hi)):
                upper = q[base + span : base + 2 * span]
                for i, matrix in enumerate(upper):
                    if l_ref is l_hi:
                        at = (slot + i) * width
                        l_ref[at : at + width] = split_cols(matrix)
                    else:
                        l_ref[slot + i] = matrix
                prod = times(jnp.concatenate(upper, axis=0), q[base + span - 1])
                for i in range(span):
                    q[base + span + i] = prod[i * width : (i + 1) * width]
            slot += span
        span *= 2
    for i in range(points):
        p_lo[i] = both[0][i]
        p_hi[i * width : (i + 1) * width] = split_cols(both[1][i])


def scanned(c, l_ref):
    points = c.shape[0]
    x = [c[i : i + 1, :] for i in range(points)]
    span, slot = 1, 0
    while span < points:
        for base in range(0, points, 2 * span):
            head = x[base + span - 1]
            for i in range(base + span, base + 2 * span):
                x[i] = x[i] + mapped_each(l_ref[slot : slot + 1], head)
                slot += 1
        span *= 2
    return jnp.concatenate(x, axis=0)


def scanned_split(c, l_ref):
    points, width = c.shape
    half = points // 2
    x = [c[i : i + 1, :] for i in range(points)]
    span, level = 1, 0
    while span < points:
        later = [i for i in range(points) if i & span]
        heads = jnp.concatenate([x[(i & ~(2 * span - 1)) + span - 1] for i in later], axis=0)
        rows = slice(level * half * width, (level + 1) * half * width)
        moved = mapped_each_split(l_ref[rows], heads)
        for slot, i in enumerate(later):
            x[i] = x[i] + moved[slot : slot + 1]
        span *= 2
        level += 1
    return jnp.concatenate(x, axis=0)


def taken(rows, lanes):
    return jnp.take_along_axis(rows, jnp.broadcast_to(lanes, rows.shape), axis=1)


def negative_residual(s, halo, inj, cap, gain, gs):
    before = jnp.concatenate([halo, s[: s.shape[0] - 1]], axis=0)
    return inj - cap * (s - before) - mapped(gs, s) - gain * jnp.tanh(s)


def corrected(nr, c_before, s_before, d_ref, js, ks):
    return mapped_each(d_ref, nr + mapped(js, c_before) + mapped(ks, s_before))


def pair_corrected(nr, s_lo, c_lo, bnd_lo, d_hi_ref, js, ks):
    return corrected(nr, taken(c_lo, bnd_lo), taken(s_lo, bnd_lo), d_hi_ref, js, ks)


def correct_both(
    s_lo, s_hi, halo_lo, halo_hi, small_ref, maps_ref, d_lo, d_hi, nr_ref, c_ref, msg_ref
):
    lo_maps, hi_maps = [maps_ref[i] for i in range(3)], [maps_ref[i] for i in range(3, 6)]
    points = s_lo.shape[0]
    inj_lo, cap_lo, gain_lo, bnd_lo = vectors(small_ref, 0, points)
    inj_hi, cap_hi, gain_hi, bnd_hi = vectors(small_ref, 1, points)
    nr_lo = negative_residual(s_lo, halo_lo, inj_lo, cap_lo, gain_lo, lo_maps[0])
    nr_hi = negative_residual(s_hi, halo_hi, inj_hi, cap_hi, gain_hi, hi_maps[0])
    nr_ref[:points], nr_ref[points:] = nr_lo, nr_hi
    msg_ref[points:] = taken(s_hi, bnd_hi)

    @pl.when(in_first_pair())
    def _():
        c_lo = mapped_each(d_lo, nr_lo)
        c_hi = pair_corrected(nr_hi, s_lo, c_lo, bnd_lo, d_hi, hi_maps[2], hi_maps[1])
        c_ref[:points], c_ref[points:] = c_lo, c_hi
        msg_ref[:points] = taken(c_hi, bnd_hi)

    @pl.when(jnp.logical_not(in_first_pair()))
    def _():
        c_ref[...] = jnp.zeros(c_ref.shape, F32)
        msg_ref[:points] = jnp.zeros((points, c_ref.shape[1]), F32)


def early_kernel(s_lo, s_hi, pack_lo, pack_hi, _, maps_ref, small_ref, nr_ref):
    points, width = s_lo.shape
    for i in range(3):
        rows = slice(i * width, (i + 1) * width)
        maps_ref[i] = split_cols(pack_lo[rows])
        maps_ref[3 + i] = split_cols(pack_hi[rows])
    none = jnp.zeros((1, width), F32)
    for g, (s_ref, pack) in enumerate(((s_lo, pack_lo), (s_hi, pack_hi))):
        at = g * (points + 24)
        small_ref[at : at + points + 24] = pack[3 * width :]
        inj, cap, gain, _ = vectors(small_ref, g, points)
        nr_ref[g * points : (g + 1) * points] = negative_residual(
            s_ref[...], none, inj, cap, gain, maps_ref[3 * g]
        )


def diagonal_kernel(_, lo_ref, d_lo, sems):
    @pl.when(in_first_pair())
    def _():
        for move in fetched((lo_ref,), (d_lo,), sems):
            move.wait()


def in_first_pair():
    return lax.axis_index("dom") < PAIR


def first_kernel(
    halo_ref, s_lo, s_hi, small_ref, maps_ref, d_lo, d_hi, old_nr, s_ref, nr_ref, c_ref, msg_ref
):
    points = s_lo.shape[0]
    bnd_lo, bnd_hi = (vectors(small_ref, g, points)[3] for g in range(PAIR))
    s_ref[:points], s_ref[points:] = s_lo[...], s_hi[...]
    msg_ref[points:] = taken(s_hi[...], bnd_hi)
    nr_ref[...] = old_nr[...]
    for g in range(PAIR):
        at = g * points
        cap = vectors(small_ref, g, points)[1]
        nr_ref[at : at + 1] = old_nr[at : at + 1] + cap * halo_ref[4 * g : 4 * g + 1]

    @pl.when(in_first_pair())
    def _():
        c_lo = mapped_each(d_lo, nr_ref[:points])
        linked = mapped(maps_ref[4], taken(s_lo[...], bnd_lo))
        c_hi = mapped_each(
            d_hi, nr_ref[points:] + linked + mapped(maps_ref[5], taken(c_lo, bnd_lo))
        )
        c_ref[:points], c_ref[points:] = c_lo, c_hi
        msg_ref[:points] = taken(c_hi, bnd_hi)

    @pl.when(jnp.logical_not(in_first_pair()))
    def _():
        c_ref[...] = jnp.zeros(c_ref.shape, F32)
        msg_ref[:points] = jnp.zeros((points, c_ref.shape[1]), F32)


def second_kernel(
    got_ref, s_ref, nr_ref, c_ref, small_ref, maps_ref, d_lo, d_hi, ss_ref, *refs
):
    new_c_ref, f_ref = refs[-2:]
    if len(refs) == 4:
        d_lo, d_hi = (d_lo, refs[0][...]), (d_hi, refs[1][...])
    points, width = got_ref.shape[0] // 2, got_ref.shape[1]
    second_pair = lax.axis_index("dom") >= PAIR

    @pl.when(second_pair)
    def _():
        bnd_lo = vectors(small_ref, 0, points)[3]
        c_lo = corrected(
            nr_ref[:points], got_ref[:points], got_ref[points:], d_lo, maps_ref[2], maps_ref[1]
        )
        new_c_ref[:points] = c_lo
        c_hi = pair_corrected(
            nr_ref[points:], s_ref[:points], c_lo, bnd_lo, d_hi, maps_ref[5], maps_ref[4]
        )
        new_c_ref[points:] = c_hi
        for g, c in enumerate((c_lo, c_hi)):
            whole = mapped_sum(ss_ref[g * points : (g + 1) * points], c)
            f_ref[8 * g : 8 * g + 8] = jnp.broadcast_to(whole, (8, width))

    @pl.when(jnp.logical_not(second_pair))
    def _():
        new_c_ref[...] = c_ref[...]
        for g in range(PAIR):
            rows = slice(g * points, (g + 1) * points)
            whole = mapped_sum(ss_ref[rows], c_ref[rows])
            f_ref[8 * g : 8 * g + 8] = jnp.broadcast_to(whole, (8, width))


def tail_and_split_kernel(c_ref, ss_ref, d_lo, d_hi, tail_ref, ds_lo, ds_hi):
    points, width = d_lo.shape[0], d_lo.shape[1]
    for i in range(points // 2):
        rows = slice(i * width, (i + 1) * width)
        ds_lo[rows] = split_cols(d_lo[points // 2 + i])
        ds_hi[rows] = split_cols(d_hi[points // 2 + i])
    tail_kernel(c_ref, ss_ref, tail_ref)


def tail_kernel(c_ref, ss_ref, tail_ref):
    points, width = c_ref.shape[0] // PAIR, c_ref.shape[1]
    each = mapped_each(ss_ref, c_ref[...])
    for g in range(PAIR):
        total = each[g * points : (g + 1) * points]
        shift = 1
        while shift < points:
            total = total + jnp.concatenate(
                [total[shift:], jnp.zeros((shift, width), F32)], axis=0
            )
            shift *= 2
        at = g * (points + 8)
        tail_ref[at : at + points] = jnp.concatenate(
            [total[1:], jnp.zeros((1, width), F32)], axis=0
        )
        tail_ref[at + points : at + points + 8] = jnp.broadcast_to(total[:1], (8, width))


def is_later(distance):
    return (lax.axis_index("tm") // distance) % 2 == 1


def sections(width):
    return [
        (slice(g * width, (g + 1) * width), slice(8 * g, 8 * g + 8)) for g in range(PAIR)
    ]


def first_maps_kernel(distance, mw_ref, gw_ref, _, tw_ref, a_ref, bw_ref, aw_ref):
    width = mw_ref.shape[1]
    later = is_later(distance)
    eye = identity(width)
    for wide, _ in sections(width):
        mw, gw = mw_ref[wide], gw_ref[wide]
        a = jnp.where(later, mw, gw)
        tw_ref[wide] = times(a, jnp.where(later, gw, mw))
        a_ref[wide] = split_cols(a)
        bw_ref[wide] = jnp.where(later, gw, eye)
        aw_ref[wide] = jnp.where(later, eye, gw)


def next_maps_kernel(
    distance, mw_ref, gw_ref, bw_ref, aw_ref, _, tw_ref, a_ref, x_ref, nbw_ref, naw_ref
):
    width = mw_ref.shape[1]
    later = is_later(distance)
    for wide, _ in sections(width):
        mw, gw, bw, aw = mw_ref[wide], gw_ref[wide], bw_ref[wide], aw_ref[wide]
        a = jnp.where(later, mw, gw)
        tw_ref[wide] = times(a, jnp.where(later, gw, mw))
        a_ref[wide] = split_cols(a)
        x = jnp.where(later, bw, gw)
        joined = times(x, jnp.where(later, gw, aw))
        x_ref[wide] = split_cols(x)
        nbw_ref[wide] = jnp.where(later, joined, bw)
        naw_ref[wide] = jnp.where(later, aw, joined)


def first_sums_kernel(distance, mf_ref, gf_ref, a_ref, _, __, tf_ref, bf_ref, af_ref):
    later = is_later(distance)
    for wide, short in sections(a_ref.shape[0] // PAIR):
        mf, gf = mf_ref[short], gf_ref[short]
        tf_ref[short] = mapped(a_ref[wide], jnp.where(later, gf, mf)) + jnp.where(later, mf, gf)
        bf_ref[short] = jnp.where(later, gf, 0.0)
        af_ref[short] = jnp.where(later, 0.0, gf)


def next_sums_kernel(
    distance, mf_ref, gf_ref, bf_ref, af_ref, a_ref, x_ref, _, tf_ref, nbf_ref, naf_ref
):
    later = is_later(distance)
    for wide, short in sections(a_ref.shape[0] // PAIR):
        mf, gf, bf, af = mf_ref[short], gf_ref[short], bf_ref[short], af_ref[short]
        tf_ref[short] = mapped(a_ref[wide], jnp.where(later, gf, mf)) + jnp.where(later, mf, gf)
        sums = mapped(x_ref[wide], jnp.where(later, gf, af)) + jnp.where(later, bf, gf)
        nbf_ref[short] = jnp.where(later, sums, bf)
        naf_ref[short] = jnp.where(later, af, sums)


def local_kernel(c_ref, l_lo, l_hi, tail_ref, aw_ref, af_ref, s_ref, base_ref, v_ref):
    points, width = s_ref.shape[0] // PAIR, s_ref.shape[1]
    for g, (wide, short) in enumerate(sections(width)):
        rows = slice(g * points, (g + 1) * points)
        long = slice(g * (points + 8), (g + 1) * (points + 8))
        scan = scanned_split if g else scanned
        base_ref[rows] = s_ref[rows] + scan(c_ref[rows], (l_lo, l_hi)[g])
        v_ref[long] = mapped(split_cols(aw_ref[wide]), tail_ref[long]) + af_ref[short][:1]


def turn_kernel(
    v_ref, gw_ref, gf_ref, bw_ref, bf_ref, p_lo, p_hi, base_ref, halo_ref, small_ref, maps_ref,
    d_lo, d_hi, ds_lo, ds_hi, s_ref, nr_ref, c_ref, msg_ref,
):
    points, width = s_ref.shape[0] // PAIR, s_ref.shape[1]
    came = []
    for g, (wide, short) in enumerate(sections(width)):
        long = slice(g * (points + 8), (g + 1) * (points + 8))
        v = mapped(split_cols(gw_ref[wide]), v_ref[long]) + gf_ref[short][:1]
        came.append(mapped(split_cols(bw_ref[wide]), v) + bf_ref[short][:1])
    moved = [
        mapped_each(p_lo, came[0][:points]),
        mapped_each_split(p_hi[...], came[1][:points]),
    ]
    s = base_ref[...] + jnp.concatenate(moved, axis=0)
    s_ref[...] = s
    correct_both(
        s[:points], s[points:],
        halo_ref[:1] + came[0][points : points + 1],
        halo_ref[4:5] + came[1][points : points + 1],
        small_ref, maps_ref, (d_lo, ds_lo[...]), (d_hi, ds_hi[...]), nr_ref, c_ref, msg_ref,
    )


def scan_kernel(c_ref, l_lo, l_hi, s_ref, base_ref):
    points = s_ref.shape[0] // PAIR
    for g, (scan, l_ref) in enumerate(((scanned, l_lo), (scanned_split, l_hi))):
        rows = slice(g * points, (g + 1) * points)
        base_ref[rows] = s_ref[rows] + scan(c_ref[rows], l_ref)


def last_local_kernel(
    tail_ref, aw_ref, af_ref, gw_ref, bw_ref, bf_ref, p_lo, p_hi, old_ref, base_ref
):
    points, width = old_ref.shape[0] // PAIR, old_ref.shape[1]
    came = []
    for g, (wide, short) in enumerate(sections(width)):
        at = g * (points + 8)
        v = mapped(split_cols(aw_ref[wide]), tail_ref[at : at + points]) + af_ref[short][:1]
        v = mapped(split_cols(gw_ref[wide]), v)
        came.append(mapped(split_cols(bw_ref[wide]), v) + bf_ref[short][:1])
    for g in range(PAIR):
        rows = slice(g * points, (g + 1) * points)
        moved = mapped_each_split(p_hi[...], came[g]) if g else mapped_each(p_lo, came[g])
        base_ref[rows] = old_ref[rows] + moved


def end_kernel(gf_ref, bw_ref, p_lo, p_hi, base_ref, s_ref):
    points, width = s_ref.shape[0] // PAIR, s_ref.shape[1]
    for g, (wide, short) in enumerate(sections(width)):
        rows = slice(g * points, (g + 1) * points)
        v = mapped(split_cols(bw_ref[wide]), gf_ref[short])
        if g:
            both = dot_nt(split_rows(v), p_hi[...])
            both = both[:1] + both[8:9]
            moved = [both[:, i * width : (i + 1) * width] for i in range(points)]
            moved = jnp.concatenate(moved, axis=0)
        else:
            moved = mapped_each(p_lo, jnp.broadcast_to(v[:1], (points, width)))
        s_ref[rows] = base_ref[rows] + moved


def choose_kernel(both_ref, got_ref, s_ref):
    points = s_ref.shape[0]
    odd = lax.axis_index("dom") % 2 == 1
    s_ref[...] = jnp.where(odd, both_ref[points:], got_ref[:points])


def exchanged(value, distance):
    return lax.ppermute(
        value, "tm", [(i, i ^ distance) for i in range(lax.axis_size("tm"))]
    )


def swapped(value, distance):
    return lax.ppermute(value, "dom", [(i, i ^ distance) for i in range(lax.axis_size("dom"))])


def both_partitions(
    s, nr, c, msg, halo, small, maps, d_lo, d_hi, r_lo, r_hi, w
):
    points, width = s.shape[0] // PAIR, s.shape[1]
    vec, square = ((PAIR * points, width), F32), ((PAIR * width, width), F32)
    square_split = ((PAIR * width, 2 * width), BF16)
    eight = ((PAIR * 8, width), F32)
    longer = ((PAIR * (points + 8), width), F32)
    many = ((PAIR * points, width, width), F32)
    steps = (points.bit_length() - 1) * points // 2
    distances = [2**k for k in range(lax.axis_size("tm").bit_length() - 1)]

    def sums_level(level, f, bf, af, beside):
        got = exchanged(f, distances[level])
        if level == 0:
            return call(
                functools.partial(first_sums_kernel, distances[0]), [eight] * 3,
                f, got, *kept[0], *beside,
            )
        return call(
            functools.partial(next_sums_kernel, distances[level]), [eight] * 3,
            f, got, bf, af, *kept[level], beside[1],
            cost=pl.CostEstimate(flops=2**33, bytes_accessed=2**25, transcendentals=0),
        )

    got = swapped(msg, 2)
    got_w = exchanged(w, distances[0])
    ss, d_lo, d_hi = call(
        suffix_kernel, [many] + [((points, width, width), F32)] * 2, r_lo, r_hi, d_lo, d_hi,
        in_hbm=2, scratch=[pltpu.SemaphoreType.DMA((2,))],
    )
    p_lo, l_lo, p_hi, l_hi = call(
        prefix_kernel,
        [((points, width, width), F32), ((steps, width, width), F32)]
        + [((points * width, 2 * width), BF16), ((steps * width, 2 * width), BF16)],
        r_lo, r_hi,
    )
    c, f = call(
        second_kernel, [vec, eight], got, s, nr, c, small, maps, d_lo, d_hi, ss
    )
    tail, ds_lo, ds_hi = call(
        tail_and_split_kernel, [longer] + [((points // 2 * width, 2 * width), BF16)] * 2,
        c, ss, d_lo, d_hi,
    )
    kept, bf, af = [], None, None
    for level, distance in enumerate(distances[:-1]):
        if level == 0:
            w, a, bw, aw = call(
                functools.partial(first_maps_kernel, distance),
                [square, square_split, square, square], w, got_w, f,
            )
            kept.append((a,))
        else:
            w, a, x, bw, aw = call(
                functools.partial(next_maps_kernel, distance),
                [square, square_split, square_split, square, square], w, got_w, bw, aw, f,
            )
            kept.append((a, x))
        got_w = exchanged(w, distances[level + 1])
        f, bf, af = sums_level(level, f, bf, af, (p_lo, p_hi))
    got, last = exchanged(f, distances[-1]), got_w
    base, v = call(local_kernel, [vec, longer], c, l_lo, l_hi, tail, aw, af, s)
    s, nr, c, msg = call(
        turn_kernel, [vec] * 4,
        v, last, got, bw, bf, p_lo, p_hi, base, halo, small, maps, d_lo, d_hi, ds_lo, ds_hi,
    )
    got = swapped(msg, 2)
    c, f = call(
        second_kernel, [vec, eight], got, s, nr, c, small, maps, d_lo, d_hi, ss, ds_lo, ds_hi
    )
    (tail,) = call(tail_kernel, [longer], c, ss)
    (base,) = call(scan_kernel, [vec], c, l_lo, l_hi, s)
    for level in range(len(distances) - 1):
        f, bf, af = sums_level(level, f, bf, af, (tail, base))
    got = exchanged(f, distances[-1])
    (base,) = call(last_local_kernel, [vec], tail, aw, af, last, bw, bf, p_lo, p_hi, base)
    return call(end_kernel, [vec], got, bw, p_lo, p_hi, base)[0]


def per_device(
    starting_voltage_guess,
    injected_amperes,
    capacitance,
    conductance,
    block_pattern,
    device_gain,
    link_weight,
    boundary_vertex_list,
    diagonal_reciprocals,
    boundary_jacobian,
    transfer,
):
    points, _, width = starting_voltage_guess.shape
    segments = lax.axis_size("tm")
    (one,) = call(
        ones_kernel, [((1, width), F32)],
        cost=pl.CostEstimate(flops=2**33, bytes_accessed=2**25, transcendentals=0),
    )
    mask = jnp.broadcast_to(block_pattern[0].astype(F32), (1, width))
    s = starting_voltage_guess[:, 0]
    near_s = swapped(starting_voltage_guess, 1)[:, 0]
    d, r, near_s, mask, one = lax.optimization_barrier(
        (diagonal_reciprocals, transfer, near_s, mask, one)
    )
    d, near_d = d[:, 0, 0], swapped(d, 1)[:, 0, 0]
    r, near_r = r[:, 0, 0], swapped(r, 1)[:, 0, 0]
    (rows,) = call(halo_kernel, [((8, width), F32)], s, near_s)
    halo = lax.ppermute(rows, "tm", [(i, (i + 1) % segments) for i in range(segments)])
    (pack,) = call(
        pack_kernel, [((3 * width + points + 24, width), F32)],
        one, conductance[0], mask, link_weight[0], boundary_jacobian[0],
        injected_amperes[:, 0], capacitance, device_gain, boundary_vertex_list,
    )
    near_pack = swapped(pack, 1)
    vec = ((PAIR * points, width), F32)
    w, d_hi = call(
        whole_kernel, [((PAIR * width, width), F32), ((points, width, width), F32)],
        near_r, r, d, in_hbm=3,
        scratch=[pltpu.VMEM((points, width, width), F32)] * 2 + [pltpu.SemaphoreType.DMA((3,))],
    )
    maps, small, nr = call(
        early_kernel,
        [((6, width, 2 * width), BF16), ((PAIR * (points + 24), width), F32), vec],
        near_s, s, near_pack, pack, w,
    )
    (d_lo,) = call(
        diagonal_kernel, [((points, width, width), F32)], nr, near_d,
        in_hbm=1, scratch=[pltpu.SemaphoreType.DMA((1,))],
    )
    s, nr, c, msg = call(
        first_kernel, [vec] * 4, halo, near_s, s, small, maps, d_lo, d_hi, nr
    )
    odd = lax.axis_index("dom") % 2 == 1
    both = lax.cond(
        odd,
        both_partitions,
        lambda s, *rest: s,
        s, nr, c, msg, halo, small, maps, near_d, d, near_r, r, w,
    )
    (s,) = call(choose_kernel, [((points, width), F32)], both, swapped(both, 1))
    return s[:, None]


def solution(mesh):
    in_specs = (
        P("tm", "dom", None),
        P("tm", "dom", None),
        P("dom", None),
        P("dom", None, None),
        P("dom", None, None),
        P("dom", None),
        P("dom", None, None),
        P("dom", None),
        P("tm", "dom", None, None, None),
        P("dom", None, None),
        P("tm", "dom", None, None, None),
    )
    out_specs = P("tm", "dom", None)
    return jax.shard_map(
        per_device, mesh=mesh, in_specs=in_specs, out_specs=out_specs, check_vma=False
    )
```
